32 devices in a mesh: rows: 8 (over z, y), cols: 4 (over x, core).
Axes of the slice: x: 2, y: 2, z: 4, core: 2. Of those that a mesh axis runs over, the one named last changes fastest.
Arguments:
- user_factors: float32 [128, 16384], P('cols', 'rows'), may hold values from -6 to 6
- item_factors: bfloat16 [128, 65536], P('cols', 'rows'), may hold values from -0.0234375 to 0.0234375
- tile_user: int32 [576], P('rows'), may hold values from 0 to 7
- tile_item: int32 [576], P('rows'), may hold values from 0 to 255, as said below
- tile_count: int32 [8], P('rows'), may hold values from 36 to 72, as said below
- tile_mask: bfloat16 [576, 256, 256], P('rows'), may hold values from 0 to 2, as said below
Outputs:
- solution_field: float32 [128, 16384], P('cols', 'rows')
- residual: float32 [128, 16384], P('cols', 'rows')
The draws below stay inside these ranges and needn't reach their ends.
Inputs may be any that keep to these rules, and one draw needn't show every extreme that they name: `tile_item`: item block b is held by index b // 32 of rows. Among the live slots of one index of rows at most 9 name item blocks held by one index of rows, and in every draw some index reaches 9. `tile_count`: some index of rows has all 72 slots live in every draw. `tile_mask`: each entry is zero or a strength of 0.5 or more.
All inputs are finite; a program needn't handle non-finite values.
Results may differ from the reference program's by a relative error of at most 0.0008.
Values may be sent and summed in bfloat16 or wider, within the bound.
No kernel may reach another device: no remote copies, remote signals or barrier semaphores. Data moves between devices by JAX's collectives and lax.ppermute only.
A program may use at most 128 MiB of HBM per device.

```python
import jax
import jax.numpy as jnp
from jax import lax

K = 128
TILE = 256
ITERS = 2
UBLK_DEV = 8
IBLK_DEV = 32
TILES_DEV = 72
CAP = 9
USERS = 16384
ITEMS = 65536
N_ROWS = 8


def draw_tile_item(key, part):
    key = jax.random.fold_in(key, 11)

    def one_device(device):
        device_key = jax.random.fold_in(key, device)
        first_key, second_key = jax.random.split(device_key)
        owners = jax.random.permutation(first_key, N_ROWS).astype(jnp.int32)
        order = jnp.arange(TILES_DEV, dtype=jnp.int32)
        holder = owners[order // CAP % N_ROWS]
        blocks = jax.random.randint(second_key, (TILES_DEV,), 0, IBLK_DEV, dtype=jnp.int32)
        return holder * IBLK_DEV + blocks
    return jax.vmap(one_device)(jnp.arange(N_ROWS, dtype=jnp.int32)).reshape(N_ROWS * TILES_DEV).astype(jnp.int32)


def draw_tile_count(key, part):
    key = jax.random.fold_in(key, 23)
    first_key, second_key = jax.random.split(key)
    counts = jax.random.randint(first_key, (N_ROWS,), max(1, TILES_DEV // 2), TILES_DEV + 1, dtype=jnp.int32)
    fullest = jax.random.randint(second_key, (), 0, N_ROWS, dtype=jnp.int32)
    places = jnp.arange(N_ROWS, dtype=jnp.int32)
    return jnp.where(places == fullest, TILES_DEV, counts).astype(jnp.int32)


def draw_tile_mask(key, part):
    key = jax.random.fold_in(key, 37)
    first_key, second_key = jax.random.split(key)
    shape = (N_ROWS * TILES_DEV, TILE, TILE)
    present = (jax.random.uniform(first_key, shape, dtype=jnp.float32) < 0.5).astype(jnp.float32)
    spread = jax.random.uniform(second_key, shape, dtype=jnp.float32)
    strength = 0.5 * jnp.exp(spread * jnp.log(4.0))
    return (present * strength).astype(jnp.bfloat16)


def set_ends(entries, own_key, low, largest):
    longest = entries.shape.index(max(entries.shape))
    spots = []
    for shift in (0, 1):
        where = [jax.random.randint(jax.random.fold_in(own_key, axis), (), 0, length) for axis, length in enumerate(entries.shape)]
        where[longest] = (where[longest] + shift) % entries.shape[longest]
        spots.append(tuple(where))
    return entries.at[spots[0]].set(low).at[spots[1]].set(largest)


def steps_of(own_key, shape, cuts, least, largest):
    gain = 1.0
    for dim, shards_of in cuts:
        heights = jax.random.uniform(jax.random.fold_in(jax.random.fold_in(own_key, 6), dim), (shards_of,), jnp.float32, least / len(cuts), largest / len(cuts))
        gain = gain * jnp.repeat(jnp.exp(heights), shape[dim] // shards_of).reshape((-1,) + (1,) * (len(shape) - 1 - dim))
    return gain


def gaussian(stream_key, dims, scale, reach, cuts=(), held_as=jnp.bfloat16):
    level = steps_of(stream_key, dims, cuts, -0.22, 0.18) if cuts else 1.0
    entries = jax.random.normal(stream_key, dims, jnp.float32) * scale * level
    return jnp.minimum(jnp.maximum(entries, -reach), reach).astype(held_as)


def setup_inputs(seed: int = 0) -> dict:
    key_list = jax.random.split(jax.random.key(seed), 7)
    return {
        "user_factors": gaussian(key_list[0], (K, USERS), 1.0, 6.0, ((0, 4), (1, 8)), jnp.float32),
        "item_factors": gaussian(key_list[1], (K, ITEMS), ITEMS ** -0.5, 0.0234375, ((0, 4), (1, 8))),
        "tile_user": set_ends(jax.random.randint(key_list[2], (N_ROWS * TILES_DEV,), 0, UBLK_DEV), jax.random.fold_in(key_list[2], 1), 0, UBLK_DEV - 1).astype(jnp.int32),
        "tile_item": draw_tile_item(jax.random.fold_in(key_list[6], 71), 0),
        "tile_count": draw_tile_count(jax.random.fold_in(key_list[6], 71), 0),
        "tile_mask": draw_tile_mask(jax.random.fold_in(key_list[6], 71), 0),
    }


ridge = 0.5
confidence = 40.0
highest = lax.Precision.HIGHEST


def collect_blocks(users_dev, terms):
    select = (users_dev[None, :] == jnp.arange(UBLK_DEV, dtype=jnp.int32)[:, None]).astype(jnp.float32)
    summed = jnp.einsum('bt,tuc->buc', select, terms, precision=highest)
    return summed.reshape(UBLK_DEV * TILE, terms.shape[2])


def device_terms(item_table, items_dev, strengths_dev, live_dev):
    item_tiles = item_table.reshape(-1, TILE, K)[items_dev]
    masks = strengths_dev.astype(jnp.float32) * live_dev[:, None, None]
    return item_tiles, masks


def reference(user_factors, item_factors, tile_user, tile_item, tile_count, tile_mask):
    item_table = item_factors.astype(jnp.float32).T
    gram = jnp.dot(item_table.T, item_table, precision=highest)
    users_all = tile_user.reshape(N_ROWS, TILES_DEV)
    items_all = tile_item.reshape(N_ROWS, TILES_DEV)
    strengths_all = tile_mask.reshape(N_ROWS, TILES_DEV, TILE, TILE)
    order = jnp.arange(TILES_DEV, dtype=jnp.int32)
    live_all = (order[None, :] < tile_count[:, None]).astype(jnp.float32)

    def rhs_dev(pack):
        users_dev, items_dev, strengths_dev, live_dev = pack
        item_tiles, masks = device_terms(item_table, items_dev, strengths_dev, live_dev)
        terms = jnp.einsum('tui,tic->tuc', masks, item_tiles, precision=highest)
        return collect_blocks(users_dev, terms)

    right_side = (1.0 + confidence) * lax.map(rhs_dev, (users_all, items_all, strengths_all, live_all)).reshape(USERS, K)

    def apply_op(dirs):
        dev_dirs = dirs.reshape(N_ROWS, UBLK_DEV * TILE, K)

        def one_dev(pack):
            dirs_dev, users_dev, items_dev, strengths_dev, live_dev = pack
            item_tiles, masks = device_terms(item_table, items_dev, strengths_dev, live_dev)
            dir_tiles = dirs_dev.reshape(UBLK_DEV, TILE, K)[users_dev]
            scores = jnp.einsum('tuk,tik->tui', dir_tiles, item_tiles, precision=highest) * masks
            terms = jnp.einsum('tui,tic->tuc', scores, item_tiles, precision=highest)
            return collect_blocks(users_dev, terms)

        sparse = lax.map(one_dev, (dev_dirs, users_all, items_all, strengths_all, live_all)).reshape(USERS, K)
        return jnp.dot(dirs, gram, precision=highest) + ridge * dirs + confidence * sparse

    solution_field = user_factors.T
    residual = right_side - apply_op(solution_field)
    direction = residual
    norm_now = jnp.sum(residual * residual)
    for iteration in range(ITERS):
        image = apply_op(direction)
        alpha = norm_now / jnp.sum(direction * image)
        solution_field = solution_field + alpha * direction
        residual = residual - alpha * image
        norm_next = jnp.sum(residual * residual)
        direction = residual + (norm_next / norm_now) * direction
        norm_now = norm_next
    return solution_field.T, residual.T
```

```python
import functools

import jax
import jax.numpy as jnp
from jax import lax
from jax.experimental import pallas as pl
from jax.experimental.pallas import tpu as pltpu
from jax.sharding import PartitionSpec as P

ridge = 0.5
confidence = 40.0
UNROLL = 8
LIMIT = 24 * 1024 * 1024
f32 = jnp.float32
bf16 = jnp.bfloat16


def matmul(left, right):
    return jnp.dot(left, right, preferred_element_type=f32)


def split(value):
    high = value.astype(bf16)
    low = (value - high.astype(f32)).astype(bf16)
    return high, low


def prepare_kernel(info_ref, x_ref, items_ref, mask_hbm, x_out, items_out, mask, sem):
    column = info_ref[1]
    n_cols, _, span = items_out.shape
    tiles, share, side = mask.shape
    copy = pltpu.make_async_copy(
        mask_hbm.at[:, pl.ds(pl.multiple_of(column * share, share), share), :], mask, sem
    )
    copy.start()
    for m in range(n_cols):
        place = pl.multiple_of((column ^ m) * span, span)
        items_out[m] = items_ref[:, pl.ds(place, span)]
        blocks = x_ref.shape[1] // side
        x_out[column ^ m] = jnp.concatenate(
            [
                x_ref[:, b * side + m * share : b * side + (m + 1) * share]
                for b in range(blocks)
            ],
            axis=1,
        )
    copy.wait()

    def clear(t, carry):
        mask[t] = jnp.zeros((share, side), bf16)
        return carry

    lax.fori_loop(info_ref[0], tiles, clear, 0)


def pick_kernel(side, items_ref, *refs):
    half = len(refs) // 2
    for wanted_ref, out_ref in zip(refs[:half], refs[half:]):
        for r in range(out_ref.shape[0]):
            block = jnp.maximum(wanted_ref[r], 0)
            start = pl.multiple_of(block * side, side)
            out_ref[r] = items_ref[:, pl.ds(start, side)]


def gram_kernel(info_ref, *refs):
    column = info_ref[1]
    pieces, out_ref, items = refs[:-2], refs[-2], refs[-1]
    width = pieces[0].shape[0]
    for m, piece in enumerate(pieces):
        items[pl.ds(pl.multiple_of((column ^ m) * width, width), width), :] = piece[...]
    out_ref[...] = lax.dot_general(
        items[...], items[...], (((1,), (1,)), ((), ())), preferred_element_type=f32
    )


def load(p_hl, vector):
    blocks, both, width = p_hl.shape
    share = both // 2
    high, low = split(vector)
    p_hl[:, :share] = high.reshape(blocks, share, width)
    p_hl[:, share:] = low.reshape(blocks, share, width)


def dense(p_hl, gram_ref, vector):
    blocks, both, width = p_hl.shape
    gram_high, gram_low = split(gram_ref[...])
    product = matmul(
        p_hl[...].reshape(blocks * both, width),
        jnp.concatenate([gram_high, gram_low], axis=1),
    ).reshape(blocks, 2, both // 2, 2 * width)
    product = product[:, 0] + product[:, 1]
    product = product[:, :, :width] + product[:, :, width:]
    return product.reshape(vector.shape) + ridge * vector


def sparse(starting, slot_ref, user_ref, y, mask, p_hl, acc, held):
    tiles, share, side = mask.shape
    groups = tiles // UNROLL
    acc[...] = jnp.zeros_like(acc)

    def score(group):
        for j in range(UNROLL):
            t = group * UNROLL + j
            scores = matmul(p_hl[user_ref[t]], y[slot_ref[t]])
            scores = scores[:share] + scores[share:]
            if starting:
                scores = (1.0 + confidence) - confidence * scores
            high, low = split(mask[t].astype(f32) * scores)
            held[group % 2, j, :share] = high
            held[group % 2, j, share:] = low

    def collect(group):
        terms = []
        for j in range(UNROLL):
            t = group * UNROLL + j
            term = lax.dot_general(
                held[group % 2, j],
                y[slot_ref[t]],
                (((1,), (1,)), ((), ())),
                preferred_element_type=f32,
            )
            terms.append(term[:share] + term[share:])
        return terms

    def add(group, terms):
        for j, term in enumerate(terms):
            acc[user_ref[group * UNROLL + j]] += term

    score(0)

    def step(group, carry):
        terms = collect(group - 1)
        score(group)
        add(group - 1, terms)
        return carry

    lax.fori_loop(1, groups, step, 0)
    add(groups - 1, collect(groups - 1))


def put(column, ref, vector):
    n_cols, piece_width, _ = ref.shape
    turned = vector.T
    for m in range(n_cols):
        ref[column ^ m] = turned[m * piece_width : (m + 1) * piece_width]


def start_kernel(n_cols, slot_ref, user_ref, info_ref, gram_ref, mask, *refs):
    n_pieces = len(refs) - 8
    x_pieces, pieces = refs[:n_cols], refs[n_cols:n_pieces]
    sent_ref, field_ref, y, x, p_hl, acc, held, sems = refs[n_pieces:]
    piece_width = y.shape[1] // n_cols
    column = info_ref[1]
    copies = []
    base = 0
    for k in range(0, len(pieces), 2):
        own, other = pieces[k], pieces[k + 1]
        slots = other.shape[0] // 2
        for m in range(n_cols):
            place = pl.multiple_of((column ^ m) * piece_width, piece_width)
            source = (other if m % 2 else own).at[pl.ds(m // 2 * slots, slots)]
            copies.append(
                pltpu.make_async_copy(
                    source,
                    y.at[pl.ds(base, slots), pl.ds(place, piece_width), :],
                    sems.at[len(copies)],
                )
            )
        base += slots
    for copy in copies:
        copy.start()
    for m, piece in enumerate(x_pieces):
        x[pl.ds(pl.multiple_of((column ^ m) * piece_width, piece_width), piece_width), :] = piece[...]
    start = x[...].T
    load(p_hl, start)
    rest = dense(p_hl, gram_ref, start)
    for copy in copies:
        copy.wait()
    sparse(True, slot_ref, user_ref, y, mask, p_hl, acc, held)
    field = acc[...].reshape(start.shape) - rest
    field_ref[...] = field
    put(column, sent_ref, field)


def first_kernel(
    slot_ref, user_ref, info_ref, field_ref, gram_ref, y, mask, sent_ref, first_ref, p_hl, acc, held
):
    field = field_ref[...]
    load(p_hl, field)
    sparse(False, slot_ref, user_ref, y, mask, p_hl, acc, held)
    first = confidence * acc[...].reshape(field.shape) + dense(p_hl, gram_ref, field)
    first_ref[...] = first
    put(info_ref[1], sent_ref, first)


def second_kernel(
    slot_ref, user_ref, info_ref, field_ref, first_ref, gram_ref, y, mask, sent_ref, dots_ref, p_hl, acc, held
):
    field = field_ref[...]
    first = first_ref[...]
    load(p_hl, first)
    sparse(False, slot_ref, user_ref, y, mask, p_hl, acc, held)
    second = confidence * acc[...].reshape(field.shape) + dense(p_hl, gram_ref, first)
    put(info_ref[1], sent_ref, second)

    def total(left, right):
        return jnp.sum(left * right)

    aa, ab, bb = total(field, field), total(field, first), total(first, first)
    guess = jnp.where(bb > 0.0, ab / jnp.where(bb > 0.0, bb, 1.0), 0.0)
    near = field - guess * first
    near_image = first - guess * second
    values = (
        aa,
        ab,
        bb,
        guess,
        total(near, near),
        total(near, first),
        total(near, near_image),
        total(near, second) + total(first, near_image),
        total(first, second),
    )
    lane = lax.broadcasted_iota(jnp.int32, dots_ref.shape, 1)
    dots = jnp.zeros(dots_ref.shape, f32)
    for j, value in enumerate(values):
        dots = jnp.where(lane == j, value, dots)
    dots_ref[...] = dots


def finish_kernel(share, info_ref, dots_ref, x_ref, *refs):
    n_cols = (len(refs) - 5) // 3
    x_out, r_out, field_ref, first_ref, second_ref = refs[3 * n_cols :]
    for v, ref in enumerate((field_ref, first_ref, second_ref)):
        for m in range(n_cols):
            ref[info_ref[1] ^ m] = refs[v * n_cols + m][...]
    dots = dots_ref[...]

    def column(j):
        return dots[:, j : j + 1]

    def total(value):
        return jnp.sum(value, axis=0, keepdims=True)

    rr0 = total(column(0))
    ab = total(column(1))
    alpha0 = rr0 / ab
    delta = alpha0 - column(3)
    rr1 = total(column(4) - 2.0 * delta * column(5) + delta * delta * column(2))
    curved = total(column(6) - delta * column(7) + delta * delta * column(8))
    crossed = total(column(5) - delta * column(2))
    beta = rr1 / rr0
    alpha1 = rr1 / (curved + 2.0 * beta * crossed + beta * beta * ab)
    along = alpha0 + alpha1 * (1.0 + beta)
    across = alpha1 * alpha0
    blocks = x_ref.shape[1] // (share * n_cols)
    for b in range(blocks):

        def gather(ref):
            return jnp.concatenate(
                [ref[m, :, b * share : (b + 1) * share] for m in range(n_cols)], axis=1
            )

        field, first, second = gather(field_ref), gather(first_ref), gather(second_ref)
        here = slice(b * share * n_cols, (b + 1) * share * n_cols)
        x_out[:, here] = x_ref[:, here] + along * field - across * first
        r_out[:, here] = field - along * first + across * second


def flip(value, axis, bit):
    size = lax.axis_size(axis)
    return lax.ppermute(value, axis, [(i, i ^ bit) for i in range(size)])


def swap(sent):
    return [sent[0]] + [flip(sent[m], "cols", m) for m in range(1, sent.shape[0])]


def after(value, other):
    return lax.optimization_barrier((value, other))[0]


def add_all(value):
    for axis in ("cols", "rows"):
        bit = 1
        while bit < lax.axis_size(axis):
            value = value + flip(value, axis, bit)
            bit *= 2
    return value


def on_device(user_factors, item_factors, tile_user, tile_item, tile_count, tile_mask):
    side = tile_mask.shape[1]
    col_width = user_factors.shape[0]
    column = lax.axis_index("cols").astype(jnp.int32)
    row = lax.axis_index("rows").astype(jnp.int32)
    row_devs = lax.axis_size("rows")
    n_cols = lax.axis_size("cols")
    devices = row_devs * n_cols
    width = col_width * n_cols
    tile_total = tile_user.shape[0]
    users = user_factors.shape[1]
    user_blocks = users // side
    item_blocks = item_factors.shape[1] // side
    share = side // n_cols
    own_users = users // n_cols
    capacity = max(2, (tile_total + row_devs - 1) // row_devs)
    direct = row_devs == 8
    vmem = pl.BlockSpec(memory_space=pltpu.VMEM)
    smem = pl.BlockSpec(memory_space=pltpu.SMEM)
    anywhere = pl.BlockSpec(memory_space=pl.ANY)
    params = pltpu.CompilerParams(vmem_limit_bytes=LIMIT)

    def call(kernel, out_shape, in_specs, name, scratch=(), flops=0):
        return pl.pallas_call(
            kernel,
            out_shape=out_shape,
            in_specs=in_specs,
            out_specs=jax.tree.map(lambda _: vmem, out_shape),
            scratch_shapes=scratch,
            compiler_params=params,
            cost_estimate=pl.CostEstimate(
                flops=flops, bytes_accessed=0, transcendentals=0
            ),
            name=name,
        )

    info = jnp.stack([tile_count[0], column])
    order = jnp.arange(tile_total, dtype=jnp.int32)
    live = (order < tile_count[0]).astype(jnp.int32)
    holder = tile_item // item_blocks
    local_block = tile_item % item_blocks
    earlier = (
        (holder[None, :] == holder[:, None])
        & (order[None, :] < order[:, None])
        & (live[None, :] > 0)
    )
    rank = jnp.sum(earlier.astype(jnp.int32), axis=1)
    near = row if direct else 0
    places = (holder ^ near) * capacity + jnp.minimum(rank, capacity - 1)
    slot_range = jnp.arange(row_devs * capacity, dtype=jnp.int32)
    hits = ((places[None, :] == slot_range[:, None]) & (live[None, :] > 0)).astype(jnp.int32)
    requests = (jnp.sum(hits * (local_block + 1)[None, :], axis=1) - 1).reshape(row_devs, capacity)
    places = jnp.where(live > 0, places, places[0])
    tile_users = jnp.where(live > 0, tile_user, tile_user[0])
    if direct:
        wanted = [flip(requests[j], "rows", j) if j else requests[j] for j in range(row_devs)]
    else:
        wanted = [lax.all_to_all(requests, "rows", split_axis=0, concat_axis=0, tiled=True).reshape(-1)]

    span = item_factors.shape[1] // n_cols
    sent = jax.ShapeDtypeStruct((n_cols, col_width, own_users), f32)
    strengths = jax.ShapeDtypeStruct((tile_total, share, side), bf16)
    start, own_items, mask = call(
        prepare_kernel,
        [sent, jax.ShapeDtypeStruct((n_cols, col_width, span), bf16), strengths],
        [smem, vmem, vmem, pl.BlockSpec(memory_space=pltpu.HBM)],
        "prepare",
        [pltpu.SemaphoreType.DMA],
        10**9,
    )(info, user_factors, item_factors, tile_mask)
    own_items = swap(own_items)
    start = swap(start)

    picked = call(
        functools.partial(pick_kernel, side),
        [jax.ShapeDtypeStruct((len(value), col_width, side), bf16) for value in wanted],
        [vmem] + [smem] * len(wanted),
        "pick",
        flops=10**9,
    )(item_factors, *wanted)
    if direct:
        far = [flip(picked[j], "rows", j) for j in (4, 5)]
        close = [flip(picked[j], "rows", j) for j in (1, 2, 3)]
        last = [flip(after(picked[j + 2], far[j - 4]), "rows", j + 2) for j in (4, 5)]
        groups = [[picked[0]], close, far, last]
        groups = [jnp.concatenate(group, axis=0) for group in groups]
    else:
        groups = [lax.all_to_all(picked[0], "rows", split_axis=0, concat_axis=0, tiled=True)]
    pieces = []
    for own in groups:
        bit = n_cols // 2
        while bit > 1:
            own = jnp.concatenate([own, flip(own, "cols", bit)], axis=0)
            bit //= 2
        pieces += [own, flip(own, "cols", 1)]

    square = jax.ShapeDtypeStruct((width, width), f32)
    gram = call(
        gram_kernel,
        square,
        [smem] + [vmem] * n_cols,
        "gram",
        [pltpu.VMEM((width, span), bf16)],
        10**9,
    )(info, *own_items)
    gram = add_all(gram)

    vector = jax.ShapeDtypeStruct((own_users, width), f32)
    held = jax.ShapeDtypeStruct((row_devs * capacity, width, side), bf16)
    work = [
        pltpu.VMEM((user_blocks, 2 * share, width), bf16),
        pltpu.VMEM((user_blocks, share, width), f32),
        pltpu.VMEM((2, UNROLL, 2 * share, side), bf16),
    ]
    lists = (places, tile_users, info)
    field_sent, field, y = call(
        functools.partial(start_kernel, n_cols),
        [sent, vector, held],
        [smem] * 3 + [vmem] * (2 + n_cols) + [anywhere] * len(pieces),
        "start",
        [pltpu.VMEM((width, own_users), f32)]
        + work
        + [pltpu.SemaphoreType.DMA((n_cols * len(groups),))],
        8 * 10**9,
    )(*lists, gram, mask, *start, *pieces)
    first_sent, first = call(
        first_kernel, [sent, vector], [smem] * 3 + [vmem] * 4, "first", work, 8 * 10**9
    )(*lists, field, gram, y, mask)
    second_sent, dots = call(
        second_kernel,
        [sent, jax.ShapeDtypeStruct((devices, 128), f32)],
        [smem] * 3 + [vmem] * 5,
        "second",
        work,
        8 * 10**9,
    )(*lists, field, first, gram, y, mask)

    turned = swap(field_sent) + swap(first_sent) + swap(second_sent)
    dots = lax.all_to_all(dots, ("rows", "cols"), split_axis=0, concat_axis=0, tiled=True)
    result = jax.ShapeDtypeStruct((col_width, users), f32)
    return tuple(
        call(
            functools.partial(finish_kernel, share),
            [result, result],
            [smem] + [vmem] * (2 + 3 * n_cols),
            "finish",
            [pltpu.VMEM((n_cols, col_width, own_users), f32)] * 3,
            10**9,
        )(info, dots, user_factors, *turned)
    )


def solution(mesh):
    return jax.shard_map(
        on_device,
        mesh=mesh,
        in_specs=(
            P("cols", "rows"),
            P("cols", "rows"),
            P("rows"),
            P("rows"),
            P("rows"),
            P("rows", None, None),
        ),
        out_specs=(P("cols", "rows"), P("cols", "rows")),
        check_vma=False,
    )
```

```python
import functools

import jax
import jax.numpy as jnp
from jax import lax
from jax.experimental import pallas as pl
from jax.experimental.pallas import tpu as pltpu
from jax.sharding import PartitionSpec as P

ridge = 0.5
confidence = 40.0
UNROLL = 8
LIMIT = 24 * 1024 * 1024
f32 = jnp.float32
bf16 = jnp.bfloat16


def matmul(left, right):
    return jnp.dot(left, right, preferred_element_type=f32)


def split(value):
    high = value.astype(bf16)
    low = (value - high.astype(f32)).astype(bf16)
    return high, low


def prepare_kernel(n_cols, side, info_ref, x_hbm, items_hbm, *refs):
    sent, (x_ref, x_pieces, sems) = refs[:n_cols], refs[n_cols:]
    column = info_ref[1]
    share = side // n_cols
    blocks = x_ref.shape[1] // side
    own_users = blocks * share
    span = sent[0].shape[1] - 2 * own_users
    copies = [
        pltpu.make_async_copy(
            items_hbm.at[:, pl.ds(pl.multiple_of((column ^ m) * span, span), span)],
            sent[m].at[:, pl.ds(2 * own_users, span)],
            sems.at[m],
        )
        for m in range(n_cols)
    ]
    fetch = pltpu.make_async_copy(x_hbm, x_ref, sems.at[n_cols])
    fetch.start()
    for copy in copies:
        copy.start()
    fetch.wait()
    for m in range(n_cols):
        x_pieces[m] = jnp.concatenate(
            [x_ref[:, b * side + m * share : b * side + (m + 1) * share] for b in range(blocks)],
            axis=1,
        )
    for m in range(n_cols):
        high, low = split(x_pieces[column ^ m])
        sent[m][:, :own_users] = high
        sent[m][:, own_users : 2 * own_users] = low
    for copy in copies:
        copy.wait()


def mask_kernel(info_ref, mask_hbm, mask, sem):
    tiles, share, side = mask.shape
    copy = pltpu.make_async_copy(
        mask_hbm.at[:, pl.ds(pl.multiple_of(info_ref[1] * share, share), share), :], mask, sem
    )
    copy.start()
    copy.wait()

    def clear(t, carry):
        mask[t] = jnp.zeros((share, side), bf16)
        return carry

    lax.fori_loop(info_ref[0], tiles, clear, 0)


def pick_kernel(direct, info_ref, wanted_ref, items_ref, *out_refs):
    capacity = wanted_ref.shape[1]
    side = out_refs[0].shape[2]
    for o, out_ref in enumerate(out_refs):
        for i in range(out_ref.shape[0] // capacity):
            dest = info_ref[2] ^ o if direct else i
            for r in range(capacity):
                block = jnp.maximum(wanted_ref[dest, r], 0)
                start = pl.multiple_of(block * side, side)
                out_ref[i * capacity + r] = items_ref[:, pl.ds(start, side)]


def pack(ref, gram):
    high, low = split(gram)
    both = jnp.concatenate([high, low], axis=1)
    for k in range(ref.shape[0]):
        ref[k] = both[k * ref.shape[1] : (k + 1) * ref.shape[1]]


def unpack(blocks):
    both = jnp.concatenate([blocks[k] for k in range(blocks.shape[0])], axis=0).astype(f32)
    width = both.shape[1] // 2
    return both[:, :width] + both[:, width:]


def gram_kernel(own_users, info_ref, *refs):
    column = info_ref[1]
    pieces = refs[:-6]
    out_ref, pack_ref, start_ref, starts, items, sems = refs[-6:]
    width = pieces[0].shape[0]
    span = items.shape[1]
    copies = []
    for m, piece in enumerate(pieces):
        place = pl.ds(pl.multiple_of((column ^ m) * width, width), width)
        for source, target in (
            (piece.at[:, pl.ds(0, 2 * own_users)], starts.at[place, :]),
            (piece.at[:, pl.ds(2 * own_users, span)], items.at[place, :]),
        ):
            copies.append(pltpu.make_async_copy(source, target, sems.at[len(copies)]))
            copies[-1].start()
    for copy in copies:
        copy.wait()
    both = starts[...].astype(f32)
    start_ref[...] = both[:, :own_users] + both[:, own_users:]
    gram = lax.dot_general(
        items[...], items[...], (((1,), (1,)), ((), ())), preferred_element_type=f32
    )
    out_ref[...] = gram
    pack(pack_ref, gram)


def add_kernel(gram_ref, arrived_ref, out_ref, pack_ref):
    extra = pack_ref.shape[0]
    total = gram_ref[...] + unpack(arrived_ref[arrived_ref.shape[0] - extra :])
    out_ref[...] = total
    pack(pack_ref, total)


def load(p_hl, vector):
    blocks, both, width = p_hl.shape
    share = both // 2
    high, low = split(vector)
    p_hl[:, :share] = high.reshape(blocks, share, width)
    p_hl[:, share:] = low.reshape(blocks, share, width)


def dense(p_hl, gram_ref, vector):
    blocks, both, width = p_hl.shape
    gram_high, gram_low = split(gram_ref[...])
    product = matmul(
        p_hl[...].reshape(blocks * both, width),
        jnp.concatenate([gram_high, gram_low], axis=1),
    ).reshape(blocks, 2, both // 2, 2 * width)
    product = product[:, 0] + product[:, 1]
    product = product[:, :, :width] + product[:, :, width:]
    return product.reshape(vector.shape) + ridge * vector


def sparse(starting, slot_ref, user_ref, y, mask, p_hl, acc, held):
    tiles, share, side = mask.shape
    groups = tiles // UNROLL
    acc[...] = jnp.zeros_like(acc)

    def score(group):
        for j in range(UNROLL):
            t = group * UNROLL + j
            scores = matmul(p_hl[user_ref[t]], y[slot_ref[t]])
            scores = scores[:share] + scores[share:]
            if starting:
                scores = (1.0 + confidence) - confidence * scores
            high, low = split(mask[t].astype(f32) * scores)
            held[group % 2, j, :share] = high
            held[group % 2, j, share:] = low

    def collect(group):
        terms = []
        for j in range(UNROLL):
            t = group * UNROLL + j
            term = lax.dot_general(
                held[group % 2, j],
                y[slot_ref[t]],
                (((1,), (1,)), ((), ())),
                preferred_element_type=f32,
            )
            terms.append(term[:share] + term[share:])
        return terms

    def add(group, terms):
        for j, term in enumerate(terms):
            acc[user_ref[group * UNROLL + j]] += term

    score(0)

    def step(group, carry):
        terms = collect(group - 1)
        score(group)
        add(group - 1, terms)
        return carry

    lax.fori_loop(1, groups, step, 0)
    add(groups - 1, collect(groups - 1))


def put(column, ref, vector, part=0):
    n_cols, rows, _ = ref.shape
    turned = vector.T
    width = turned.shape[0] // n_cols
    for m in range(n_cols):
        ref[column ^ m, part * width : (part + 1) * width] = turned[m * width : (m + 1) * width]


def start_kernel(
    n_cols, slots, extra, slot_ref, user_ref, info_ref, x_ref, gram_ref, mask, *refs
):
    pieces = refs[: 2 * len(slots)]
    sent_ref, field_ref, gram_out, y, tail, p_hl, acc, held, sems = refs[2 * len(slots) :]
    piece_width = y.shape[1] // n_cols
    column = info_ref[1]
    copies = []
    base = 0
    for k, count in enumerate(slots):
        for m in range(n_cols):
            place = pl.multiple_of((column ^ m) * piece_width, piece_width)
            source = pieces[2 * k + m % 2].at[pl.ds(m // 2 * count, count)]
            copies.append(
                pltpu.make_async_copy(
                    source,
                    y.at[pl.ds(base, count), pl.ds(place, piece_width), :],
                    sems.at[len(copies)],
                )
            )
        base += count
    if extra:
        blocks = pieces[-1].shape[0]
        copies.append(
            pltpu.make_async_copy(
                pieces[-1].at[pl.ds(blocks - extra, extra)], tail, sems.at[len(copies)]
            )
        )
    for copy in copies:
        copy.start()
    start = x_ref[...].T
    load(p_hl, start)
    for copy in copies:
        copy.wait()
    gram = gram_ref[...]
    if extra:
        gram = gram + unpack(tail)
    gram_out[...] = gram
    sparse(True, slot_ref, user_ref, y, mask, p_hl, acc, held)
    field = acc[...].reshape(start.shape) - dense(p_hl, gram_out, start)
    field_ref[...] = field
    put(column, sent_ref, field)


def first_kernel(
    slot_ref, user_ref, info_ref, field_ref, gram_ref, y, mask, first_ref, p_hl, acc, held
):
    field = field_ref[...]
    load(p_hl, field)
    sparse(False, slot_ref, user_ref, y, mask, p_hl, acc, held)
    first = confidence * acc[...].reshape(field.shape) + dense(p_hl, gram_ref, field)
    first_ref[...] = first


def second_kernel(
    slot_ref, user_ref, info_ref, field_ref, first_ref, gram_ref, y, mask, sent_ref, dots_ref, p_hl, acc, held
):
    field = field_ref[...]
    first = first_ref[...]
    load(p_hl, first)
    sparse(False, slot_ref, user_ref, y, mask, p_hl, acc, held)
    second = confidence * acc[...].reshape(field.shape) + dense(p_hl, gram_ref, first)
    put(info_ref[1], sent_ref, first)
    put(info_ref[1], sent_ref, second, 1)

    def total(left, right):
        return jnp.sum(left * right)

    aa, ab, bb = total(field, field), total(field, first), total(first, first)
    guess = jnp.where(bb > 0.0, ab / jnp.where(bb > 0.0, bb, 1.0), 0.0)
    near = field - guess * first
    near_image = first - guess * second
    values = (
        aa,
        ab,
        bb,
        guess,
        total(near, near),
        total(near, first),
        total(near, near_image),
        total(near, second) + total(first, near_image),
        total(first, second),
    )
    lane = lax.broadcasted_iota(jnp.int32, dots_ref.shape, 1)
    dots = jnp.zeros(dots_ref.shape, f32)
    for j, value in enumerate(values):
        dots = jnp.where(lane == j, value, dots)
    dots_ref[...] = dots


def finish_kernel(share, info_ref, dots_ref, x_ref, *refs):
    n_cols = (len(refs) - 5) // 2
    x_out, r_out, field_ref, first_ref, second_ref = refs[2 * n_cols :]
    width = field_ref.shape[1]
    for m in range(n_cols):
        place = info_ref[1] ^ m
        field_ref[place] = refs[m][...]
        first_ref[place] = refs[n_cols + m][:width]
        second_ref[place] = refs[n_cols + m][width:]
    dots = dots_ref[...]

    def column(j):
        return dots[:, j : j + 1]

    def total(value):
        return jnp.sum(value, axis=0, keepdims=True)

    rr0 = total(column(0))
    ab = total(column(1))
    alpha0 = rr0 / ab
    delta = alpha0 - column(3)
    rr1 = total(column(4) - 2.0 * delta * column(5) + delta * delta * column(2))
    curved = total(column(6) - delta * column(7) + delta * delta * column(8))
    crossed = total(column(5) - delta * column(2))
    beta = rr1 / rr0
    alpha1 = rr1 / (curved + 2.0 * beta * crossed + beta * beta * ab)
    along = alpha0 + alpha1 * (1.0 + beta)
    across = alpha1 * alpha0
    blocks = x_ref.shape[1] // (share * n_cols)
    for b in range(blocks):

        def gather(ref):
            return jnp.concatenate(
                [ref[m, :, b * share : (b + 1) * share] for m in range(n_cols)], axis=1
            )

        field, first, second = gather(field_ref), gather(first_ref), gather(second_ref)
        here = slice(b * share * n_cols, (b + 1) * share * n_cols)
        x_out[:, here] = x_ref[:, here] + along * field - across * first
        r_out[:, here] = field - along * first + across * second


def flip(value, axis, bit):
    size = lax.axis_size(axis)
    return lax.ppermute(value, axis, [(i, i ^ bit) for i in range(size)])


def swap(sent):
    return [sent[0]] + [flip(sent[m], "cols", m) for m in range(1, len(sent))]


def after(value, *others):
    return lax.optimization_barrier((value, *others))[0]


def add_all(value):
    for axis in ("cols", "rows"):
        bit = 1
        while bit < lax.axis_size(axis):
            value = value + flip(value, axis, bit)
            bit *= 2
    return value


def on_device(user_factors, item_factors, tile_user, tile_item, tile_count, tile_mask):
    side = tile_mask.shape[1]
    col_width = user_factors.shape[0]
    column = lax.axis_index("cols").astype(jnp.int32)
    row = lax.axis_index("rows").astype(jnp.int32)
    row_devs = lax.axis_size("rows")
    n_cols = lax.axis_size("cols")
    devices = row_devs * n_cols
    width = col_width * n_cols
    tile_total = tile_user.shape[0]
    users = user_factors.shape[1]
    user_blocks = users // side
    item_blocks = item_factors.shape[1] // side
    share = side // n_cols
    own_users = users // n_cols
    capacity = max(2, (tile_total + row_devs - 1) // row_devs)
    direct = row_devs == 8 and 2 * width == side
    vmem = pl.BlockSpec(memory_space=pltpu.VMEM)
    smem = pl.BlockSpec(memory_space=pltpu.SMEM)
    anywhere = pl.BlockSpec(memory_space=pl.ANY)
    params = pltpu.CompilerParams(vmem_limit_bytes=LIMIT)

    def call(kernel, out_shape, in_specs, name, scratch=(), flops=0):
        return pl.pallas_call(
            kernel,
            out_shape=out_shape,
            in_specs=in_specs,
            out_specs=jax.tree.map(lambda _: vmem, out_shape),
            scratch_shapes=scratch,
            compiler_params=params,
            cost_estimate=pl.CostEstimate(
                flops=flops, bytes_accessed=0, transcendentals=0
            ),
            name=name,
        )

    info = jnp.stack([tile_count[0], column, row])
    span = item_factors.shape[1] // n_cols
    sent = call(
        functools.partial(prepare_kernel, n_cols, side),
        [jax.ShapeDtypeStruct((col_width, 2 * own_users + span), bf16)] * n_cols,
        [smem, anywhere, anywhere],
        "prepare",
        [
            pltpu.VMEM(user_factors.shape, f32),
            pltpu.VMEM((n_cols, col_width, own_users), f32),
            pltpu.SemaphoreType.DMA((n_cols + 1,)),
        ],
        10**9,
    )(
        info,
        pltpu.with_memory_space_constraint(user_factors, pltpu.HBM),
        pltpu.with_memory_space_constraint(item_factors, pltpu.HBM),
    )
    shared = swap(sent)

    order = jnp.arange(tile_total, dtype=jnp.int32)
    live = (order < tile_count[0]).astype(jnp.int32)
    tile_item = after(tile_item, sent[0])
    holder = tile_item // item_blocks
    local_block = tile_item % item_blocks
    earlier = (
        (holder[None, :] == holder[:, None])
        & (order[None, :] < order[:, None])
        & (live[None, :] > 0)
    )
    rank = jnp.sum(earlier.astype(jnp.int32), axis=1)
    slot_ids = jnp.minimum(holder * capacity + rank, row_devs * capacity - 1)
    slot_range = jnp.arange(row_devs * capacity, dtype=jnp.int32)
    hits = ((slot_ids[None, :] == slot_range[:, None]) & (live[None, :] > 0)).astype(jnp.int32)
    requests = (jnp.sum(hits * (local_block + 1)[None, :], axis=1) - 1).reshape(row_devs, capacity)
    wanted = lax.all_to_all(requests, "rows", split_axis=0, concat_axis=0, tiled=True)
    block = holder
    if direct:
        step = holder ^ row
        block = step
        for j, spot in ((1, 1), (3, 2), (2, 3), (5, 4), (6, 5), (7, 6), (4, 7)):
            block = jnp.where(step == j, spot, block)
    places = block * capacity + jnp.minimum(rank, capacity - 1)
    places = jnp.where(live > 0, places, places[0])
    tile_users = jnp.where(live > 0, tile_user, tile_user[0])

    picked = call(
        functools.partial(pick_kernel, direct),
        [jax.ShapeDtypeStruct((capacity, col_width, side), bf16)] * row_devs
        if direct
        else [jax.ShapeDtypeStruct((row_devs * capacity, col_width, side), bf16)],
        [smem, smem, vmem],
        "pick",
        flops=10**9,
    )(after(info, *shared), wanted, item_factors)

    def join(*arrays):
        return jnp.concatenate(arrays, axis=0)

    def add(gram, arrived):
        return call(add_kernel, [square, packed], [vmem] * 2, "add")(gram, arrived)

    got = {0: picked[0]}
    if direct:
        for j, ready in ((1, None), (3, None), (2, None), (5, None), (6, None), (7, 3), (4, 5)):
            message = picked[j] if ready is None else after(picked[j], got[ready])
            got[j] = flip(message, "rows", j)

    strengths = jax.ShapeDtypeStruct((tile_total, share, side), bf16)
    (mask,) = call(
        mask_kernel,
        [strengths],
        [smem, anywhere],
        "mask",
        [pltpu.SemaphoreType.DMA],
        10**9,
    )(
        after(info, got[1] if direct else picked[0]),
        pltpu.with_memory_space_constraint(tile_mask, pltpu.HBM),
    )
    square = jax.ShapeDtypeStruct((width, width), f32)
    extra = width // col_width
    packed = jax.ShapeDtypeStruct((extra, col_width, 2 * width), bf16)
    gram, carried, start = call(
        functools.partial(gram_kernel, own_users),
        [square, packed, jax.ShapeDtypeStruct((width, own_users), f32)],
        [smem] + [anywhere] * n_cols,
        "gram",
        [
            pltpu.VMEM((width, 2 * own_users), bf16),
            pltpu.VMEM((width, span), bf16),
            pltpu.SemaphoreType.DMA((2 * n_cols,)),
        ],
        10**9,
    )(after(info, got[1] if direct else picked[0]), *shared)
    if direct:
        slots = (3 * capacity, 3 * capacity, 2 * capacity)
        pieces = []
        for group in ((0, 1, 3), (2, 5, 6)):
            own = join(*[got[j] for j in group])
            own = after(own, got[6], *pieces[:1])
            own = join(own, flip(own, "cols", 2))
            pieces += [own, flip(own, "cols", 1)]
        carried = after(carried, got[7])
        for bit in (1, 2, 4):
            gram, carried = add(gram, flip(carried, "rows", bit))
        own = join(got[7], got[4])
        arrived = flip(join(own, carried), "cols", 2)
        gram, carried = add(gram, arrived)
        own = join(own, arrived[: 2 * capacity], carried)
        pieces += [own, flip(own, "cols", 1)]
    else:
        slots = (row_devs * capacity,)
        extra = 0
        gram = add_all(gram)
        own = lax.all_to_all(picked[0], "rows", split_axis=0, concat_axis=0, tiled=True)
        own = join(own, flip(own, "cols", 2))
        pieces = [own, flip(own, "cols", 1)]

    vector = jax.ShapeDtypeStruct((own_users, width), f32)
    held = jax.ShapeDtypeStruct((row_devs * capacity, width, side), bf16)
    work = [
        pltpu.VMEM((user_blocks, 2 * share, width), bf16),
        pltpu.VMEM((user_blocks, share, width), f32),
        pltpu.VMEM((2, UNROLL, 2 * share, side), bf16),
    ]
    lists = (places, tile_users, info)
    field_sent, field, gram, y = call(
        functools.partial(start_kernel, n_cols, slots, extra),
        [
            jax.ShapeDtypeStruct((n_cols, col_width, own_users), f32),
            vector,
            square,
            held,
        ],
        [smem] * 3 + [vmem] * 3 + [anywhere] * len(pieces),
        "start",
        [pltpu.VMEM(packed.shape, bf16)]
        + work
        + [pltpu.SemaphoreType.DMA((n_cols * len(slots) + 1,))],
        8 * 10**9,
    )(*lists, start, gram, mask, *pieces)
    (first,) = call(
        first_kernel, [vector], [smem] * 3 + [vmem] * 4, "first", work, 8 * 10**9
    )(*lists, field, gram, y, mask)
    turned = swap(field_sent)
    field = after(field, *turned)
    second_sent, dots = call(
        second_kernel,
        [
            jax.ShapeDtypeStruct((n_cols, 2 * col_width, own_users), f32),
            jax.ShapeDtypeStruct((devices, 128), f32),
        ],
        [smem] * 3 + [vmem] * 5,
        "second",
        work,
        8 * 10**9,
    )(*lists, field, first, gram, y, mask)

    turned += swap(second_sent)
    dots = lax.all_to_all(dots, ("rows", "cols"), split_axis=0, concat_axis=0, tiled=True)
    result = jax.ShapeDtypeStruct((col_width, users), f32)
    return tuple(
        call(
            functools.partial(finish_kernel, share),
            [result, result],
            [smem] + [vmem] * (2 + 2 * n_cols),
            "finish",
            [pltpu.VMEM((n_cols, col_width, own_users), f32)] * 3,
            10**9,
        )(info, dots, user_factors, *turned)
    )


def solution(mesh):
    return jax.shard_map(
        on_device,
        mesh=mesh,
        in_specs=(
            P("cols", "rows"),
            P("cols", "rows"),
            P("rows"),
            P("rows"),
            P("rows"),
            P("rows", None, None),
        ),
        out_specs=(P("cols", "rows"), P("cols", "rows")),
        check_vma=False,
    )
```

```python
import functools

import jax
import jax.numpy as jnp
from jax import lax
from jax.experimental import pallas as pl
from jax.experimental.pallas import tpu as pltpu
from jax.sharding import PartitionSpec as P

ridge = 0.5
confidence = 40.0
UNROLL = 8
LIMIT = 24 * 1024 * 1024
f32 = jnp.float32
bf16 = jnp.bfloat16


def matmul(left, right):
    return jnp.dot(left, right, preferred_element_type=f32)


def split(value):
    high = value.astype(bf16)
    low = (value - high.astype(f32)).astype(bf16)
    return high, low


def prepare_kernel(n_cols, side, info_ref, x_hbm, items_hbm, *refs):
    sent, (x_ref, x_pieces, sems) = refs[:n_cols], refs[n_cols:]
    column = info_ref[1]
    share = side // n_cols
    blocks = x_ref.shape[1] // side
    own_users = blocks * share
    span = sent[0].shape[1] - 2 * own_users
    copies = [
        pltpu.make_async_copy(
            items_hbm.at[:, pl.ds(pl.multiple_of((column ^ m) * span, span), span)],
            sent[m].at[:, pl.ds(2 * own_users, span)],
            sems.at[m],
        )
        for m in range(n_cols)
    ]
    fetch = pltpu.make_async_copy(x_hbm, x_ref, sems.at[n_cols])
    fetch.start()
    for copy in copies:
        copy.start()
    fetch.wait()
    for m in range(n_cols):
        x_pieces[m] = jnp.concatenate(
            [x_ref[:, b * side + m * share : b * side + (m + 1) * share] for b in range(blocks)],
            axis=1,
        )
    for m in range(n_cols):
        high, low = split(x_pieces[column ^ m])
        sent[m][:, :own_users] = high
        sent[m][:, own_users : 2 * own_users] = low
    for copy in copies:
        copy.wait()


def mask_kernel(info_ref, mask_hbm, mask, sem):
    tiles, share, side = mask.shape
    copy = pltpu.make_async_copy(
        mask_hbm.at[:, pl.ds(pl.multiple_of(info_ref[1] * share, share), share), :], mask, sem
    )
    copy.start()
    copy.wait()

    def clear(t, carry):
        mask[t] = jnp.zeros((share, side), bf16)
        return carry

    lax.fori_loop(info_ref[0], tiles, clear, 0)


def pick_kernel(direct, info_ref, wanted_ref, items_ref, *out_refs):
    capacity = wanted_ref.shape[1]
    side = out_refs[0].shape[2]
    for o, out_ref in enumerate(out_refs):
        for i in range(out_ref.shape[0] // capacity):
            dest = info_ref[2] ^ o if direct else i
            for r in range(capacity):
                block = jnp.maximum(wanted_ref[dest, r], 0)
                start = pl.multiple_of(block * side, side)
                out_ref[i * capacity + r] = items_ref[:, pl.ds(start, side)]


def pack(ref, gram):
    high, low = split(gram)
    both = jnp.concatenate([high, low], axis=1)
    for k in range(ref.shape[0]):
        ref[k] = both[k * ref.shape[1] : (k + 1) * ref.shape[1]]


def unpack(blocks):
    both = jnp.concatenate([blocks[k] for k in range(blocks.shape[0])], axis=0).astype(f32)
    width = both.shape[1] // 2
    return both[:, :width] + both[:, width:]


def gram_kernel(own_users, info_ref, *refs):
    column = info_ref[1]
    pieces = refs[:-6]
    out_ref, pack_ref, start_ref, starts, items, sems = refs[-6:]
    width = pieces[0].shape[0]
    span = items.shape[1]
    copies = []
    for m, piece in enumerate(pieces):
        place = pl.ds(pl.multiple_of((column ^ m) * width, width), width)
        for source, target in (
            (piece.at[:, pl.ds(0, 2 * own_users)], starts.at[place, :]),
            (piece.at[:, pl.ds(2 * own_users, span)], items.at[place, :]),
        ):
            copies.append(pltpu.make_async_copy(source, target, sems.at[len(copies)]))
            copies[-1].start()
    for copy in copies:
        copy.wait()
    both = starts[...].astype(f32)
    start_ref[...] = both[:, :own_users] + both[:, own_users:]
    gram = lax.dot_general(
        items[...], items[...], (((1,), (1,)), ((), ())), preferred_element_type=f32
    )
    out_ref[...] = gram
    pack(pack_ref, gram)


def add_kernel(gram_ref, arrived_ref, out_ref, pack_ref):
    extra = pack_ref.shape[0]
    total = gram_ref[...] + unpack(arrived_ref[arrived_ref.shape[0] - extra :])
    out_ref[...] = total
    pack(pack_ref, total)


def join_kernel(*refs):
    sources, out_ref, sems = refs[:-2], refs[-2], refs[-1]
    copies = []
    base = 0
    for source in sources:
        rows = source.shape[0]
        copies.append(
            pltpu.make_async_copy(source, out_ref.at[pl.ds(base, rows)], sems.at[len(copies)])
        )
        copies[-1].start()
        base += rows
    for copy in copies:
        copy.wait()


def load(p_hl, vector):
    blocks, both, width = p_hl.shape
    share = both // 2
    high, low = split(vector)
    p_hl[:, :share] = high.reshape(blocks, share, width)
    p_hl[:, share:] = low.reshape(blocks, share, width)


def dense(p_hl, gram_ref, vector):
    blocks, both, width = p_hl.shape
    gram_high, gram_low = split(gram_ref[...])
    product = matmul(
        p_hl[...].reshape(blocks * both, width),
        jnp.concatenate([gram_high, gram_low], axis=1),
    ).reshape(blocks, 2, both // 2, 2 * width)
    product = product[:, 0] + product[:, 1]
    product = product[:, :, :width] + product[:, :, width:]
    return product.reshape(vector.shape) + ridge * vector


def sparse(starting, slot_ref, user_ref, y, mask, p_hl, acc, held):
    tiles, share, side = mask.shape
    groups = tiles // UNROLL
    acc[...] = jnp.zeros_like(acc)

    def score(group):
        for j in range(UNROLL):
            t = group * UNROLL + j
            scores = matmul(p_hl[user_ref[t]], y[slot_ref[t]])
            scores = scores[:share] + scores[share:]
            if starting:
                scores = (1.0 + confidence) - confidence * scores
            high, low = split(mask[t].astype(f32) * scores)
            held[group % 2, j, :share] = high
            held[group % 2, j, share:] = low

    def collect(group):
        terms = []
        for j in range(UNROLL):
            t = group * UNROLL + j
            term = lax.dot_general(
                held[group % 2, j],
                y[slot_ref[t]],
                (((1,), (1,)), ((), ())),
                preferred_element_type=f32,
            )
            terms.append(term[:share] + term[share:])
        return terms

    def add(group, terms):
        for j, term in enumerate(terms):
            acc[user_ref[group * UNROLL + j]] += term

    score(0)

    def step(group, carry):
        terms = collect(group - 1)
        score(group)
        add(group - 1, terms)
        return carry

    lax.fori_loop(1, groups, step, 0)
    add(groups - 1, collect(groups - 1))


def put(column, ref, vector, part=0):
    n_cols, rows, _ = ref.shape
    turned = vector.T
    width = turned.shape[0] // n_cols
    for m in range(n_cols):
        ref[column ^ m, part * width : (part + 1) * width] = turned[m * width : (m + 1) * width]


def start_kernel(n_cols, slots, slot_ref, user_ref, info_ref, x_ref, mask, *refs):
    pieces = refs[: 2 * len(slots)]
    part_ref, y, p_hl, acc, held, sems = refs[2 * len(slots) :]
    piece_width = y.shape[1] // n_cols
    column = info_ref[1]
    copies = []
    base = 0
    for k, count in enumerate(slots):
        for m in range(n_cols):
            place = pl.multiple_of((column ^ m) * piece_width, piece_width)
            source = pieces[2 * k + m % 2].at[pl.ds(m // 2 * count, count)]
            copies.append(
                pltpu.make_async_copy(
                    source,
                    y.at[pl.ds(base, count), pl.ds(place, piece_width), :],
                    sems.at[len(copies)],
                )
            )
        base += count
    for copy in copies:
        copy.start()
    load(p_hl, x_ref[...].T)
    for copy in copies:
        copy.wait()
    sparse(True, slot_ref, user_ref, y, mask, p_hl, acc, held)
    part_ref[...] = acc[...].reshape(part_ref.shape)


def first_kernel(
    slot_ref, user_ref, info_ref, x_ref, part_ref, gram_ref, y, mask,
    sent_ref, field_ref, first_ref, p_hl, acc, held,
):
    start = x_ref[...].T
    load(p_hl, start)
    field = part_ref[...] - dense(p_hl, gram_ref, start)
    field_ref[...] = field
    put(info_ref[1], sent_ref, field)
    load(p_hl, field)
    sparse(False, slot_ref, user_ref, y, mask, p_hl, acc, held)
    first = confidence * acc[...].reshape(field.shape) + dense(p_hl, gram_ref, field)
    first_ref[...] = first
    put(info_ref[1], sent_ref, first, 1)


def second_kernel(
    slot_ref, user_ref, info_ref, field_ref, first_ref, gram_ref, y, mask, sent_ref, dots_ref, p_hl, acc, held
):
    field = field_ref[...]
    first = first_ref[...]
    load(p_hl, first)
    sparse(False, slot_ref, user_ref, y, mask, p_hl, acc, held)
    second = confidence * acc[...].reshape(field.shape) + dense(p_hl, gram_ref, first)
    put(info_ref[1], sent_ref, second)

    def total(left, right):
        return jnp.sum(left * right)

    aa, ab, bb = total(field, field), total(field, first), total(first, first)
    guess = jnp.where(bb > 0.0, ab / jnp.where(bb > 0.0, bb, 1.0), 0.0)
    near = field - guess * first
    near_image = first - guess * second
    values = (
        aa,
        ab,
        bb,
        guess,
        total(near, near),
        total(near, first),
        total(near, near_image),
        total(near, second) + total(first, near_image),
        total(first, second),
    )
    lane = lax.broadcasted_iota(jnp.int32, dots_ref.shape, 1)
    dots = jnp.zeros(dots_ref.shape, f32)
    for j, value in enumerate(values):
        dots = jnp.where(lane == j, value, dots)
    dots_ref[...] = dots


def finish_kernel(share, info_ref, dots_ref, x_ref, *refs):
    n_cols = (len(refs) - 5) // 2
    x_out, r_out, field_ref, first_ref, second_ref = refs[2 * n_cols :]
    width = field_ref.shape[1]
    for m in range(n_cols):
        place = info_ref[1] ^ m
        field_ref[place] = refs[m][:width]
        first_ref[place] = refs[m][width:]
        second_ref[place] = refs[n_cols + m][...]
    dots = dots_ref[...]

    def column(j):
        return dots[:, j : j + 1]

    def total(value):
        return jnp.sum(value, axis=0, keepdims=True)

    rr0 = total(column(0))
    ab = total(column(1))
    alpha0 = rr0 / ab
    delta = alpha0 - column(3)
    rr1 = total(column(4) - 2.0 * delta * column(5) + delta * delta * column(2))
    curved = total(column(6) - delta * column(7) + delta * delta * column(8))
    crossed = total(column(5) - delta * column(2))
    beta = rr1 / rr0
    alpha1 = rr1 / (curved + 2.0 * beta * crossed + beta * beta * ab)
    along = alpha0 + alpha1 * (1.0 + beta)
    across = alpha1 * alpha0
    blocks = x_ref.shape[1] // (share * n_cols)
    for b in range(blocks):

        def gather(ref):
            return jnp.concatenate(
                [ref[m, :, b * share : (b + 1) * share] for m in range(n_cols)], axis=1
            )

        field, first, second = gather(field_ref), gather(first_ref), gather(second_ref)
        here = slice(b * share * n_cols, (b + 1) * share * n_cols)
        x_out[:, here] = x_ref[:, here] + along * field - across * first
        r_out[:, here] = field - along * first + across * second


def flip(value, axis, bit):
    size = lax.axis_size(axis)
    return lax.ppermute(value, axis, [(i, i ^ bit) for i in range(size)])


def swap(sent):
    return [sent[0]] + [flip(sent[m], "cols", m) for m in range(1, len(sent))]


def after(value, *others):
    return lax.optimization_barrier((value, *others))[0]


def add_all(value):
    for axis in ("cols", "rows"):
        bit = 1
        while bit < lax.axis_size(axis):
            value = value + flip(value, axis, bit)
            bit *= 2
    return value


def on_device(user_factors, item_factors, tile_user, tile_item, tile_count, tile_mask):
    side = tile_mask.shape[1]
    col_width = user_factors.shape[0]
    column = lax.axis_index("cols").astype(jnp.int32)
    row = lax.axis_index("rows").astype(jnp.int32)
    row_devs = lax.axis_size("rows")
    n_cols = lax.axis_size("cols")
    devices = row_devs * n_cols
    width = col_width * n_cols
    tile_total = tile_user.shape[0]
    users = user_factors.shape[1]
    user_blocks = users // side
    item_blocks = item_factors.shape[1] // side
    share = side // n_cols
    own_users = users // n_cols
    capacity = max(2, (tile_total + row_devs - 1) // row_devs)
    direct = row_devs == 8 and 2 * width == side
    vmem = pl.BlockSpec(memory_space=pltpu.VMEM)
    smem = pl.BlockSpec(memory_space=pltpu.SMEM)
    anywhere = pl.BlockSpec(memory_space=pl.ANY)
    params = pltpu.CompilerParams(vmem_limit_bytes=LIMIT)

    def call(kernel, out_shape, in_specs, name, scratch=(), flops=0):
        return pl.pallas_call(
            kernel,
            out_shape=out_shape,
            in_specs=in_specs,
            out_specs=jax.tree.map(lambda _: vmem, out_shape),
            scratch_shapes=scratch,
            compiler_params=params,
            cost_estimate=pl.CostEstimate(
                flops=flops, bytes_accessed=0, transcendentals=0
            ),
            name=name,
        )

    info = jnp.stack([tile_count[0], column, row])
    span = item_factors.shape[1] // n_cols
    sent = call(
        functools.partial(prepare_kernel, n_cols, side),
        [jax.ShapeDtypeStruct((col_width, 2 * own_users + span), bf16)] * n_cols,
        [smem, anywhere, anywhere],
        "prepare",
        [
            pltpu.VMEM(user_factors.shape, f32),
            pltpu.VMEM((n_cols, col_width, own_users), f32),
            pltpu.SemaphoreType.DMA((n_cols + 1,)),
        ],
        10**9,
    )(
        info,
        pltpu.with_memory_space_constraint(user_factors, pltpu.HBM),
        pltpu.with_memory_space_constraint(item_factors, pltpu.HBM),
    )
    shared = swap(sent)

    order = jnp.arange(tile_total, dtype=jnp.int32)
    live = (order < tile_count[0]).astype(jnp.int32)
    tile_item = after(tile_item, sent[0])
    holder = tile_item // item_blocks
    local_block = tile_item % item_blocks
    earlier = (
        (holder[None, :] == holder[:, None])
        & (order[None, :] < order[:, None])
        & (live[None, :] > 0)
    )
    rank = jnp.sum(earlier.astype(jnp.int32), axis=1)
    slot_ids = jnp.minimum(holder * capacity + rank, row_devs * capacity - 1)
    slot_range = jnp.arange(row_devs * capacity, dtype=jnp.int32)
    hits = ((slot_ids[None, :] == slot_range[:, None]) & (live[None, :] > 0)).astype(jnp.int32)
    requests = (jnp.sum(hits * (local_block + 1)[None, :], axis=1) - 1).reshape(row_devs, capacity)
    wanted = lax.all_to_all(requests, "rows", split_axis=0, concat_axis=0, tiled=True)
    block = holder
    if direct:
        step = holder ^ row
        block = step
        for j, spot in ((1, 1), (3, 2), (2, 3), (5, 4), (6, 5), (7, 6), (4, 7)):
            block = jnp.where(step == j, spot, block)
    places = block * capacity + jnp.minimum(rank, capacity - 1)
    places = jnp.where(live > 0, places, places[0])
    tile_users = jnp.where(live > 0, tile_user, tile_user[0])

    picked = call(
        functools.partial(pick_kernel, direct),
        [jax.ShapeDtypeStruct((capacity, col_width, side), bf16)] * row_devs
        if direct
        else [jax.ShapeDtypeStruct((row_devs * capacity, col_width, side), bf16)],
        [smem, smem, vmem],
        "pick",
        flops=10**9,
    )(after(info, *shared), wanted, item_factors)

    def join(*arrays):
        return jnp.concatenate(arrays, axis=0)

    def gather(*arrays):
        rows = sum(array.shape[0] for array in arrays)
        return call(
            join_kernel,
            [jax.ShapeDtypeStruct((rows, *arrays[0].shape[1:]), bf16)],
            [anywhere] * len(arrays),
            "join",
            [pltpu.SemaphoreType.DMA((len(arrays),))],
            2 * 10**10,
        )(*arrays)[0]

    def add(gram, arrived):
        return call(add_kernel, [square, packed], [vmem] * 2, "add")(gram, arrived)

    got = {0: picked[0]}
    if direct:
        for j in (1, 3, 5, 6, 2, 7, 4):
            message = picked[j] if j not in (4, 7) else after(picked[j], got[5], got[6])
            got[j] = flip(message, "rows", j)

    strengths = jax.ShapeDtypeStruct((tile_total, share, side), bf16)
    (mask,) = call(
        mask_kernel,
        [strengths],
        [smem, anywhere],
        "mask",
        [pltpu.SemaphoreType.DMA],
        10**9,
    )(
        after(info, got[1] if direct else picked[0]),
        pltpu.with_memory_space_constraint(tile_mask, pltpu.HBM),
    )
    square = jax.ShapeDtypeStruct((width, width), f32)
    extra = width // col_width
    packed = jax.ShapeDtypeStruct((extra, col_width, 2 * width), bf16)
    gram, carried, start = call(
        functools.partial(gram_kernel, own_users),
        [square, packed, jax.ShapeDtypeStruct((width, own_users), f32)],
        [smem] + [anywhere] * n_cols,
        "gram",
        [
            pltpu.VMEM((width, 2 * own_users), bf16),
            pltpu.VMEM((width, span), bf16),
            pltpu.SemaphoreType.DMA((2 * n_cols,)),
        ],
        10**9,
    )(after(info, got[1] if direct else picked[0]), *shared)
    if direct:
        slots = (3 * capacity, 3 * capacity, 2 * capacity)
        own = gather(got[0], got[1], got[3])
        early = join(own, flip(own, "cols", 2))
        pieces = [early, flip(early, "cols", 1)]

        own = after(gather(got[2], got[5], got[6], carried), early)
        arrived = flip(own, "cols", 2)
        gram, carried = add(gram, arrived)
        own = join(own[: 3 * capacity], arrived[: 3 * capacity], carried)
        arrived = flip(own, "cols", 1)
        gram, carried = add(gram, arrived)
        pieces += [own, arrived]

        own = gather(got[7], got[4])
        arrived = flip(own, "cols", 2)
        for bit in (1, 2, 4):
            gram, carried = add(gram, flip(carried, "rows", bit))
            if bit == 1:
                own = after(own, carried, mask)
        own = join(own, arrived)
        pieces += [own, flip(own, "cols", 1)]
    else:
        slots = (row_devs * capacity,)
        gram = add_all(gram)
        own = lax.all_to_all(picked[0], "rows", split_axis=0, concat_axis=0, tiled=True)
        own = join(own, flip(own, "cols", 2))
        pieces = [own, flip(own, "cols", 1)]

    vector = jax.ShapeDtypeStruct((own_users, width), f32)
    held = jax.ShapeDtypeStruct((row_devs * capacity, width, side), bf16)
    work = [
        pltpu.VMEM((user_blocks, 2 * share, width), bf16),
        pltpu.VMEM((user_blocks, share, width), f32),
        pltpu.VMEM((2, UNROLL, 2 * share, side), bf16),
    ]
    lists = (places, tile_users, info)
    part, y = call(
        functools.partial(start_kernel, n_cols, slots),
        [vector, held],
        [smem] * 3 + [vmem] * 2 + [anywhere] * len(pieces),
        "start",
        work + [pltpu.SemaphoreType.DMA((n_cols * len(slots),))],
        8 * 10**9,
    )(*lists, start, mask, *pieces)
    pair = jax.ShapeDtypeStruct((n_cols, 2 * col_width, own_users), f32)
    pair_sent, field, first = call(
        first_kernel,
        [pair, vector, vector],
        [smem] * 3 + [vmem] * 5,
        "first",
        work,
        8 * 10**9,
    )(*lists, start, part, gram, y, mask)
    second_sent, dots = call(
        second_kernel,
        [
            jax.ShapeDtypeStruct((n_cols, col_width, own_users), f32),
            jax.ShapeDtypeStruct((devices, 128), f32),
        ],
        [smem] * 3 + [vmem] * 5,
        "second",
        work,
        8 * 10**9,
    )(*lists, field, first, gram, y, mask)

    turned = swap(pair_sent)
    dots = after(dots, *turned)
    turned += swap(second_sent)
    dots = lax.all_to_all(dots, ("rows", "cols"), split_axis=0, concat_axis=0, tiled=True)
    result = jax.ShapeDtypeStruct((col_width, users), f32)
    return tuple(
        call(
            functools.partial(finish_kernel, share),
            [result, result],
            [smem] + [vmem] * (2 + 2 * n_cols),
            "finish",
            [pltpu.VMEM((n_cols, col_width, own_users), f32)] * 3,
            10**9,
        )(info, dots, user_factors, *turned)
    )


def solution(mesh):
    return jax.shard_map(
        on_device,
        mesh=mesh,
        in_specs=(
            P("cols", "rows"),
            P("cols", "rows"),
            P("rows"),
            P("rows"),
            P("rows"),
            P("rows", None, None),
        ),
        out_specs=(P("cols", "rows"), P("cols", "rows")),
        check_vma=False,
    )
```

```python
import functools

import jax
import jax.numpy as jnp
from jax import lax
from jax.experimental import pallas as pl
from jax.experimental.pallas import tpu as pltpu
from jax.sharding import PartitionSpec as P

ridge = 0.5
confidence = 40.0
UNROLL = 8
LIMIT = 24 * 1024 * 1024
f32 = jnp.float32
bf16 = jnp.bfloat16


def matmul(left, right):
    return jnp.dot(left, right, preferred_element_type=f32)


def split(value):
    high = value.astype(bf16)
    low = (value - high.astype(f32)).astype(bf16)
    return high, low


def prepare_kernel(n_cols, side, info_ref, x_hbm, items_hbm, *refs):
    sent, (x_ref, x_pieces, sems) = refs[:n_cols], refs[n_cols:]
    column = info_ref[1]
    share = side // n_cols
    blocks = x_ref.shape[1] // side
    own_users = blocks * share
    span = sent[0].shape[1] - 2 * own_users
    copies = [
        pltpu.make_async_copy(
            items_hbm.at[:, pl.ds(pl.multiple_of((column ^ m) * span, span), span)],
            sent[m].at[:, pl.ds(2 * own_users, span)],
            sems.at[m],
        )
        for m in range(n_cols)
    ]
    fetch = pltpu.make_async_copy(x_hbm, x_ref, sems.at[n_cols])
    fetch.start()
    for copy in copies:
        copy.start()
    fetch.wait()
    for m in range(n_cols):
        x_pieces[m] = jnp.concatenate(
            [x_ref[:, b * side + m * share : b * side + (m + 1) * share] for b in range(blocks)],
            axis=1,
        )
    for m in range(n_cols):
        high, low = split(x_pieces[column ^ m])
        sent[m][:, :own_users] = high
        sent[m][:, own_users : 2 * own_users] = low
    for copy in copies:
        copy.wait()


def mask_kernel(info_ref, mask_hbm, mask, sem):
    tiles, share, side = mask.shape
    copy = pltpu.make_async_copy(
        mask_hbm.at[:, pl.ds(pl.multiple_of(info_ref[1] * share, share), share), :], mask, sem
    )
    copy.start()
    copy.wait()

    def clear(t, carry):
        mask[t] = jnp.zeros((share, side), bf16)
        return carry

    lax.fori_loop(info_ref[0], tiles, clear, 0)


def pick_kernel(direct, info_ref, wanted_ref, items_ref, *out_refs):
    capacity = wanted_ref.shape[1]
    side = out_refs[0].shape[2]
    for o, out_ref in enumerate(out_refs):
        for i in range(out_ref.shape[0] // capacity):
            dest = info_ref[2] ^ o if direct else i
            for r in range(capacity):
                block = jnp.maximum(wanted_ref[dest, r], 0)
                start = pl.multiple_of(block * side, side)
                out_ref[i * capacity + r] = items_ref[:, pl.ds(start, side)]


def pack(ref, gram):
    high, low = split(gram)
    both = jnp.concatenate([high, low], axis=1)
    for k in range(ref.shape[0]):
        ref[k] = both[k * ref.shape[1] : (k + 1) * ref.shape[1]]


def unpack(blocks):
    both = jnp.concatenate([blocks[k] for k in range(blocks.shape[0])], axis=0).astype(f32)
    width = both.shape[1] // 2
    return both[:, :width] + both[:, width:]


def gram_kernel(own_users, info_ref, *refs):
    column = info_ref[1]
    pieces = refs[:-6]
    out_ref, pack_ref, start_ref, starts, items, sems = refs[-6:]
    width = pieces[0].shape[0]
    span = items.shape[1]
    copies = []
    for m, piece in enumerate(pieces):
        place = pl.ds(pl.multiple_of((column ^ m) * width, width), width)
        for source, target in (
            (piece.at[:, pl.ds(0, 2 * own_users)], starts.at[place, :]),
            (piece.at[:, pl.ds(2 * own_users, span)], items.at[place, :]),
        ):
            copies.append(pltpu.make_async_copy(source, target, sems.at[len(copies)]))
            copies[-1].start()
    for copy in copies:
        copy.wait()
    both = starts[...].astype(f32)
    start_ref[...] = both[:, :own_users] + both[:, own_users:]
    gram = lax.dot_general(
        items[...], items[...], (((1,), (1,)), ((), ())), preferred_element_type=f32
    )
    out_ref[...] = gram
    pack(pack_ref, gram)


def add_kernel(gram_ref, arrived_ref, out_ref, pack_ref):
    extra = pack_ref.shape[0]
    total = gram_ref[...] + unpack(arrived_ref[arrived_ref.shape[0] - extra :])
    out_ref[...] = total
    pack(pack_ref, total)


def join_kernel(*refs):
    sources, out_ref, sems = refs[:-2], refs[-2], refs[-1]
    copies = []
    base = 0
    for source in sources:
        rows = source.shape[0]
        copies.append(
            pltpu.make_async_copy(source, out_ref.at[pl.ds(base, rows)], sems.at[len(copies)])
        )
        copies[-1].start()
        base += rows
    for copy in copies:
        copy.wait()


def load(p_hl, vector):
    blocks, both, width = p_hl.shape
    share = both // 2
    high, low = split(vector)
    p_hl[:, :share] = high.reshape(blocks, share, width)
    p_hl[:, share:] = low.reshape(blocks, share, width)


def dense(p_hl, gram_ref, vector):
    blocks, both, width = p_hl.shape
    gram_high, gram_low = split(gram_ref[...])
    product = matmul(
        p_hl[...].reshape(blocks * both, width),
        jnp.concatenate([gram_high, gram_low], axis=1),
    ).reshape(blocks, 2, both // 2, 2 * width)
    product = product[:, 0] + product[:, 1]
    product = product[:, :, :width] + product[:, :, width:]
    return product.reshape(vector.shape) + ridge * vector


def sparse(starting, slot_ref, user_ref, y, mask, p_hl, acc, held):
    tiles, share, side = mask.shape
    groups = tiles // UNROLL
    acc[...] = jnp.zeros_like(acc)

    def score(group):
        for j in range(UNROLL):
            t = group * UNROLL + j
            scores = matmul(p_hl[user_ref[t]], y[slot_ref[t]])
            scores = scores[:share] + scores[share:]
            if starting:
                scores = (1.0 + confidence) - confidence * scores
            high, low = split(mask[t].astype(f32) * scores)
            held[group % 2, j, :share] = high
            held[group % 2, j, share:] = low

    def collect(group):
        terms = []
        for j in range(UNROLL):
            t = group * UNROLL + j
            term = lax.dot_general(
                held[group % 2, j],
                y[slot_ref[t]],
                (((1,), (1,)), ((), ())),
                preferred_element_type=f32,
            )
            terms.append(term[:share] + term[share:])
        return terms

    def add(group, terms):
        for j, term in enumerate(terms):
            acc[user_ref[group * UNROLL + j]] += term

    score(0)

    def step(group, carry):
        terms = collect(group - 1)
        score(group)
        add(group - 1, terms)
        return carry

    lax.fori_loop(1, groups, step, 0)
    add(groups - 1, collect(groups - 1))


def put(column, ref, vector, part=0):
    n_cols, rows, _ = ref.shape
    turned = vector.T
    width = turned.shape[0] // n_cols
    for m in range(n_cols):
        ref[column ^ m, part * width : (part + 1) * width] = turned[m * width : (m + 1) * width]


def start_kernel(n_cols, slots, slot_ref, user_ref, info_ref, x_ref, mask, *refs):
    pieces = refs[: 2 * len(slots)]
    part_ref, y, p_hl, acc, held, sems = refs[2 * len(slots) :]
    piece_width = y.shape[1] // n_cols
    column = info_ref[1]
    copies = []
    base = 0
    for k, count in enumerate(slots):
        for m in range(n_cols):
            place = pl.multiple_of((column ^ m) * piece_width, piece_width)
            source = pieces[2 * k + m % 2].at[pl.ds(m // 2 * count, count)]
            copies.append(
                pltpu.make_async_copy(
                    source,
                    y.at[pl.ds(base, count), pl.ds(place, piece_width), :],
                    sems.at[len(copies)],
                )
            )
        base += count
    for copy in copies:
        copy.start()
    load(p_hl, x_ref[...].T)
    for copy in copies:
        copy.wait()
    sparse(True, slot_ref, user_ref, y, mask, p_hl, acc, held)
    part_ref[...] = acc[...].reshape(part_ref.shape)


def first_kernel(
    slot_ref, user_ref, info_ref, x_ref, part_ref, gram_ref, y, mask,
    sent_ref, field_ref, first_ref, p_hl, acc, held,
):
    start = x_ref[...].T
    load(p_hl, start)
    field = part_ref[...] - dense(p_hl, gram_ref, start)
    field_ref[...] = field
    put(info_ref[1], sent_ref, field)
    load(p_hl, field)
    sparse(False, slot_ref, user_ref, y, mask, p_hl, acc, held)
    first = confidence * acc[...].reshape(field.shape) + dense(p_hl, gram_ref, field)
    first_ref[...] = first
    put(info_ref[1], sent_ref, first, 1)


def second_kernel(
    slot_ref, user_ref, info_ref, field_ref, first_ref, gram_ref, y, mask, sent_ref, dots_ref, p_hl, acc, held
):
    field = field_ref[...]
    first = first_ref[...]
    load(p_hl, first)
    sparse(False, slot_ref, user_ref, y, mask, p_hl, acc, held)
    second = confidence * acc[...].reshape(field.shape) + dense(p_hl, gram_ref, first)
    put(info_ref[1], sent_ref, second)

    def total(left, right):
        return jnp.sum(left * right)

    aa, ab, bb = total(field, field), total(field, first), total(first, first)
    guess = jnp.where(bb > 0.0, ab / jnp.where(bb > 0.0, bb, 1.0), 0.0)
    near = field - guess * first
    near_image = first - guess * second
    values = (
        aa,
        ab,
        bb,
        guess,
        total(near, near),
        total(near, first),
        total(near, near_image),
        total(near, second) + total(first, near_image),
        total(first, second),
    )
    lane = lax.broadcasted_iota(jnp.int32, dots_ref.shape, 1)
    dots = jnp.zeros(dots_ref.shape, f32)
    for j, value in enumerate(values):
        dots = jnp.where(lane == j, value, dots)
    dots_ref[...] = dots


def finish_kernel(share, info_ref, dots_ref, x_ref, *refs):
    n_cols = (len(refs) - 5) // 2
    x_out, r_out, field_ref, first_ref, second_ref = refs[2 * n_cols :]
    width = field_ref.shape[1]
    for m in range(n_cols):
        place = info_ref[1] ^ m
        field_ref[place] = refs[m][:width]
        first_ref[place] = refs[m][width:]
        second_ref[place] = refs[n_cols + m][...]
    dots = dots_ref[...]

    def column(j):
        return dots[:, j : j + 1]

    def total(value):
        return jnp.sum(value, axis=0, keepdims=True)

    rr0 = total(column(0))
    ab = total(column(1))
    alpha0 = rr0 / ab
    delta = alpha0 - column(3)
    rr1 = total(column(4) - 2.0 * delta * column(5) + delta * delta * column(2))
    curved = total(column(6) - delta * column(7) + delta * delta * column(8))
    crossed = total(column(5) - delta * column(2))
    beta = rr1 / rr0
    alpha1 = rr1 / (curved + 2.0 * beta * crossed + beta * beta * ab)
    along = alpha0 + alpha1 * (1.0 + beta)
    across = alpha1 * alpha0
    blocks = x_ref.shape[1] // (share * n_cols)
    for b in range(blocks):

        def gather(ref):
            return jnp.concatenate(
                [ref[m, :, b * share : (b + 1) * share] for m in range(n_cols)], axis=1
            )

        field, first, second = gather(field_ref), gather(first_ref), gather(second_ref)
        here = slice(b * share * n_cols, (b + 1) * share * n_cols)
        x_out[:, here] = x_ref[:, here] + along * field - across * first
        r_out[:, here] = field - along * first + across * second


def flip(value, axis, bit):
    size = lax.axis_size(axis)
    return lax.ppermute(value, axis, [(i, i ^ bit) for i in range(size)])


def swap(sent):
    return [sent[0]] + [flip(sent[m], "cols", m) for m in range(1, len(sent))]


def after(value, *others):
    return lax.optimization_barrier((value, *others))[0]


def add_all(value):
    for axis in ("cols", "rows"):
        bit = 1
        while bit < lax.axis_size(axis):
            value = value + flip(value, axis, bit)
            bit *= 2
    return value


def on_device(user_factors, item_factors, tile_user, tile_item, tile_count, tile_mask):
    side = tile_mask.shape[1]
    col_width = user_factors.shape[0]
    column = lax.axis_index("cols").astype(jnp.int32)
    row = lax.axis_index("rows").astype(jnp.int32)
    row_devs = lax.axis_size("rows")
    n_cols = lax.axis_size("cols")
    devices = row_devs * n_cols
    width = col_width * n_cols
    tile_total = tile_user.shape[0]
    users = user_factors.shape[1]
    user_blocks = users // side
    item_blocks = item_factors.shape[1] // side
    share = side // n_cols
    own_users = users // n_cols
    capacity = max(2, (tile_total + row_devs - 1) // row_devs)
    direct = row_devs == 8 and 2 * width == side
    vmem = pl.BlockSpec(memory_space=pltpu.VMEM)
    smem = pl.BlockSpec(memory_space=pltpu.SMEM)
    anywhere = pl.BlockSpec(memory_space=pl.ANY)
    params = pltpu.CompilerParams(vmem_limit_bytes=LIMIT)

    def call(kernel, out_shape, in_specs, name, scratch=(), flops=0):
        return pl.pallas_call(
            kernel,
            out_shape=out_shape,
            in_specs=in_specs,
            out_specs=jax.tree.map(lambda _: vmem, out_shape),
            scratch_shapes=scratch,
            compiler_params=params,
            cost_estimate=pl.CostEstimate(
                flops=flops, bytes_accessed=0, transcendentals=0
            ),
            name=name,
        )

    info = jnp.stack([tile_count[0], column, row])
    span = item_factors.shape[1] // n_cols
    sent = call(
        functools.partial(prepare_kernel, n_cols, side),
        [jax.ShapeDtypeStruct((col_width, 2 * own_users + span), bf16)] * n_cols,
        [smem, anywhere, anywhere],
        "prepare",
        [
            pltpu.VMEM(user_factors.shape, f32),
            pltpu.VMEM((n_cols, col_width, own_users), f32),
            pltpu.SemaphoreType.DMA((n_cols + 1,)),
        ],
        10**9,
    )(
        info,
        pltpu.with_memory_space_constraint(user_factors, pltpu.HBM),
        pltpu.with_memory_space_constraint(item_factors, pltpu.HBM),
    )
    shared = swap(sent)

    order = jnp.arange(tile_total, dtype=jnp.int32)
    live = (order < tile_count[0]).astype(jnp.int32)
    tile_item = after(tile_item, sent[0])
    holder = tile_item // item_blocks
    local_block = tile_item % item_blocks
    earlier = (
        (holder[None, :] == holder[:, None])
        & (order[None, :] < order[:, None])
        & (live[None, :] > 0)
    )
    rank = jnp.sum(earlier.astype(jnp.int32), axis=1)
    slot_ids = jnp.minimum(holder * capacity + rank, row_devs * capacity - 1)
    slot_range = jnp.arange(row_devs * capacity, dtype=jnp.int32)
    hits = ((slot_ids[None, :] == slot_range[:, None]) & (live[None, :] > 0)).astype(jnp.int32)
    requests = (jnp.sum(hits * (local_block + 1)[None, :], axis=1) - 1).reshape(row_devs, capacity)
    wanted = lax.all_to_all(requests, "rows", split_axis=0, concat_axis=0, tiled=True)
    block = holder
    if direct:
        step = holder ^ row
        block = step
        for j, spot in ((1, 1), (3, 2), (2, 3), (5, 4), (6, 5), (7, 6), (4, 7)):
            block = jnp.where(step == j, spot, block)
    places = block * capacity + jnp.minimum(rank, capacity - 1)
    places = jnp.where(live > 0, places, places[0])
    tile_users = jnp.where(live > 0, tile_user, tile_user[0])

    picked = call(
        functools.partial(pick_kernel, direct),
        [jax.ShapeDtypeStruct((capacity, col_width, side), bf16)] * row_devs
        if direct
        else [jax.ShapeDtypeStruct((row_devs * capacity, col_width, side), bf16)],
        [smem, smem, vmem],
        "pick",
        flops=10**9,
    )(after(info, *shared), wanted, item_factors)

    def add(gram, arrived):
        return call(add_kernel, [square, packed], [vmem] * 2, "add")(gram, arrived)

    def join(*arrays):
        return jnp.concatenate(arrays, axis=0)

    def gather(*arrays):
        rows = sum(array.shape[0] for array in arrays)
        return call(
            join_kernel,
            [jax.ShapeDtypeStruct((rows, *arrays[0].shape[1:]), bf16)],
            [anywhere] * len(arrays),
            "join",
            [pltpu.SemaphoreType.DMA((len(arrays),))],
            2 * 10**10,
        )(*arrays)[0]

    got = {0: picked[0]}
    if direct:
        for j in (1, 3, 5, 6, 2, 7, 4):
            message = picked[j] if j not in (4, 7) else after(picked[j], got[5], got[6])
            got[j] = flip(message, "rows", j)

    strengths = jax.ShapeDtypeStruct((tile_total, share, side), bf16)
    (mask,) = call(
        mask_kernel,
        [strengths],
        [smem, anywhere],
        "mask",
        [pltpu.SemaphoreType.DMA],
        10**9,
    )(
        after(info, got[1] if direct else picked[0]),
        pltpu.with_memory_space_constraint(tile_mask, pltpu.HBM),
    )
    if direct:
        own = gather(got[0], got[1], got[3])
    square = jax.ShapeDtypeStruct((width, width), f32)
    extra = width // col_width
    packed = jax.ShapeDtypeStruct((extra, col_width, 2 * width), bf16)
    gram, carried, start = call(
        functools.partial(gram_kernel, own_users),
        [square, packed, jax.ShapeDtypeStruct((width, own_users), f32)],
        [smem] + [anywhere] * n_cols,
        "gram",
        [
            pltpu.VMEM((width, 2 * own_users), bf16),
            pltpu.VMEM((width, span), bf16),
            pltpu.SemaphoreType.DMA((2 * n_cols,)),
        ],
        10**9,
    )(after(info, own if direct else picked[0]), *shared)
    if direct:
        slots = (3 * capacity, 3 * capacity, 2 * capacity)
        early = join(own, flip(own, "cols", 2))
        pieces = [early, flip(early, "cols", 1)]

        middle = after(gather(after(got[2], mask), got[5], got[6]), early)
        own = middle
        own = join(own, flip(own, "cols", 2))
        pieces += [own, flip(own, "cols", 1)]

        for bit in (1, 2, 4):
            gram, carried = add(gram, flip(carried, "rows", bit))
            if bit == 1:
                carried = after(carried, got[5], got[6])
            if bit == 2:
                carried = after(carried, middle)
        own = gather(got[7], got[4], carried)
        arrived = flip(own, "cols", 2)
        gram, carried = add(gram, arrived)
        own = join(own[: 2 * capacity], arrived[: 2 * capacity], carried)
        arrived = flip(own, "cols", 1)
        gram, carried = add(gram, arrived)
        pieces += [own, arrived]
    else:
        slots = (row_devs * capacity,)
        gram = add_all(gram)
        own = lax.all_to_all(picked[0], "rows", split_axis=0, concat_axis=0, tiled=True)
        own = join(own, flip(own, "cols", 2))
        pieces = [own, flip(own, "cols", 1)]

    vector = jax.ShapeDtypeStruct((own_users, width), f32)
    held = jax.ShapeDtypeStruct((row_devs * capacity, width, side), bf16)
    work = [
        pltpu.VMEM((user_blocks, 2 * share, width), bf16),
        pltpu.VMEM((user_blocks, share, width), f32),
        pltpu.VMEM((2, UNROLL, 2 * share, side), bf16),
    ]
    lists = (places, tile_users, info)
    part, y = call(
        functools.partial(start_kernel, n_cols, slots),
        [vector, held],
        [smem] * 3 + [vmem] * 2 + [anywhere] * len(pieces),
        "start",
        work + [pltpu.SemaphoreType.DMA((n_cols * len(slots),))],
        8 * 10**9,
    )(*lists, start, mask, *pieces)
    pair = jax.ShapeDtypeStruct((n_cols, 2 * col_width, own_users), f32)
    pair_sent, field, first = call(
        first_kernel,
        [pair, vector, vector],
        [smem] * 3 + [vmem] * 5,
        "first",
        work,
        8 * 10**9,
    )(*lists, start, part, gram, y, mask)
    second_sent, dots = call(
        second_kernel,
        [
            jax.ShapeDtypeStruct((n_cols, col_width, own_users), f32),
            jax.ShapeDtypeStruct((devices, 128), f32),
        ],
        [smem] * 3 + [vmem] * 5,
        "second",
        work,
        8 * 10**9,
    )(*lists, field, first, gram, y, mask)

    turned = swap(pair_sent)
    dots = after(dots, *turned)
    turned += swap(second_sent)
    dots = lax.all_to_all(dots, ("rows", "cols"), split_axis=0, concat_axis=0, tiled=True)
    result = jax.ShapeDtypeStruct((col_width, users), f32)
    return tuple(
        call(
            functools.partial(finish_kernel, share),
            [result, result],
            [smem] + [vmem] * (2 + 2 * n_cols),
            "finish",
            [pltpu.VMEM((n_cols, col_width, own_users), f32)] * 3,
            10**9,
        )(info, dots, user_factors, *turned)
    )


def solution(mesh):
    return jax.shard_map(
        on_device,
        mesh=mesh,
        in_specs=(
            P("cols", "rows"),
            P("cols", "rows"),
            P("rows"),
            P("rows"),
            P("rows"),
            P("rows", None, None),
        ),
        out_specs=(P("cols", "rows"), P("cols", "rows")),
        check_vma=False,
    )
```

```python
import functools

import jax
import jax.numpy as jnp
from jax import lax
from jax.experimental import pallas as pl
from jax.experimental.pallas import tpu as pltpu
from jax.sharding import PartitionSpec as P

ridge = 0.5
confidence = 40.0
UNROLL = 8
LIMIT = 24 * 1024 * 1024
f32 = jnp.float32
bf16 = jnp.bfloat16


def matmul(left, right):
    return jnp.dot(left, right, preferred_element_type=f32)


def split(value):
    high = value.astype(bf16)
    low = (value - high.astype(f32)).astype(bf16)
    return high, low


def prepare_kernel(n_cols, side, info_ref, x_hbm, items_hbm, *refs):
    sent, (x_ref, x_pieces, sems) = refs[:n_cols], refs[n_cols:]
    column = info_ref[1]
    share = side // n_cols
    blocks = x_ref.shape[1] // side
    own_users = blocks * share
    span = sent[0].shape[1] - 2 * own_users
    copies = [
        pltpu.make_async_copy(
            items_hbm.at[:, pl.ds(pl.multiple_of((column ^ m) * span, span), span)],
            sent[m].at[:, pl.ds(2 * own_users, span)],
            sems.at[m],
        )
        for m in range(n_cols)
    ]
    fetch = pltpu.make_async_copy(x_hbm, x_ref, sems.at[n_cols])
    fetch.start()
    for copy in copies:
        copy.start()
    fetch.wait()
    for m in range(n_cols):
        x_pieces[m] = jnp.concatenate(
            [x_ref[:, b * side + m * share : b * side + (m + 1) * share] for b in range(blocks)],
            axis=1,
        )
    for m in range(n_cols):
        high, low = split(x_pieces[column ^ m])
        sent[m][:, :own_users] = high
        sent[m][:, own_users : 2 * own_users] = low
    for copy in copies:
        copy.wait()


def mask_kernel(info_ref, mask_hbm, mask, sem):
    tiles, share, side = mask.shape
    copy = pltpu.make_async_copy(
        mask_hbm.at[:, pl.ds(pl.multiple_of(info_ref[1] * share, share), share), :], mask, sem
    )
    copy.start()
    copy.wait()

    def clear(t, carry):
        mask[t] = jnp.zeros((share, side), bf16)
        return carry

    lax.fori_loop(info_ref[0], tiles, clear, 0)


def pick_kernel(direct, info_ref, wanted_ref, items_ref, *out_refs):
    capacity = wanted_ref.shape[1]
    side = out_refs[0].shape[2]
    for o, out_ref in enumerate(out_refs):
        for i in range(out_ref.shape[0] // capacity):
            dest = info_ref[2] ^ o if direct else i
            for r in range(capacity):
                block = jnp.maximum(wanted_ref[dest, r], 0)
                start = pl.multiple_of(block * side, side)
                out_ref[i * capacity + r] = items_ref[:, pl.ds(start, side)]


def pack(ref, gram):
    high, low = split(gram)
    both = jnp.concatenate([high, low], axis=1)
    for k in range(ref.shape[0]):
        ref[k] = both[k * ref.shape[1] : (k + 1) * ref.shape[1]]


def unpack(blocks):
    both = jnp.concatenate([blocks[k] for k in range(blocks.shape[0])], axis=0).astype(f32)
    width = both.shape[1] // 2
    return both[:, :width] + both[:, width:]


def gram_kernel(own_users, info_ref, *refs):
    column = info_ref[1]
    pieces = refs[:-6]
    out_ref, pack_ref, start_ref, starts, items, sems = refs[-6:]
    width = pieces[0].shape[0]
    span = items.shape[1]
    copies = []
    for m, piece in enumerate(pieces):
        place = pl.ds(pl.multiple_of((column ^ m) * width, width), width)
        for source, target in (
            (piece.at[:, pl.ds(0, 2 * own_users)], starts.at[place, :]),
            (piece.at[:, pl.ds(2 * own_users, span)], items.at[place, :]),
        ):
            copies.append(pltpu.make_async_copy(source, target, sems.at[len(copies)]))
            copies[-1].start()
    for copy in copies:
        copy.wait()
    both = starts[...].astype(f32)
    start_ref[...] = both[:, :own_users] + both[:, own_users:]
    gram = lax.dot_general(
        items[...], items[...], (((1,), (1,)), ((), ())), preferred_element_type=f32
    )
    out_ref[...] = gram
    pack(pack_ref, gram)


def add_kernel(gram_ref, arrived_ref, out_ref, pack_ref):
    extra = pack_ref.shape[0]
    total = gram_ref[...] + unpack(arrived_ref[arrived_ref.shape[0] - extra :])
    out_ref[...] = total
    pack(pack_ref, total)


def join_kernel(*refs):
    sources, out_ref, sems = refs[:-2], refs[-2], refs[-1]
    copies = []
    base = 0
    for source in sources:
        rows = source.shape[0]
        copies.append(
            pltpu.make_async_copy(source, out_ref.at[pl.ds(base, rows)], sems.at[len(copies)])
        )
        copies[-1].start()
        base += rows
    for copy in copies:
        copy.wait()


def load(p_hl, vector):
    blocks, share, both = p_hl.shape
    width = both // 2
    high, low = split(vector)
    p_hl[:, :, :width] = high.reshape(blocks, share, width)
    p_hl[:, :, width:] = low.reshape(blocks, share, width)


def dense(p_hl, gram_ref, vector):
    blocks, share, both = p_hl.shape
    width = both // 2
    high, low = split(gram_ref[...])
    table = jnp.concatenate(
        [
            jnp.concatenate([high, low], axis=1),
            jnp.concatenate([high, jnp.zeros_like(low)], axis=1),
        ],
        axis=0,
    )
    product = matmul(p_hl[...].reshape(blocks * share, both), table)
    return product[:, :width] + product[:, width:] + ridge * vector


def sparse(starting, slot_ref, user_ref, y, mask, p_hl, acc, held):
    tiles, share, side = mask.shape
    groups = tiles // UNROLL
    acc[...] = jnp.zeros_like(acc)

    def score(group):
        for j in range(UNROLL):
            t = group * UNROLL + j
            tile = y[slot_ref[t]]
            scores = matmul(p_hl[user_ref[t]], jnp.concatenate([tile, tile], axis=0))
            if starting:
                scores = (1.0 + confidence) - confidence * scores
            high, low = split(mask[t].astype(f32) * scores)
            held[group % 2, j, :share] = high
            held[group % 2, j, share:] = low

    def collect(group):
        terms = []
        for j in range(UNROLL):
            t = group * UNROLL + j
            term = lax.dot_general(
                held[group % 2, j],
                y[slot_ref[t]],
                (((1,), (1,)), ((), ())),
                preferred_element_type=f32,
            )
            terms.append(term[:share] + term[share:])
        return terms

    def add(group, terms):
        for j, term in enumerate(terms):
            acc[user_ref[group * UNROLL + j]] += term

    score(0)

    def step(group, carry):
        terms = collect(group - 1)
        score(group)
        add(group - 1, terms)
        return carry

    lax.fori_loop(1, groups, step, 0)
    add(groups - 1, collect(groups - 1))


def put(column, ref, vector, part=0):
    n_cols, rows, _ = ref.shape
    turned = vector.T
    width = turned.shape[0] // n_cols
    for m in range(n_cols):
        ref[column ^ m, part * width : (part + 1) * width] = turned[m * width : (m + 1) * width]


def start_kernel(n_cols, slots, slot_ref, user_ref, info_ref, x_ref, mask, *refs):
    pieces = refs[: 2 * len(slots)]
    part_ref, y, p_hl, acc, held, sems = refs[2 * len(slots) :]
    piece_width = y.shape[1] // n_cols
    column = info_ref[1]
    copies = []
    base = 0
    for k, count in enumerate(slots):
        for m in range(n_cols):
            place = pl.multiple_of((column ^ m) * piece_width, piece_width)
            source = pieces[2 * k + m % 2].at[pl.ds(m // 2 * count, count)]
            copies.append(
                pltpu.make_async_copy(
                    source,
                    y.at[pl.ds(base, count), pl.ds(place, piece_width), :],
                    sems.at[len(copies)],
                )
            )
        base += count
    for copy in copies:
        copy.start()
    load(p_hl, x_ref[...].T)
    for copy in copies:
        copy.wait()
    sparse(True, slot_ref, user_ref, y, mask, p_hl, acc, held)
    part_ref[...] = acc[...].reshape(part_ref.shape)


def first_kernel(
    slot_ref, user_ref, info_ref, x_ref, part_ref, gram_ref, y, mask,
    sent_ref, field_ref, first_ref, p_hl, acc, held,
):
    start = x_ref[...].T
    load(p_hl, start)
    field = part_ref[...] - dense(p_hl, gram_ref, start)
    field_ref[...] = field
    put(info_ref[1], sent_ref, field)
    load(p_hl, field)
    sparse(False, slot_ref, user_ref, y, mask, p_hl, acc, held)
    first = confidence * acc[...].reshape(field.shape) + dense(p_hl, gram_ref, field)
    first_ref[...] = first
    put(info_ref[1], sent_ref, first, 1)


def second_kernel(
    slot_ref, user_ref, info_ref, field_ref, first_ref, gram_ref, y, mask, sent_ref, dots_ref, p_hl, acc, held
):
    field = field_ref[...]
    first = first_ref[...]
    load(p_hl, first)
    sparse(False, slot_ref, user_ref, y, mask, p_hl, acc, held)
    second = confidence * acc[...].reshape(field.shape) + dense(p_hl, gram_ref, first)
    put(info_ref[1], sent_ref, second)

    def total(left, right):
        return jnp.sum(left * right)

    aa, ab, bb = total(field, field), total(field, first), total(first, first)
    guess = jnp.where(bb > 0.0, ab / jnp.where(bb > 0.0, bb, 1.0), 0.0)
    near = field - guess * first
    near_image = first - guess * second
    values = (
        aa,
        ab,
        bb,
        guess,
        total(near, near),
        total(near, first),
        total(near, near_image),
        total(near, second) + total(first, near_image),
        total(first, second),
    )
    lane = lax.broadcasted_iota(jnp.int32, dots_ref.shape, 1)
    dots = jnp.zeros(dots_ref.shape, f32)
    for j, value in enumerate(values):
        dots = jnp.where(lane == j, value, dots)
    dots_ref[...] = dots


def finish_kernel(share, info_ref, dots_ref, x_ref, *refs):
    n_cols = (len(refs) - 5) // 2
    x_out, r_out, field_ref, first_ref, second_ref = refs[2 * n_cols :]
    width = field_ref.shape[1]
    for m in range(n_cols):
        place = info_ref[1] ^ m
        field_ref[place] = refs[m][:width]
        first_ref[place] = refs[m][width:]
        second_ref[place] = refs[n_cols + m][...]
    dots = dots_ref[...]

    def column(j):
        return dots[:, j : j + 1]

    def total(value):
        return jnp.sum(value, axis=0, keepdims=True)

    rr0 = total(column(0))
    ab = total(column(1))
    alpha0 = rr0 / ab
    delta = alpha0 - column(3)
    rr1 = total(column(4) - 2.0 * delta * column(5) + delta * delta * column(2))
    curved = total(column(6) - delta * column(7) + delta * delta * column(8))
    crossed = total(column(5) - delta * column(2))
    beta = rr1 / rr0
    alpha1 = rr1 / (curved + 2.0 * beta * crossed + beta * beta * ab)
    along = alpha0 + alpha1 * (1.0 + beta)
    across = alpha1 * alpha0
    blocks = x_ref.shape[1] // (share * n_cols)
    for b in range(blocks):

        def gather(ref):
            return jnp.concatenate(
                [ref[m, :, b * share : (b + 1) * share] for m in range(n_cols)], axis=1
            )

        field, first, second = gather(field_ref), gather(first_ref), gather(second_ref)
        here = slice(b * share * n_cols, (b + 1) * share * n_cols)
        x_out[:, here] = x_ref[:, here] + along * field - across * first
        r_out[:, here] = field - along * first + across * second


def flip(value, axis, bit):
    size = lax.axis_size(axis)
    return lax.ppermute(value, axis, [(i, i ^ bit) for i in range(size)])


def swap(sent):
    return [sent[0]] + [flip(sent[m], "cols", m) for m in range(1, len(sent))]


def after(value, *others):
    return lax.optimization_barrier((value, *others))[0]


def add_all(value):
    for axis in ("cols", "rows"):
        bit = 1
        while bit < lax.axis_size(axis):
            value = value + flip(value, axis, bit)
            bit *= 2
    return value


def on_device(user_factors, item_factors, tile_user, tile_item, tile_count, tile_mask):
    side = tile_mask.shape[1]
    col_width = user_factors.shape[0]
    column = lax.axis_index("cols").astype(jnp.int32)
    row = lax.axis_index("rows").astype(jnp.int32)
    row_devs = lax.axis_size("rows")
    n_cols = lax.axis_size("cols")
    devices = row_devs * n_cols
    width = col_width * n_cols
    tile_total = tile_user.shape[0]
    users = user_factors.shape[1]
    user_blocks = users // side
    item_blocks = item_factors.shape[1] // side
    share = side // n_cols
    own_users = users // n_cols
    capacity = max(2, (tile_total + row_devs - 1) // row_devs)
    direct = row_devs == 8 and 2 * width == side
    vmem = pl.BlockSpec(memory_space=pltpu.VMEM)
    smem = pl.BlockSpec(memory_space=pltpu.SMEM)
    anywhere = pl.BlockSpec(memory_space=pl.ANY)
    params = pltpu.CompilerParams(vmem_limit_bytes=LIMIT)

    def call(kernel, out_shape, in_specs, name, scratch=(), flops=0):
        return pl.pallas_call(
            kernel,
            out_shape=out_shape,
            in_specs=in_specs,
            out_specs=jax.tree.map(lambda _: vmem, out_shape),
            scratch_shapes=scratch,
            compiler_params=params,
            cost_estimate=pl.CostEstimate(
                flops=flops, bytes_accessed=0, transcendentals=0
            ),
            name=name,
        )

    info = jnp.stack([tile_count[0], column, row])
    span = item_factors.shape[1] // n_cols
    sent = call(
        functools.partial(prepare_kernel, n_cols, side),
        [jax.ShapeDtypeStruct((col_width, 2 * own_users + span), bf16)] * n_cols,
        [smem, anywhere, anywhere],
        "prepare",
        [
            pltpu.VMEM(user_factors.shape, f32),
            pltpu.VMEM((n_cols, col_width, own_users), f32),
            pltpu.SemaphoreType.DMA((n_cols + 1,)),
        ],
        10**9,
    )(
        info,
        pltpu.with_memory_space_constraint(user_factors, pltpu.HBM),
        pltpu.with_memory_space_constraint(item_factors, pltpu.HBM),
    )
    shared = swap(sent)

    order = jnp.arange(tile_total, dtype=jnp.int32)
    live = (order < tile_count[0]).astype(jnp.int32)
    tile_item = after(tile_item, sent[0])
    holder = tile_item // item_blocks
    local_block = tile_item % item_blocks
    earlier = (
        (holder[None, :] == holder[:, None])
        & (order[None, :] < order[:, None])
        & (live[None, :] > 0)
    )
    rank = jnp.sum(earlier.astype(jnp.int32), axis=1)
    slot_ids = jnp.minimum(holder * capacity + rank, row_devs * capacity - 1)
    slot_range = jnp.arange(row_devs * capacity, dtype=jnp.int32)
    hits = ((slot_ids[None, :] == slot_range[:, None]) & (live[None, :] > 0)).astype(jnp.int32)
    requests = (jnp.sum(hits * (local_block + 1)[None, :], axis=1) - 1).reshape(row_devs, capacity)
    wanted = lax.all_to_all(requests, "rows", split_axis=0, concat_axis=0, tiled=True)
    block = holder
    if direct:
        step = holder ^ row
        block = step
        for j, spot in ((1, 1), (3, 2), (2, 3), (5, 4), (6, 5), (7, 6), (4, 7)):
            block = jnp.where(step == j, spot, block)
    places = block * capacity + jnp.minimum(rank, capacity - 1)
    places = jnp.where(live > 0, places, places[0])
    tile_users = jnp.where(live > 0, tile_user, tile_user[0])

    picked = call(
        functools.partial(pick_kernel, direct),
        [jax.ShapeDtypeStruct((capacity, col_width, side), bf16)] * row_devs
        if direct
        else [jax.ShapeDtypeStruct((row_devs * capacity, col_width, side), bf16)],
        [smem, smem, vmem],
        "pick",
        flops=10**9,
    )(after(info, *shared), wanted, item_factors)

    def join(*arrays):
        return jnp.concatenate(arrays, axis=0)

    def gather(*arrays):
        rows = sum(array.shape[0] for array in arrays)
        return call(
            join_kernel,
            [jax.ShapeDtypeStruct((rows, *arrays[0].shape[1:]), bf16)],
            [anywhere] * len(arrays),
            "join",
            [pltpu.SemaphoreType.DMA((len(arrays),))],
            2 * 10**10,
        )(*arrays)[0]

    def add(gram, arrived):
        return call(add_kernel, [square, packed], [vmem] * 2, "add")(gram, arrived)

    got = {0: picked[0]}
    if direct:
        for j in (1, 3, 5, 6, 2, 7, 4):
            message = picked[j] if j not in (4, 7) else after(picked[j], got[5], got[6])
            got[j] = flip(message, "rows", j)

    strengths = jax.ShapeDtypeStruct((tile_total, share, side), bf16)
    (mask,) = call(
        mask_kernel,
        [strengths],
        [smem, anywhere],
        "mask",
        [pltpu.SemaphoreType.DMA],
        10**9,
    )(
        after(info, got[1] if direct else picked[0]),
        pltpu.with_memory_space_constraint(tile_mask, pltpu.HBM),
    )
    square = jax.ShapeDtypeStruct((width, width), f32)
    extra = width // col_width
    packed = jax.ShapeDtypeStruct((extra, col_width, 2 * width), bf16)
    gram, carried, start = call(
        functools.partial(gram_kernel, own_users),
        [square, packed, jax.ShapeDtypeStruct((width, own_users), f32)],
        [smem] + [anywhere] * n_cols,
        "gram",
        [
            pltpu.VMEM((width, 2 * own_users), bf16),
            pltpu.VMEM((width, span), bf16),
            pltpu.SemaphoreType.DMA((2 * n_cols,)),
        ],
        10**9,
    )(after(info, got[1] if direct else picked[0]), *shared)
    if direct:
        slots = (3 * capacity, 3 * capacity, 2 * capacity)
        own = gather(got[0], got[1], got[3])
        early = join(own, flip(own, "cols", 2))
        pieces = [early, flip(early, "cols", 1)]

        own = after(gather(got[2], got[5], got[6], carried), early)
        arrived = flip(own, "cols", 2)
        gram, carried = add(gram, arrived)
        own = join(own[: 3 * capacity], arrived[: 3 * capacity], carried)
        arrived = flip(after(own, mask), "cols", 1)
        gram, carried = add(gram, arrived)
        pieces += [own, arrived]

        own = gather(got[7], got[4])
        own = join(own, flip(own, "cols", 2))
        gram, carried = add(gram, flip(carried, "rows", 1))
        pieces += [own, flip(after(own, carried), "cols", 1)]
        gram, carried = add(gram, flip(carried, "rows", 2))
        arrived = flip(carried, "rows", 4)
    else:
        slots = (row_devs * capacity,)
        gram = add_all(gram)
        own = lax.all_to_all(picked[0], "rows", split_axis=0, concat_axis=0, tiled=True)
        own = join(own, flip(own, "cols", 2))
        pieces = [own, flip(own, "cols", 1)]

    vector = jax.ShapeDtypeStruct((own_users, width), f32)
    held = jax.ShapeDtypeStruct((row_devs * capacity, width, side), bf16)
    work = [
        pltpu.VMEM((user_blocks, share, 2 * width), bf16),
        pltpu.VMEM((user_blocks, share, width), f32),
        pltpu.VMEM((2, UNROLL, 2 * share, side), bf16),
    ]
    lists = (places, tile_users, info)
    part, y = call(
        functools.partial(start_kernel, n_cols, slots),
        [vector, held],
        [smem] * 3 + [vmem] * 2 + [anywhere] * len(pieces),
        "start",
        work + [pltpu.SemaphoreType.DMA((n_cols * len(slots),))],
        8 * 10**9,
    )(*lists, start, mask, *pieces)
    if direct:
        gram, _ = add(gram, after(arrived, part))
    pair = jax.ShapeDtypeStruct((n_cols, 2 * col_width, own_users), f32)
    pair_sent, field, first = call(
        first_kernel,
        [pair, vector, vector],
        [smem] * 3 + [vmem] * 5,
        "first",
        work,
        8 * 10**9,
    )(*lists, start, part, gram, y, mask)
    second_sent, dots = call(
        second_kernel,
        [
            jax.ShapeDtypeStruct((n_cols, col_width, own_users), f32),
            jax.ShapeDtypeStruct((devices, 128), f32),
        ],
        [smem] * 3 + [vmem] * 5,
        "second",
        work,
        8 * 10**9,
    )(*lists, field, first, gram, y, mask)

    turned = swap(pair_sent)
    dots = after(dots, *turned)
    turned += swap(second_sent)
    dots = lax.all_to_all(dots, ("rows", "cols"), split_axis=0, concat_axis=0, tiled=True)
    result = jax.ShapeDtypeStruct((col_width, users), f32)
    return tuple(
        call(
            functools.partial(finish_kernel, share),
            [result, result],
            [smem] + [vmem] * (2 + 2 * n_cols),
            "finish",
            [pltpu.VMEM((n_cols, col_width, own_users), f32)] * 3,
            10**9,
        )(info, dots, user_factors, *turned)
    )


def solution(mesh):
    return jax.shard_map(
        on_device,
        mesh=mesh,
        in_specs=(
            P("cols", "rows"),
            P("cols", "rows"),
            P("rows"),
            P("rows"),
            P("rows"),
            P("rows", None, None),
        ),
        out_specs=(P("cols", "rows"), P("cols", "rows")),
        check_vma=False,
    )
```

```python
import functools

import jax
import jax.numpy as jnp
from jax import lax
from jax.experimental import pallas as pl
from jax.experimental.pallas import tpu as pltpu
from jax.sharding import PartitionSpec as P

ridge = 0.5
confidence = 40.0
LIMIT = 24 * 1024 * 1024
f32 = jnp.float32
bf16 = jnp.bfloat16


def matmul(left, right):
    return jnp.dot(left, right, preferred_element_type=f32)


def split(value):
    high = value.astype(bf16)
    low = (value - high.astype(f32)).astype(bf16)
    return high, low


def prepare_kernel(n_cols, side, info_ref, x_hbm, items_hbm, *refs):
    sent, (x_ref, x_pieces, sems) = refs[:n_cols], refs[n_cols:]
    column = info_ref[1]
    share = side // n_cols
    blocks = x_ref.shape[1] // side
    own_users = blocks * share
    span = sent[0].shape[1] - 2 * own_users
    copies = [
        pltpu.make_async_copy(
            items_hbm.at[:, pl.ds(pl.multiple_of((column ^ m) * span, span), span)],
            sent[m].at[:, pl.ds(2 * own_users, span)],
            sems.at[m],
        )
        for m in range(n_cols)
    ]
    fetch = pltpu.make_async_copy(x_hbm, x_ref, sems.at[n_cols])
    fetch.start()
    for copy in copies:
        copy.start()
    fetch.wait()
    for m in range(n_cols):
        x_pieces[m] = jnp.concatenate(
            [x_ref[:, b * side + m * share : b * side + (m + 1) * share] for b in range(blocks)],
            axis=1,
        )
    for m in range(n_cols):
        high, low = split(x_pieces[column ^ m])
        sent[m][:, :own_users] = high
        sent[m][:, own_users : 2 * own_users] = low
    for copy in copies:
        copy.wait()


def mask_kernel(tile_ref, info_ref, mask_hbm, mask, sem):
    slots, share, side = mask.shape
    place = pl.multiple_of(info_ref[1] * share, share)
    for s in range(slots):
        pltpu.make_async_copy(
            mask_hbm.at[jnp.maximum(tile_ref[s], 0), pl.ds(place, share), :], mask.at[s], sem
        ).start()
    pltpu.make_async_copy(mask, mask, sem).wait()

    def clear(s, carry):
        @pl.when(tile_ref[s] < 0)
        def _():
            mask[s] = jnp.zeros((share, side), bf16)

        return carry

    lax.fori_loop(0, slots, clear, 0)


def pick_kernel(direct, info_ref, wanted_ref, items_ref, *out_refs):
    capacity = wanted_ref.shape[1]
    side = out_refs[0].shape[2]
    for o, out_ref in enumerate(out_refs):
        for i in range(out_ref.shape[0] // capacity):
            dest = info_ref[2] ^ o if direct else i
            for r in range(capacity):
                block = jnp.maximum(wanted_ref[dest, r], 0)
                start = pl.multiple_of(block * side, side)
                out_ref[i * capacity + r] = items_ref[:, pl.ds(start, side)]


def pack(ref, gram):
    high, low = split(gram)
    both = jnp.concatenate([high, low], axis=1)
    for k in range(ref.shape[0]):
        ref[k] = both[k * ref.shape[1] : (k + 1) * ref.shape[1]]


def unpack(blocks):
    both = jnp.concatenate([blocks[k] for k in range(blocks.shape[0])], axis=0).astype(f32)
    width = both.shape[1] // 2
    return both[:, :width] + both[:, width:]


def gram_kernel(own_users, info_ref, *refs):
    column = info_ref[1]
    pieces = refs[:-6]
    out_ref, pack_ref, start_ref, starts, items, sems = refs[-6:]
    width = pieces[0].shape[0]
    span = items.shape[1]
    copies = []
    for m, piece in enumerate(pieces):
        place = pl.ds(pl.multiple_of((column ^ m) * width, width), width)
        for source, target in (
            (piece.at[:, pl.ds(0, 2 * own_users)], starts.at[place, :]),
            (piece.at[:, pl.ds(2 * own_users, span)], items.at[place, :]),
        ):
            copies.append(pltpu.make_async_copy(source, target, sems.at[len(copies)]))
            copies[-1].start()
    for copy in copies:
        copy.wait()
    both = starts[...].astype(f32)
    start_ref[...] = both[:, :own_users] + both[:, own_users:]
    gram = lax.dot_general(
        items[...], items[...], (((1,), (1,)), ((), ())), preferred_element_type=f32
    )
    out_ref[...] = gram
    pack(pack_ref, gram)


def add_kernel(gram_ref, arrived_ref, out_ref, pack_ref):
    extra = pack_ref.shape[0]
    total = gram_ref[...] + unpack(arrived_ref[arrived_ref.shape[0] - extra :])
    out_ref[...] = total
    pack(pack_ref, total)


def join_kernel(*refs):
    sources, out_ref, sems = refs[:-2], refs[-2], refs[-1]
    copies = []
    base = 0
    for source in sources:
        rows = source.shape[0]
        copies.append(
            pltpu.make_async_copy(source, out_ref.at[pl.ds(base, rows)], sems.at[len(copies)])
        )
        copies[-1].start()
        base += rows
    for copy in copies:
        copy.wait()


def load(p_hl, vector):
    blocks, share, both = p_hl.shape
    width = both // 2
    high, low = split(vector)
    p_hl[:, :, :width] = high.reshape(blocks, share, width)
    p_hl[:, :, width:] = low.reshape(blocks, share, width)


def dense(p_hl, gram_ref, vector):
    blocks, share, both = p_hl.shape
    width = both // 2
    high, low = split(gram_ref[...])
    table = jnp.concatenate(
        [
            jnp.concatenate([high, low], axis=1),
            jnp.concatenate([high, jnp.zeros_like(low)], axis=1),
        ],
        axis=0,
    )
    product = matmul(p_hl[...].reshape(blocks * share, both), table)
    return product[:, :width] + product[:, width:] + ridge * vector


def sparse(starting, first_slot, slots, user_ref, y, mask, p_hl, acc, held):
    share = mask.shape[1]
    unroll = held.shape[1]
    groups = slots // unroll

    def score(group):
        for j in range(unroll):
            s = first_slot + group * unroll + j
            tile = y[s]
            scores = matmul(p_hl[user_ref[s]], jnp.concatenate([tile, tile], axis=0))
            if starting:
                scores = (1.0 + confidence) - confidence * scores
            high, low = split(mask[s].astype(f32) * scores)
            held[group % 2, j, :share] = high
            held[group % 2, j, share:] = low

    def collect(group):
        terms = []
        for j in range(unroll):
            term = lax.dot_general(
                held[group % 2, j],
                y[first_slot + group * unroll + j],
                (((1,), (1,)), ((), ())),
                preferred_element_type=f32,
            )
            terms.append(term[:share] + term[share:])
        return terms

    def add(group, terms):
        for j, term in enumerate(terms):
            acc[user_ref[first_slot + group * unroll + j]] += term

    score(0)

    def step(group, carry):
        terms = collect(group - 1)
        score(group)
        add(group - 1, terms)
        return carry

    lax.fori_loop(1, groups, step, 0)
    add(groups - 1, collect(groups - 1))


def put(column, ref, vector, part=0):
    n_cols, rows, _ = ref.shape
    turned = vector.T
    width = turned.shape[0] // n_cols
    for m in range(n_cols):
        ref[column ^ m, part * width : (part + 1) * width] = turned[m * width : (m + 1) * width]


def start_kernel(n_cols, first_slot, slots, user_ref, info_ref, x_ref, mask, own, other, *refs):
    part_ref, y, p_hl, held, sems = refs[-5:]
    piece_width = y.shape[1] // n_cols
    column = info_ref[1]
    copies = []
    for m in range(n_cols):
        place = pl.multiple_of((column ^ m) * piece_width, piece_width)
        copies.append(
            pltpu.make_async_copy(
                (other if m % 2 else own).at[pl.ds(m // 2 * slots, slots)],
                y.at[pl.ds(first_slot, slots), pl.ds(place, piece_width), :],
                sems.at[m],
            )
        )
        copies[-1].start()
    load(p_hl, x_ref[...].T)
    if first_slot:
        part_ref[...] = refs[0][...]
    else:
        part_ref[...] = jnp.zeros_like(part_ref)
    for copy in copies:
        copy.wait()
    sparse(True, first_slot, slots, user_ref, y, mask, p_hl, part_ref, held)


def first_kernel(
    user_ref, info_ref, x_ref, part_ref, gram_ref, y, mask,
    sent_ref, field_ref, first_ref, p_hl, acc, held,
):
    start = x_ref[...].T
    load(p_hl, start)
    field = part_ref[...].reshape(start.shape) - dense(p_hl, gram_ref, start)
    field_ref[...] = field
    put(info_ref[1], sent_ref, field)
    load(p_hl, field)
    acc[...] = jnp.zeros_like(acc)
    sparse(False, 0, y.shape[0], user_ref, y, mask, p_hl, acc, held)
    first = confidence * acc[...].reshape(field.shape) + dense(p_hl, gram_ref, field)
    first_ref[...] = first
    put(info_ref[1], sent_ref, first, 1)


def second_kernel(
    user_ref, info_ref, field_ref, first_ref, gram_ref, y, mask, sent_ref, dots_ref, p_hl, acc, held
):
    field = field_ref[...]
    first = first_ref[...]
    load(p_hl, first)
    acc[...] = jnp.zeros_like(acc)
    sparse(False, 0, y.shape[0], user_ref, y, mask, p_hl, acc, held)
    second = confidence * acc[...].reshape(field.shape) + dense(p_hl, gram_ref, first)
    put(info_ref[1], sent_ref, second)

    def total(left, right):
        return jnp.sum(left * right)

    aa, ab, bb = total(field, field), total(field, first), total(first, first)
    guess = jnp.where(bb > 0.0, ab / jnp.where(bb > 0.0, bb, 1.0), 0.0)
    near = field - guess * first
    near_image = first - guess * second
    values = (
        aa,
        ab,
        bb,
        guess,
        total(near, near),
        total(near, first),
        total(near, near_image),
        total(near, second) + total(first, near_image),
        total(first, second),
    )
    lane = lax.broadcasted_iota(jnp.int32, dots_ref.shape, 1)
    dots = jnp.zeros(dots_ref.shape, f32)
    for j, value in enumerate(values):
        dots = jnp.where(lane == j, value, dots)
    dots_ref[...] = dots


def finish_kernel(share, info_ref, dots_ref, x_ref, *refs):
    n_cols = (len(refs) - 5) // 2
    x_out, r_out, field_ref, first_ref, second_ref = refs[2 * n_cols :]
    width = field_ref.shape[1]
    for m in range(n_cols):
        place = info_ref[1] ^ m
        field_ref[place] = refs[m][:width]
        first_ref[place] = refs[m][width:]
        second_ref[place] = refs[n_cols + m][...]
    dots = dots_ref[...]

    def column(j):
        return dots[:, j : j + 1]

    def total(value):
        return jnp.sum(value, axis=0, keepdims=True)

    rr0 = total(column(0))
    ab = total(column(1))
    alpha0 = rr0 / ab
    delta = alpha0 - column(3)
    rr1 = total(column(4) - 2.0 * delta * column(5) + delta * delta * column(2))
    curved = total(column(6) - delta * column(7) + delta * delta * column(8))
    crossed = total(column(5) - delta * column(2))
    beta = rr1 / rr0
    alpha1 = rr1 / (curved + 2.0 * beta * crossed + beta * beta * ab)
    along = alpha0 + alpha1 * (1.0 + beta)
    across = alpha1 * alpha0
    blocks = x_ref.shape[1] // (share * n_cols)
    for b in range(blocks):

        def gather(ref):
            return jnp.concatenate(
                [ref[m, :, b * share : (b + 1) * share] for m in range(n_cols)], axis=1
            )

        field, first, second = gather(field_ref), gather(first_ref), gather(second_ref)
        here = slice(b * share * n_cols, (b + 1) * share * n_cols)
        x_out[:, here] = x_ref[:, here] + along * field - across * first
        r_out[:, here] = field - along * first + across * second


def flip(value, axis, bit):
    size = lax.axis_size(axis)
    return lax.ppermute(value, axis, [(i, i ^ bit) for i in range(size)])


def swap(sent):
    return [sent[0]] + [flip(sent[m], "cols", m) for m in range(1, len(sent))]


def after(value, *others):
    return lax.optimization_barrier((value, *others))[0]


def add_all(value):
    for axis in ("cols", "rows"):
        bit = 1
        while bit < lax.axis_size(axis):
            value = value + flip(value, axis, bit)
            bit *= 2
    return value


def on_device(user_factors, item_factors, tile_user, tile_item, tile_count, tile_mask):
    side = tile_mask.shape[1]
    col_width = user_factors.shape[0]
    column = lax.axis_index("cols").astype(jnp.int32)
    row = lax.axis_index("rows").astype(jnp.int32)
    row_devs = lax.axis_size("rows")
    n_cols = lax.axis_size("cols")
    devices = row_devs * n_cols
    width = col_width * n_cols
    tile_total = tile_user.shape[0]
    users = user_factors.shape[1]
    user_blocks = users // side
    item_blocks = item_factors.shape[1] // side
    share = side // n_cols
    own_users = users // n_cols
    capacity = max(2, (tile_total + row_devs - 1) // row_devs)
    direct = row_devs == 8 and 2 * width == side
    vmem = pl.BlockSpec(memory_space=pltpu.VMEM)
    smem = pl.BlockSpec(memory_space=pltpu.SMEM)
    anywhere = pl.BlockSpec(memory_space=pl.ANY)
    params = pltpu.CompilerParams(vmem_limit_bytes=LIMIT)

    def call(kernel, out_shape, in_specs, name, scratch=(), flops=0, aliases={}):
        return pl.pallas_call(
            kernel,
            out_shape=out_shape,
            in_specs=in_specs,
            out_specs=jax.tree.map(lambda _: vmem, out_shape),
            scratch_shapes=scratch,
            compiler_params=params,
            input_output_aliases=aliases,
            cost_estimate=pl.CostEstimate(
                flops=flops, bytes_accessed=0, transcendentals=0
            ),
            name=name,
        )

    info = jnp.stack([tile_count[0], column, row])
    span = item_factors.shape[1] // n_cols
    sent = call(
        functools.partial(prepare_kernel, n_cols, side),
        [jax.ShapeDtypeStruct((col_width, 2 * own_users + span), bf16)] * n_cols,
        [smem, anywhere, anywhere],
        "prepare",
        [
            pltpu.VMEM(user_factors.shape, f32),
            pltpu.VMEM((n_cols, col_width, own_users), f32),
            pltpu.SemaphoreType.DMA((n_cols + 1,)),
        ],
        10**9,
    )(
        info,
        pltpu.with_memory_space_constraint(user_factors, pltpu.HBM),
        pltpu.with_memory_space_constraint(item_factors, pltpu.HBM),
    )
    shared = swap(sent)

    order = jnp.arange(tile_total, dtype=jnp.int32)
    live = (order < tile_count[0]).astype(jnp.int32)
    tile_item = after(tile_item, sent[0])
    holder = tile_item // item_blocks
    local_block = tile_item % item_blocks
    earlier = (
        (holder[None, :] == holder[:, None])
        & (order[None, :] < order[:, None])
        & (live[None, :] > 0)
    )
    rank = jnp.sum(earlier.astype(jnp.int32), axis=1)
    slot_ids = jnp.minimum(holder * capacity + rank, row_devs * capacity - 1)
    slot_range = jnp.arange(row_devs * capacity, dtype=jnp.int32)
    hits = ((slot_ids[None, :] == slot_range[:, None]) & (live[None, :] > 0)).astype(jnp.int32)
    requests = (jnp.sum(hits * (local_block + 1)[None, :], axis=1) - 1).reshape(row_devs, capacity)
    wanted = lax.all_to_all(requests, "rows", split_axis=0, concat_axis=0, tiled=True)
    block = holder
    if direct:
        step = holder ^ row
        block = step
        for j, spot in ((1, 1), (3, 2), (2, 3), (5, 4), (6, 5), (7, 6), (4, 7)):
            block = jnp.where(step == j, spot, block)
    places = block * capacity + jnp.minimum(rank, capacity - 1)
    hits = (places[None, :] == slot_range[:, None]) & (live[None, :] > 0)
    slot_tiles = jnp.sum(hits.astype(jnp.int32) * (order + 1)[None, :], axis=1) - 1
    slot_users = jnp.sum(hits.astype(jnp.int32) * tile_user[None, :], axis=1)

    picked = call(
        functools.partial(pick_kernel, direct),
        [jax.ShapeDtypeStruct((capacity, col_width, side), bf16)] * row_devs
        if direct
        else [jax.ShapeDtypeStruct((row_devs * capacity, col_width, side), bf16)],
        [smem, smem, vmem],
        "pick",
        flops=10**9,
    )(after(info, *shared), wanted, item_factors)

    def add(gram, arrived):
        return call(add_kernel, [square, packed], [vmem] * 2, "add")(gram, arrived)

    def join(*arrays):
        return jnp.concatenate(arrays, axis=0)

    def gather(*arrays):
        rows = sum(array.shape[0] for array in arrays)
        return call(
            join_kernel,
            [jax.ShapeDtypeStruct((rows, *arrays[0].shape[1:]), bf16)],
            [anywhere] * len(arrays),
            "join",
            [pltpu.SemaphoreType.DMA((len(arrays),))],
            2 * 10**10,
        )(*arrays)[0]

    got = {0: picked[0]}
    if direct:
        for j in (1, 3, 5, 6, 2):
            got[j] = flip(picked[j], "rows", j)
        across = flip(got[0], "cols", 2)
        near = after(gather(got[1], got[3]), across)
        for j in (7, 4):
            got[j] = flip(after(picked[j], got[5], got[6], near), "rows", j)

    square = jax.ShapeDtypeStruct((width, width), f32)
    extra = width // col_width
    packed = jax.ShapeDtypeStruct((extra, col_width, 2 * width), bf16)
    gram, carried, start = call(
        functools.partial(gram_kernel, own_users),
        [square, packed, jax.ShapeDtypeStruct((width, own_users), f32)],
        [smem] + [anywhere] * n_cols,
        "gram",
        [
            pltpu.VMEM((width, 2 * own_users), bf16),
            pltpu.VMEM((width, span), bf16),
            pltpu.SemaphoreType.DMA((2 * n_cols,)),
        ],
        10**9,
    )(after(info, got[1] if direct else picked[0]), *shared)
    strengths = jax.ShapeDtypeStruct((row_devs * capacity, share, side), bf16)
    unroll = capacity if direct else 8
    vector = jax.ShapeDtypeStruct((own_users, width), f32)
    held = jax.ShapeDtypeStruct((row_devs * capacity, width, side), bf16)
    work = [
        pltpu.VMEM((user_blocks, share, 2 * width), bf16),
        pltpu.VMEM((user_blocks, share, width), f32),
        pltpu.VMEM((2, unroll, 2 * share, side), bf16),
    ]
    lists = (slot_users, info)

    def slice_mask(ready):
        return call(
            mask_kernel,
            [strengths],
            [smem, smem, anywhere],
            "mask",
            [pltpu.SemaphoreType.DMA],
            10**9,
        )(
            slot_tiles,
            after(info, ready),
            pltpu.with_memory_space_constraint(tile_mask, pltpu.HBM),
        )[0]

    def begin(first_slot, slots, own, other, *earlier, flops=3 * 10**9):
        return call(
            functools.partial(start_kernel, n_cols, first_slot, slots),
            [jax.ShapeDtypeStruct((user_blocks, share, width), f32), held],
            [smem] * 2 + [vmem] * 2 + [anywhere] * 2 + [vmem] * len(earlier),
            "start",
            [work[0], work[2], pltpu.SemaphoreType.DMA((n_cols,))],
            flops,
            {7: 1} if earlier else {},
        )(*lists, start, mask, own, other, *earlier)

    if direct:
        early = join(got[0], near, across, flip(near, "cols", 2))
        own = gather(got[2], got[5], got[6], carried)
        early_other = flip(after(early, own), "cols", 1)
        own = after(own, early)
        mask = slice_mask(own)
        arrived = flip(own, "cols", 2)
        state = begin(0, 3 * capacity, early, early_other, flops=2 * 10**10)
        last = gather(got[7], got[4])
        arrived = after(arrived, state[0], got[7], got[4])
        gram, carried = add(gram, arrived)
        middle = join(own[: 3 * capacity], arrived[: 3 * capacity], carried)
        middle_other = flip(middle, "cols", 1)
        gram, carried = add(gram, middle_other)

        late = flip(last, "cols", 2)
        state = begin(
            3 * capacity, 3 * capacity, middle, middle_other, *state, flops=2 * 10**10
        )
        gram, carried = add(gram, flip(after(carried, state[0]), "rows", 1))
        late = join(last, after(late, carried))
        late_other = flip(late, "cols", 1)
        gram, carried = add(gram, flip(carried, "rows", 2))
        state = after(state, carried)
        arrived = flip(carried, "rows", 4)
        part, y = begin(6 * capacity, 2 * capacity, late, late_other, *state)
    else:
        mask = slice_mask(gram)
        gram = add_all(gram)
        own = lax.all_to_all(picked[0], "rows", split_axis=0, concat_axis=0, tiled=True)
        own = join(own, flip(own, "cols", 2))
        part, y = begin(0, row_devs * capacity, own, flip(own, "cols", 1))
    if direct:
        gram, _ = add(gram, after(arrived, part))
    pair = jax.ShapeDtypeStruct((n_cols, 2 * col_width, own_users), f32)
    pair_sent, field, first = call(
        first_kernel,
        [pair, vector, vector],
        [smem] * 2 + [vmem] * 5,
        "first",
        work,
        8 * 10**9,
    )(*lists, start, part, gram, y, mask)
    second_sent, dots = call(
        second_kernel,
        [
            jax.ShapeDtypeStruct((n_cols, col_width, own_users), f32),
            jax.ShapeDtypeStruct((devices, 128), f32),
        ],
        [smem] * 2 + [vmem] * 5,
        "second",
        work,
        8 * 10**9,
    )(*lists, field, first, gram, y, mask)

    turned = swap(pair_sent)
    dots = after(dots, *turned)
    turned += swap(second_sent)
    dots = lax.all_to_all(dots, ("rows", "cols"), split_axis=0, concat_axis=0, tiled=True)
    result = jax.ShapeDtypeStruct((col_width, users), f32)
    return tuple(
        call(
            functools.partial(finish_kernel, share),
            [result, result],
            [smem] + [vmem] * (2 + 2 * n_cols),
            "finish",
            [pltpu.VMEM((n_cols, col_width, own_users), f32)] * 3,
            10**9,
        )(info, dots, user_factors, *turned)
    )


def solution(mesh):
    return jax.shard_map(
        on_device,
        mesh=mesh,
        in_specs=(
            P("cols", "rows"),
            P("cols", "rows"),
            P("rows"),
            P("rows"),
            P("rows"),
            P("rows", None, None),
        ),
        out_specs=(P("cols", "rows"), P("cols", "rows")),
        check_vma=False,
    )
```

```python
import functools

import jax
import jax.numpy as jnp
from jax import lax
from jax.experimental import pallas as pl
from jax.experimental.pallas import tpu as pltpu
from jax.sharding import PartitionSpec as P

ridge = 0.5
confidence = 40.0
UNROLL = 8
LIMIT = 24 * 1024 * 1024
f32 = jnp.float32
bf16 = jnp.bfloat16


def matmul(left, right):
    return jnp.dot(left, right, preferred_element_type=f32)


def split(value):
    high = value.astype(bf16)
    low = (value - high.astype(f32)).astype(bf16)
    return high, low


def prepare_kernel(n_cols, side, info_ref, x_hbm, items_hbm, *refs):
    sent, (x_ref, x_pieces, sems) = refs[:n_cols], refs[n_cols:]
    column = info_ref[1]
    share = side // n_cols
    blocks = x_ref.shape[1] // side
    own_users = blocks * share
    span = sent[0].shape[1] - 2 * own_users
    copies = [
        pltpu.make_async_copy(
            items_hbm.at[:, pl.ds(pl.multiple_of((column ^ m) * span, span), span)],
            sent[m].at[:, pl.ds(2 * own_users, span)],
            sems.at[m],
        )
        for m in range(n_cols)
    ]
    fetch = pltpu.make_async_copy(x_hbm, x_ref, sems.at[n_cols])
    fetch.start()
    for copy in copies:
        copy.start()
    fetch.wait()
    for m in range(n_cols):
        x_pieces[m] = jnp.concatenate(
            [x_ref[:, b * side + m * share : b * side + (m + 1) * share] for b in range(blocks)],
            axis=1,
        )
    for m in range(n_cols):
        high, low = split(x_pieces[column ^ m])
        sent[m][:, :own_users] = high
        sent[m][:, own_users : 2 * own_users] = low
    for copy in copies:
        copy.wait()


def mask_kernel(info_ref, mask_hbm, mask, sem):
    tiles, share, side = mask.shape
    copy = pltpu.make_async_copy(
        mask_hbm.at[:, pl.ds(pl.multiple_of(info_ref[1] * share, share), share), :], mask, sem
    )
    copy.start()
    copy.wait()

    def clear(t, carry):
        mask[t] = jnp.zeros((share, side), bf16)
        return carry

    lax.fori_loop(info_ref[0], tiles, clear, 0)


def pick_kernel(direct, info_ref, wanted_ref, items_ref, *out_refs):
    capacity = wanted_ref.shape[1]
    side = out_refs[0].shape[2]
    for o, out_ref in enumerate(out_refs):
        for i in range(out_ref.shape[0] // capacity):
            dest = info_ref[2] ^ o if direct else i
            for r in range(capacity):
                block = jnp.maximum(wanted_ref[dest, r], 0)
                start = pl.multiple_of(block * side, side)
                out_ref[i * capacity + r] = items_ref[:, pl.ds(start, side)]


def pack(ref, gram):
    high, low = split(gram)
    both = jnp.concatenate([high, low], axis=1)
    for k in range(ref.shape[0]):
        ref[k] = both[k * ref.shape[1] : (k + 1) * ref.shape[1]]


def unpack(blocks):
    both = jnp.concatenate([blocks[k] for k in range(blocks.shape[0])], axis=0).astype(f32)
    width = both.shape[1] // 2
    return both[:, :width] + both[:, width:]


def gram_kernel(own_users, info_ref, *refs):
    column = info_ref[1]
    pieces = refs[:-6]
    out_ref, pack_ref, start_ref, starts, items, sems = refs[-6:]
    width = pieces[0].shape[0]
    span = items.shape[1]
    copies = []
    for m, piece in enumerate(pieces):
        place = pl.ds(pl.multiple_of((column ^ m) * width, width), width)
        for source, target in (
            (piece.at[:, pl.ds(0, 2 * own_users)], starts.at[place, :]),
            (piece.at[:, pl.ds(2 * own_users, span)], items.at[place, :]),
        ):
            copies.append(pltpu.make_async_copy(source, target, sems.at[len(copies)]))
            copies[-1].start()
    for copy in copies:
        copy.wait()
    both = starts[...].astype(f32)
    start_ref[...] = both[:, :own_users] + both[:, own_users:]
    gram = lax.dot_general(
        items[...], items[...], (((1,), (1,)), ((), ())), preferred_element_type=f32
    )
    out_ref[...] = gram
    pack(pack_ref, gram)


def add_kernel(gram_ref, arrived_ref, out_ref, pack_ref):
    extra = pack_ref.shape[0]
    total = gram_ref[...] + unpack(arrived_ref[arrived_ref.shape[0] - extra :])
    out_ref[...] = total
    pack(pack_ref, total)


def join_kernel(*refs):
    sources, out_ref, sems = refs[:-2], refs[-2], refs[-1]
    copies = []
    base = 0
    for source in sources:
        rows = source.shape[0]
        copies.append(
            pltpu.make_async_copy(source, out_ref.at[pl.ds(base, rows)], sems.at[len(copies)])
        )
        copies[-1].start()
        base += rows
    for copy in copies:
        copy.wait()


def load(p_hl, vector):
    blocks, share, both = p_hl.shape
    width = both // 2
    high, low = split(vector)
    p_hl[:, :, :width] = high.reshape(blocks, share, width)
    p_hl[:, :, width:] = low.reshape(blocks, share, width)


def dense(p_hl, gram_ref, vector):
    blocks, share, both = p_hl.shape
    width = both // 2
    high, low = split(gram_ref[...])
    table = jnp.concatenate(
        [
            jnp.concatenate([high, low], axis=1),
            jnp.concatenate([high, jnp.zeros_like(low)], axis=1),
        ],
        axis=0,
    )
    product = matmul(p_hl[...].reshape(blocks * share, both), table)
    return product[:, :width] + product[:, width:] + ridge * vector


def sparse(starting, slot_ref, user_ref, y, mask, p_hl, acc, held):
    tiles, share, side = mask.shape
    groups = tiles // UNROLL
    acc[...] = jnp.zeros_like(acc)

    def score(group):
        for j in range(UNROLL):
            t = group * UNROLL + j
            tile = y[slot_ref[t]]
            scores = matmul(p_hl[user_ref[t]], jnp.concatenate([tile, tile], axis=0))
            if starting:
                scores = (1.0 + confidence) - confidence * scores
            high, low = split(mask[t].astype(f32) * scores)
            held[group % 2, j, :share] = high
            held[group % 2, j, share:] = low

    def collect(group):
        terms = []
        for j in range(UNROLL):
            t = group * UNROLL + j
            term = lax.dot_general(
                held[group % 2, j],
                y[slot_ref[t]],
                (((1,), (1,)), ((), ())),
                preferred_element_type=f32,
            )
            terms.append(term[:share] + term[share:])
        return terms

    def add(group, terms):
        for j, term in enumerate(terms):
            acc[user_ref[group * UNROLL + j]] += term

    score(0)

    def step(group, carry):
        terms = collect(group - 1)
        score(group)
        add(group - 1, terms)
        return carry

    lax.fori_loop(1, groups, step, 0)
    add(groups - 1, collect(groups - 1))


def put(column, ref, vector, part=0):
    n_cols, rows, _ = ref.shape
    turned = vector.T
    width = turned.shape[0] // n_cols
    for m in range(n_cols):
        ref[column ^ m, part * width : (part + 1) * width] = turned[m * width : (m + 1) * width]


def start_kernel(n_cols, slots, slot_ref, user_ref, info_ref, x_ref, mask, *refs):
    pieces = refs[: 2 * len(slots)]
    part_ref, y, p_hl, acc, held, sems = refs[2 * len(slots) :]
    piece_width = y.shape[1] // n_cols
    column = info_ref[1]
    copies = []
    base = 0
    for k, count in enumerate(slots):
        for m in range(n_cols):
            place = pl.multiple_of((column ^ m) * piece_width, piece_width)
            source = pieces[2 * k + m % 2].at[pl.ds(m // 2 * count, count)]
            copies.append(
                pltpu.make_async_copy(
                    source,
                    y.at[pl.ds(base, count), pl.ds(place, piece_width), :],
                    sems.at[len(copies)],
                )
            )
        base += count
    for copy in copies:
        copy.start()
    load(p_hl, x_ref[...].T)
    for copy in copies:
        copy.wait()
    sparse(True, slot_ref, user_ref, y, mask, p_hl, acc, held)
    part_ref[...] = acc[...].reshape(part_ref.shape)


def first_kernel(
    slot_ref, user_ref, info_ref, x_ref, part_ref, gram_ref, y, mask,
    sent_ref, field_ref, first_ref, p_hl, acc, held,
):
    start = x_ref[...].T
    load(p_hl, start)
    field = part_ref[...] - dense(p_hl, gram_ref, start)
    field_ref[...] = field
    put(info_ref[1], sent_ref, field)
    load(p_hl, field)
    sparse(False, slot_ref, user_ref, y, mask, p_hl, acc, held)
    first = confidence * acc[...].reshape(field.shape) + dense(p_hl, gram_ref, field)
    first_ref[...] = first
    put(info_ref[1], sent_ref, first, 1)


def second_kernel(
    slot_ref, user_ref, info_ref, field_ref, first_ref, gram_ref, y, mask, sent_ref, dots_ref, p_hl, acc, held
):
    field = field_ref[...]
    first = first_ref[...]
    load(p_hl, first)
    sparse(False, slot_ref, user_ref, y, mask, p_hl, acc, held)
    second = confidence * acc[...].reshape(field.shape) + dense(p_hl, gram_ref, first)
    put(info_ref[1], sent_ref, second)

    def total(left, right):
        return jnp.sum(left * right)

    aa, ab, bb = total(field, field), total(field, first), total(first, first)
    guess = jnp.where(bb > 0.0, ab / jnp.where(bb > 0.0, bb, 1.0), 0.0)
    near = field - guess * first
    near_image = first - guess * second
    values = (
        aa,
        ab,
        bb,
        guess,
        total(near, near),
        total(near, first),
        total(near, near_image),
        total(near, second) + total(first, near_image),
        total(first, second),
    )
    lane = lax.broadcasted_iota(jnp.int32, dots_ref.shape, 1)
    dots = jnp.zeros(dots_ref.shape, f32)
    for j, value in enumerate(values):
        dots = jnp.where(lane == j, value, dots)
    dots_ref[...] = dots


def finish_kernel(share, info_ref, dots_ref, x_ref, *refs):
    n_cols = (len(refs) - 5) // 2
    x_out, r_out, field_ref, first_ref, second_ref = refs[2 * n_cols :]
    width = field_ref.shape[1]
    for m in range(n_cols):
        place = info_ref[1] ^ m
        field_ref[place] = refs[m][:width]
        first_ref[place] = refs[m][width:]
        second_ref[place] = refs[n_cols + m][...]
    dots = dots_ref[...]

    def column(j):
        return dots[:, j : j + 1]

    def total(value):
        return jnp.sum(value, axis=0, keepdims=True)

    rr0 = total(column(0))
    ab = total(column(1))
    alpha0 = rr0 / ab
    delta = alpha0 - column(3)
    rr1 = total(column(4) - 2.0 * delta * column(5) + delta * delta * column(2))
    curved = total(column(6) - delta * column(7) + delta * delta * column(8))
    crossed = total(column(5) - delta * column(2))
    beta = rr1 / rr0
    alpha1 = rr1 / (curved + 2.0 * beta * crossed + beta * beta * ab)
    along = alpha0 + alpha1 * (1.0 + beta)
    across = alpha1 * alpha0
    blocks = x_ref.shape[1] // (share * n_cols)
    for b in range(blocks):

        def gather(ref):
            return jnp.concatenate(
                [ref[m, :, b * share : (b + 1) * share] for m in range(n_cols)], axis=1
            )

        field, first, second = gather(field_ref), gather(first_ref), gather(second_ref)
        here = slice(b * share * n_cols, (b + 1) * share * n_cols)
        x_out[:, here] = x_ref[:, here] + along * field - across * first
        r_out[:, here] = field - along * first + across * second


def flip(value, axis, bit):
    size = lax.axis_size(axis)
    return lax.ppermute(value, axis, [(i, i ^ bit) for i in range(size)])


def swap(sent):
    return [sent[0]] + [flip(sent[m], "cols", m) for m in range(1, len(sent))]


def after(value, *others):
    return lax.optimization_barrier((value, *others))[0]


def add_all(value):
    for axis in ("cols", "rows"):
        bit = 1
        while bit < lax.axis_size(axis):
            value = value + flip(value, axis, bit)
            bit *= 2
    return value


def on_device(user_factors, item_factors, tile_user, tile_item, tile_count, tile_mask):
    side = tile_mask.shape[1]
    col_width = user_factors.shape[0]
    column = lax.axis_index("cols").astype(jnp.int32)
    row = lax.axis_index("rows").astype(jnp.int32)
    row_devs = lax.axis_size("rows")
    n_cols = lax.axis_size("cols")
    devices = row_devs * n_cols
    width = col_width * n_cols
    tile_total = tile_user.shape[0]
    users = user_factors.shape[1]
    user_blocks = users // side
    item_blocks = item_factors.shape[1] // side
    share = side // n_cols
    own_users = users // n_cols
    capacity = max(2, (tile_total + row_devs - 1) // row_devs)
    direct = row_devs == 8 and 2 * width == side
    vmem = pl.BlockSpec(memory_space=pltpu.VMEM)
    smem = pl.BlockSpec(memory_space=pltpu.SMEM)
    anywhere = pl.BlockSpec(memory_space=pl.ANY)
    params = pltpu.CompilerParams(vmem_limit_bytes=LIMIT)

    def call(kernel, out_shape, in_specs, name, scratch=(), flops=0):
        return pl.pallas_call(
            kernel,
            out_shape=out_shape,
            in_specs=in_specs,
            out_specs=jax.tree.map(lambda _: vmem, out_shape),
            scratch_shapes=scratch,
            compiler_params=params,
            cost_estimate=pl.CostEstimate(
                flops=flops, bytes_accessed=0, transcendentals=0
            ),
            name=name,
        )

    info = jnp.stack([tile_count[0], column, row])
    span = item_factors.shape[1] // n_cols
    sent = call(
        functools.partial(prepare_kernel, n_cols, side),
        [jax.ShapeDtypeStruct((col_width, 2 * own_users + span), bf16)] * n_cols,
        [smem, anywhere, anywhere],
        "prepare",
        [
            pltpu.VMEM(user_factors.shape, f32),
            pltpu.VMEM((n_cols, col_width, own_users), f32),
            pltpu.SemaphoreType.DMA((n_cols + 1,)),
        ],
        10**9,
    )(
        info,
        pltpu.with_memory_space_constraint(user_factors, pltpu.HBM),
        pltpu.with_memory_space_constraint(item_factors, pltpu.HBM),
    )
    shared = swap(sent)

    order = jnp.arange(tile_total, dtype=jnp.int32)
    live = (order < tile_count[0]).astype(jnp.int32)
    tile_item = after(tile_item, sent[0])
    holder = tile_item // item_blocks
    local_block = tile_item % item_blocks
    earlier = (
        (holder[None, :] == holder[:, None])
        & (order[None, :] < order[:, None])
        & (live[None, :] > 0)
    )
    rank = jnp.sum(earlier.astype(jnp.int32), axis=1)
    slot_ids = jnp.minimum(holder * capacity + rank, row_devs * capacity - 1)
    slot_range = jnp.arange(row_devs * capacity, dtype=jnp.int32)
    hits = ((slot_ids[None, :] == slot_range[:, None]) & (live[None, :] > 0)).astype(jnp.int32)
    requests = (jnp.sum(hits * (local_block + 1)[None, :], axis=1) - 1).reshape(row_devs, capacity)
    wanted = lax.all_to_all(requests, "rows", split_axis=0, concat_axis=0, tiled=True)
    block = holder
    if direct:
        step = holder ^ row
        block = step
        for j, spot in ((2, 3), (3, 2), (5, 6), (6, 5)):
            block = jnp.where(step == j, spot, block)
    places = block * capacity + jnp.minimum(rank, capacity - 1)
    places = jnp.where(live > 0, places, places[0])
    tile_users = jnp.where(live > 0, tile_user, tile_user[0])

    picked = call(
        functools.partial(pick_kernel, direct),
        [jax.ShapeDtypeStruct((capacity, col_width, side), bf16)] * row_devs
        if direct
        else [jax.ShapeDtypeStruct((row_devs * capacity, col_width, side), bf16)],
        [smem, smem, vmem],
        "pick",
        flops=10**9,
    )(after(info, *shared), wanted, item_factors)

    def join(*arrays):
        return jnp.concatenate(arrays, axis=0)

    def gather(*arrays):
        rows = sum(array.shape[0] for array in arrays)
        return call(
            join_kernel,
            [jax.ShapeDtypeStruct((rows, *arrays[0].shape[1:]), bf16)],
            [anywhere] * len(arrays),
            "join",
            [pltpu.SemaphoreType.DMA((len(arrays),))],
            2 * 10**10,
        )(*arrays)[0]

    def add(gram, arrived):
        return call(add_kernel, [square, packed], [vmem] * 2, "add")(gram, arrived)

    got = {0: picked[0]}
    if direct:
        for j in (1, 3, 4, 6, 2):
            got[j] = flip(picked[j], "rows", j)
        across = flip(got[0], "cols", 2)
        near = after(gather(got[1], got[3]), across)
        for j in (5, 7):
            got[j] = flip(after(picked[j], got[4], got[6], near), "rows", j)

    square = jax.ShapeDtypeStruct((width, width), f32)
    extra = width // col_width
    packed = jax.ShapeDtypeStruct((extra, col_width, 2 * width), bf16)
    gram, carried, start = call(
        functools.partial(gram_kernel, own_users),
        [square, packed, jax.ShapeDtypeStruct((width, own_users), f32)],
        [smem] + [anywhere] * n_cols,
        "gram",
        [
            pltpu.VMEM((width, 2 * own_users), bf16),
            pltpu.VMEM((width, span), bf16),
            pltpu.SemaphoreType.DMA((2 * n_cols,)),
        ],
        10**9,
    )(after(info, near if direct else picked[0]), *shared)
    strengths = jax.ShapeDtypeStruct((tile_total, share, side), bf16)

    def slice_mask(ready):
        return call(
            mask_kernel,
            [strengths],
            [smem, anywhere],
            "mask",
            [pltpu.SemaphoreType.DMA],
            10**9,
        )(after(info, ready), pltpu.with_memory_space_constraint(tile_mask, pltpu.HBM))[0]

    if direct:
        slots = (3 * capacity, 3 * capacity, 2 * capacity)
        early = join(got[0], near, across, flip(near, "cols", 2))
        pieces = [early, flip(early, "cols", 1)]

        arrived = flip(carried, "rows", 1)
        gram, carried = add(gram, after(arrived, got[4], got[6]))
        own = after(gather(got[2], got[4], got[6]), early)
        mask = slice_mask(own)
        arrived = flip(after(carried, own), "rows", 2)
        gram, carried = add(gram, after(arrived, mask))
        own = join(own, flip(own, "cols", 2))
        pieces += [own, flip(after(own, mask), "cols", 1)]

        gram, carried = add(gram, after(flip(carried, "rows", 4), own))
        own = gather(got[5], got[7], carried)
        arrived = flip(own, "cols", 2)
        gram, carried = add(gram, arrived)
        own = join(own[: 2 * capacity], arrived[: 2 * capacity], carried)
        arrived = flip(own, "cols", 1)
        pieces += [own, arrived]
    else:
        slots = (row_devs * capacity,)
        mask = slice_mask(gram)
        gram = add_all(gram)
        own = lax.all_to_all(picked[0], "rows", split_axis=0, concat_axis=0, tiled=True)
        own = join(own, flip(own, "cols", 2))
        pieces = [own, flip(own, "cols", 1)]

    vector = jax.ShapeDtypeStruct((own_users, width), f32)
    held = jax.ShapeDtypeStruct((row_devs * capacity, width, side), bf16)
    work = [
        pltpu.VMEM((user_blocks, share, 2 * width), bf16),
        pltpu.VMEM((user_blocks, share, width), f32),
        pltpu.VMEM((2, UNROLL, 2 * share, side), bf16),
    ]
    lists = (places, tile_users, info)
    part, y = call(
        functools.partial(start_kernel, n_cols, slots),
        [vector, held],
        [smem] * 3 + [vmem] * 2 + [anywhere] * len(pieces),
        "start",
        work + [pltpu.SemaphoreType.DMA((n_cols * len(slots),))],
        8 * 10**9,
    )(*lists, start, mask, *pieces)
    if direct:
        gram, _ = add(gram, after(arrived, part))
    pair = jax.ShapeDtypeStruct((n_cols, 2 * col_width, own_users), f32)
    pair_sent, field, first = call(
        first_kernel,
        [pair, vector, vector],
        [smem] * 3 + [vmem] * 5,
        "first",
        work,
        8 * 10**9,
    )(*lists, start, part, gram, y, mask)
    second_sent, dots = call(
        second_kernel,
        [
            jax.ShapeDtypeStruct((n_cols, col_width, own_users), f32),
            jax.ShapeDtypeStruct((devices, 128), f32),
        ],
        [smem] * 3 + [vmem] * 5,
        "second",
        work,
        8 * 10**9,
    )(*lists, field, first, gram, y, mask)

    turned = swap(pair_sent)
    dots = after(dots, *turned)
    turned += swap(second_sent)
    dots = lax.all_to_all(dots, ("rows", "cols"), split_axis=0, concat_axis=0, tiled=True)
    result = jax.ShapeDtypeStruct((col_width, users), f32)
    return tuple(
        call(
            functools.partial(finish_kernel, share),
            [result, result],
            [smem] + [vmem] * (2 + 2 * n_cols),
            "finish",
            [pltpu.VMEM((n_cols, col_width, own_users), f32)] * 3,
            10**9,
        )(info, dots, user_factors, *turned)
    )


def solution(mesh):
    return jax.shard_map(
        on_device,
        mesh=mesh,
        in_specs=(
            P("cols", "rows"),
            P("cols", "rows"),
            P("rows"),
            P("rows"),
            P("rows"),
            P("rows", None, None),
        ),
        out_specs=(P("cols", "rows"), P("cols", "rows")),
        check_vma=False,
    )
```

```python
import functools

import jax
import jax.numpy as jnp
from jax import lax
from jax.experimental import pallas as pl
from jax.experimental.pallas import tpu as pltpu
from jax.sharding import PartitionSpec as P

ridge = 0.5
confidence = 40.0
UNROLL = 8
LIMIT = 24 * 1024 * 1024
f32 = jnp.float32
bf16 = jnp.bfloat16


def matmul(left, right):
    return jnp.dot(left, right, preferred_element_type=f32)


def split(value):
    high = value.astype(bf16)
    low = (value - high.astype(f32)).astype(bf16)
    return high, low


def prepare_kernel(n_cols, side, info_ref, x_hbm, items_hbm, *refs):
    sent, (x_ref, x_pieces, sems) = refs[:n_cols], refs[n_cols:]
    column = info_ref[1]
    share = side // n_cols
    blocks = x_ref.shape[1] // side
    own_users = blocks * share
    span = sent[0].shape[1] - 2 * own_users
    copies = [
        pltpu.make_async_copy(
            items_hbm.at[:, pl.ds(pl.multiple_of((column ^ m) * span, span), span)],
            sent[m].at[:, pl.ds(2 * own_users, span)],
            sems.at[m],
        )
        for m in range(n_cols)
    ]
    fetch = pltpu.make_async_copy(x_hbm, x_ref, sems.at[n_cols])
    fetch.start()
    for copy in copies:
        copy.start()
    fetch.wait()
    for m in range(n_cols):
        x_pieces[m] = jnp.concatenate(
            [x_ref[:, b * side + m * share : b * side + (m + 1) * share] for b in range(blocks)],
            axis=1,
        )
    for m in range(n_cols):
        high, low = split(x_pieces[column ^ m])
        sent[m][:, :own_users] = high
        sent[m][:, own_users : 2 * own_users] = low
    for copy in copies:
        copy.wait()


def mask_kernel(info_ref, mask_hbm, mask, sem):
    tiles, share, side = mask.shape
    copy = pltpu.make_async_copy(
        mask_hbm.at[:, pl.ds(pl.multiple_of(info_ref[1] * share, share), share), :], mask, sem
    )
    copy.start()
    copy.wait()

    def clear(t, carry):
        mask[t] = jnp.zeros((share, side), bf16)
        return carry

    lax.fori_loop(info_ref[0], tiles, clear, 0)


def pick_kernel(direct, info_ref, wanted_ref, items_ref, *out_refs):
    capacity = wanted_ref.shape[1]
    side = out_refs[0].shape[2]
    for o, out_ref in enumerate(out_refs):
        for i in range(out_ref.shape[0] // capacity):
            dest = info_ref[2] ^ o if direct else i
            for r in range(capacity):
                block = jnp.maximum(wanted_ref[dest, r], 0)
                start = pl.multiple_of(block * side, side)
                out_ref[i * capacity + r] = items_ref[:, pl.ds(start, side)]


def pack(ref, gram):
    high, low = split(gram)
    both = jnp.concatenate([high, low], axis=1)
    for k in range(ref.shape[0]):
        ref[k] = both[k * ref.shape[1] : (k + 1) * ref.shape[1]]


def unpack(blocks):
    both = jnp.concatenate([blocks[k] for k in range(blocks.shape[0])], axis=0).astype(f32)
    width = both.shape[1] // 2
    return both[:, :width] + both[:, width:]


def gram_kernel(own_users, info_ref, *refs):
    column = info_ref[1]
    pieces = refs[:-6]
    out_ref, pack_ref, start_ref, starts, items, sems = refs[-6:]
    width = pieces[0].shape[0]
    span = items.shape[1]
    copies = []
    for m, piece in enumerate(pieces):
        place = pl.ds(pl.multiple_of((column ^ m) * width, width), width)
        for source, target in (
            (piece.at[:, pl.ds(0, 2 * own_users)], starts.at[place, :]),
            (piece.at[:, pl.ds(2 * own_users, span)], items.at[place, :]),
        ):
            copies.append(pltpu.make_async_copy(source, target, sems.at[len(copies)]))
            copies[-1].start()
    for copy in copies:
        copy.wait()
    both = starts[...].astype(f32)
    start_ref[...] = both[:, :own_users] + both[:, own_users:]
    gram = lax.dot_general(
        items[...], items[...], (((1,), (1,)), ((), ())), preferred_element_type=f32
    )
    out_ref[...] = gram
    pack(pack_ref, gram)


def add_kernel(gram_ref, *refs):
    out_ref, pack_ref = refs[-2:]
    extra = pack_ref.shape[0]
    total = gram_ref[...]
    for arrived_ref in refs[:-2]:
        total = total + unpack(arrived_ref[arrived_ref.shape[0] - extra :])
    out_ref[...] = total
    pack(pack_ref, total)


def join_kernel(*refs):
    sources, out_ref, sems = refs[:-2], refs[-2], refs[-1]
    copies = []
    base = 0
    for source in sources:
        rows = source.shape[0]
        copies.append(
            pltpu.make_async_copy(source, out_ref.at[pl.ds(base, rows)], sems.at[len(copies)])
        )
        copies[-1].start()
        base += rows
    for copy in copies:
        copy.wait()


def load(p_hl, vector):
    blocks, share, both = p_hl.shape
    width = both // 2
    high, low = split(vector)
    p_hl[:, :, :width] = high.reshape(blocks, share, width)
    p_hl[:, :, width:] = low.reshape(blocks, share, width)


def dense(p_hl, gram_ref, vector):
    blocks, share, both = p_hl.shape
    width = both // 2
    high, low = split(gram_ref[...])
    table = jnp.concatenate(
        [
            jnp.concatenate([high, low], axis=1),
            jnp.concatenate([high, jnp.zeros_like(low)], axis=1),
        ],
        axis=0,
    )
    product = matmul(p_hl[...].reshape(blocks * share, both), table)
    return product[:, :width] + product[:, width:] + ridge * vector


def sparse(starting, slot_ref, user_ref, y, mask, p_hl, acc, held):
    tiles, share, side = mask.shape
    groups = tiles // UNROLL
    acc[...] = jnp.zeros_like(acc)

    def score(group):
        for j in range(UNROLL):
            t = group * UNROLL + j
            tile = y[slot_ref[t]]
            scores = matmul(p_hl[user_ref[t]], jnp.concatenate([tile, tile], axis=0))
            if starting:
                scores = (1.0 + confidence) - confidence * scores
            high, low = split(mask[t].astype(f32) * scores)
            held[group % 2, j, :share] = high
            held[group % 2, j, share:] = low

    def collect(group):
        terms = []
        for j in range(UNROLL):
            t = group * UNROLL + j
            term = lax.dot_general(
                held[group % 2, j],
                y[slot_ref[t]],
                (((1,), (1,)), ((), ())),
                preferred_element_type=f32,
            )
            terms.append(term[:share] + term[share:])
        return terms

    def add(group, terms):
        for j, term in enumerate(terms):
            acc[user_ref[group * UNROLL + j]] += term

    score(0)

    def step(group, carry):
        terms = collect(group - 1)
        score(group)
        add(group - 1, terms)
        return carry

    lax.fori_loop(1, groups, step, 0)
    add(groups - 1, collect(groups - 1))


def put(column, ref, vector, part=0):
    n_cols, rows, _ = ref.shape
    turned = vector.T
    width = turned.shape[0] // n_cols
    for m in range(n_cols):
        ref[column ^ m, part * width : (part + 1) * width] = turned[m * width : (m + 1) * width]


def start_kernel(n_cols, slots, slot_ref, user_ref, info_ref, x_ref, mask, *refs):
    pieces = refs[: 2 * len(slots)]
    part_ref, y, p_hl, acc, held, sems = refs[2 * len(slots) :]
    piece_width = y.shape[1] // n_cols
    column = info_ref[1]
    copies = []
    base = 0
    for k, count in enumerate(slots):
        for m in range(n_cols):
            place = pl.multiple_of((column ^ m) * piece_width, piece_width)
            source = pieces[2 * k + m % 2].at[pl.ds(m // 2 * count, count)]
            copies.append(
                pltpu.make_async_copy(
                    source,
                    y.at[pl.ds(base, count), pl.ds(place, piece_width), :],
                    sems.at[len(copies)],
                )
            )
        base += count
    for copy in copies:
        copy.start()
    load(p_hl, x_ref[...].T)
    for copy in copies:
        copy.wait()
    sparse(True, slot_ref, user_ref, y, mask, p_hl, acc, held)
    part_ref[...] = acc[...].reshape(part_ref.shape)


def first_kernel(
    slot_ref, user_ref, info_ref, x_ref, part_ref, gram_ref, y, mask,
    sent_ref, field_ref, first_ref, p_hl, acc, held,
):
    start = x_ref[...].T
    load(p_hl, start)
    field = part_ref[...] - dense(p_hl, gram_ref, start)
    field_ref[...] = field
    put(info_ref[1], sent_ref, field)
    load(p_hl, field)
    sparse(False, slot_ref, user_ref, y, mask, p_hl, acc, held)
    first = confidence * acc[...].reshape(field.shape) + dense(p_hl, gram_ref, field)
    first_ref[...] = first
    put(info_ref[1], sent_ref, first, 1)


def second_kernel(
    slot_ref, user_ref, info_ref, field_ref, first_ref, gram_ref, y, mask, sent_ref, dots_ref, p_hl, acc, held
):
    field = field_ref[...]
    first = first_ref[...]
    load(p_hl, first)
    sparse(False, slot_ref, user_ref, y, mask, p_hl, acc, held)
    second = confidence * acc[...].reshape(field.shape) + dense(p_hl, gram_ref, first)
    put(info_ref[1], sent_ref, second)

    def total(left, right):
        return jnp.sum(left * right)

    aa, ab, bb = total(field, field), total(field, first), total(first, first)
    guess = jnp.where(bb > 0.0, ab / jnp.where(bb > 0.0, bb, 1.0), 0.0)
    near = field - guess * first
    near_image = first - guess * second
    values = (
        aa,
        ab,
        bb,
        guess,
        total(near, near),
        total(near, first),
        total(near, near_image),
        total(near, second) + total(first, near_image),
        total(first, second),
    )
    lane = lax.broadcasted_iota(jnp.int32, dots_ref.shape, 1)
    dots = jnp.zeros(dots_ref.shape, f32)
    for j, value in enumerate(values):
        dots = jnp.where(lane == j, value, dots)
    dots_ref[...] = dots


def finish_kernel(share, info_ref, dots_ref, x_ref, *refs):
    n_cols = (len(refs) - 5) // 2
    x_out, r_out, field_ref, first_ref, second_ref = refs[2 * n_cols :]
    width = field_ref.shape[1]
    for m in range(n_cols):
        place = info_ref[1] ^ m
        field_ref[place] = refs[m][:width]
        first_ref[place] = refs[m][width:]
        second_ref[place] = refs[n_cols + m][...]
    dots = dots_ref[...]

    def column(j):
        return dots[:, j : j + 1]

    def total(value):
        return jnp.sum(value, axis=0, keepdims=True)

    rr0 = total(column(0))
    ab = total(column(1))
    alpha0 = rr0 / ab
    delta = alpha0 - column(3)
    rr1 = total(column(4) - 2.0 * delta * column(5) + delta * delta * column(2))
    curved = total(column(6) - delta * column(7) + delta * delta * column(8))
    crossed = total(column(5) - delta * column(2))
    beta = rr1 / rr0
    alpha1 = rr1 / (curved + 2.0 * beta * crossed + beta * beta * ab)
    along = alpha0 + alpha1 * (1.0 + beta)
    across = alpha1 * alpha0
    blocks = x_ref.shape[1] // (share * n_cols)
    for b in range(blocks):

        def gather(ref):
            return jnp.concatenate(
                [ref[m, :, b * share : (b + 1) * share] for m in range(n_cols)], axis=1
            )

        field, first, second = gather(field_ref), gather(first_ref), gather(second_ref)
        here = slice(b * share * n_cols, (b + 1) * share * n_cols)
        x_out[:, here] = x_ref[:, here] + along * field - across * first
        r_out[:, here] = field - along * first + across * second


def flip(value, axis, bit):
    size = lax.axis_size(axis)
    return lax.ppermute(value, axis, [(i, i ^ bit) for i in range(size)])


def swap(sent):
    return [sent[0]] + [flip(sent[m], "cols", m) for m in range(1, len(sent))]


def after(value, *others):
    return lax.optimization_barrier((value, *others))[0]


def add_all(value):
    for axis in ("cols", "rows"):
        bit = 1
        while bit < lax.axis_size(axis):
            value = value + flip(value, axis, bit)
            bit *= 2
    return value


def on_device(user_factors, item_factors, tile_user, tile_item, tile_count, tile_mask):
    side = tile_mask.shape[1]
    col_width = user_factors.shape[0]
    column = lax.axis_index("cols").astype(jnp.int32)
    row = lax.axis_index("rows").astype(jnp.int32)
    row_devs = lax.axis_size("rows")
    n_cols = lax.axis_size("cols")
    devices = row_devs * n_cols
    width = col_width * n_cols
    tile_total = tile_user.shape[0]
    users = user_factors.shape[1]
    user_blocks = users // side
    item_blocks = item_factors.shape[1] // side
    share = side // n_cols
    own_users = users // n_cols
    capacity = max(2, (tile_total + row_devs - 1) // row_devs)
    direct = row_devs == 8 and 2 * width == side
    vmem = pl.BlockSpec(memory_space=pltpu.VMEM)
    smem = pl.BlockSpec(memory_space=pltpu.SMEM)
    anywhere = pl.BlockSpec(memory_space=pl.ANY)
    params = pltpu.CompilerParams(vmem_limit_bytes=LIMIT)

    def call(kernel, out_shape, in_specs, name, scratch=(), flops=0):
        return pl.pallas_call(
            kernel,
            out_shape=out_shape,
            in_specs=in_specs,
            out_specs=jax.tree.map(lambda _: vmem, out_shape),
            scratch_shapes=scratch,
            compiler_params=params,
            cost_estimate=pl.CostEstimate(
                flops=flops, bytes_accessed=0, transcendentals=0
            ),
            name=name,
        )

    info = jnp.stack([tile_count[0], column, row])
    span = item_factors.shape[1] // n_cols
    sent = call(
        functools.partial(prepare_kernel, n_cols, side),
        [jax.ShapeDtypeStruct((col_width, 2 * own_users + span), bf16)] * n_cols,
        [smem, anywhere, anywhere],
        "prepare",
        [
            pltpu.VMEM(user_factors.shape, f32),
            pltpu.VMEM((n_cols, col_width, own_users), f32),
            pltpu.SemaphoreType.DMA((n_cols + 1,)),
        ],
        10**9,
    )(
        info,
        pltpu.with_memory_space_constraint(user_factors, pltpu.HBM),
        pltpu.with_memory_space_constraint(item_factors, pltpu.HBM),
    )
    shared = swap(sent)

    order = jnp.arange(tile_total, dtype=jnp.int32)
    live = (order < tile_count[0]).astype(jnp.int32)
    tile_item = after(tile_item, sent[0])
    holder = tile_item // item_blocks
    local_block = tile_item % item_blocks
    earlier = (
        (holder[None, :] == holder[:, None])
        & (order[None, :] < order[:, None])
        & (live[None, :] > 0)
    )
    rank = jnp.sum(earlier.astype(jnp.int32), axis=1)
    slot_ids = jnp.minimum(holder * capacity + rank, row_devs * capacity - 1)
    slot_range = jnp.arange(row_devs * capacity, dtype=jnp.int32)
    hits = ((slot_ids[None, :] == slot_range[:, None]) & (live[None, :] > 0)).astype(jnp.int32)
    requests = (jnp.sum(hits * (local_block + 1)[None, :], axis=1) - 1).reshape(row_devs, capacity)
    wanted = lax.all_to_all(requests, "rows", split_axis=0, concat_axis=0, tiled=True)
    block = holder
    if direct:
        step = holder ^ row
        block = step
        for j, spot in ((2, 3), (3, 2), (5, 6), (6, 5)):
            block = jnp.where(step == j, spot, block)
    places = block * capacity + jnp.minimum(rank, capacity - 1)
    places = jnp.where(live > 0, places, places[0])
    tile_users = jnp.where(live > 0, tile_user, tile_user[0])

    picked = call(
        functools.partial(pick_kernel, direct),
        [jax.ShapeDtypeStruct((capacity, col_width, side), bf16)] * row_devs
        if direct
        else [jax.ShapeDtypeStruct((row_devs * capacity, col_width, side), bf16)],
        [smem, smem, vmem],
        "pick",
        flops=10**9,
    )(after(info, *shared), wanted, item_factors)

    def join(*arrays):
        return jnp.concatenate(arrays, axis=0)

    def gather(*arrays):
        rows = sum(array.shape[0] for array in arrays)
        return call(
            join_kernel,
            [jax.ShapeDtypeStruct((rows, *arrays[0].shape[1:]), bf16)],
            [anywhere] * len(arrays),
            "join",
            [pltpu.SemaphoreType.DMA((len(arrays),))],
            2 * 10**10,
        )(*arrays)[0]

    def add(gram, *arrived):
        return call(add_kernel, [square, packed], [vmem] * (1 + len(arrived)), "add")(
            gram, *arrived
        )

    got = {0: picked[0]}
    if direct:
        for j in (1, 3, 4, 6, 2):
            got[j] = flip(picked[j], "rows", j)
        across = flip(got[0], "cols", 2)
        near = after(gather(got[1], got[3]), across)
        for j in (5, 7):
            got[j] = flip(after(picked[j], got[4], got[6], near), "rows", j)

    square = jax.ShapeDtypeStruct((width, width), f32)
    extra = width // col_width
    packed = jax.ShapeDtypeStruct((extra, col_width, 2 * width), bf16)
    gram, carried, start = call(
        functools.partial(gram_kernel, own_users),
        [square, packed, jax.ShapeDtypeStruct((width, own_users), f32)],
        [smem] + [anywhere] * n_cols,
        "gram",
        [
            pltpu.VMEM((width, 2 * own_users), bf16),
            pltpu.VMEM((width, span), bf16),
            pltpu.SemaphoreType.DMA((2 * n_cols,)),
        ],
        10**9,
    )(after(info, near if direct else picked[0]), *shared)
    strengths = jax.ShapeDtypeStruct((tile_total, share, side), bf16)

    def slice_mask(ready):
        return call(
            mask_kernel,
            [strengths],
            [smem, anywhere],
            "mask",
            [pltpu.SemaphoreType.DMA],
            10**9,
        )(after(info, ready), pltpu.with_memory_space_constraint(tile_mask, pltpu.HBM))[0]

    if direct:
        slots = (3 * capacity, 3 * capacity, 2 * capacity)
        early = join(got[0], near, across, flip(near, "cols", 2))
        pieces = [early, flip(early, "cols", 1)]

        own = after(gather(got[2], got[4], got[6], carried), early)
        mask = slice_mask(own)
        arrived = flip(own, "cols", 2)
        gram, carried = add(gram, arrived)
        own = join(own[: 3 * capacity], arrived[: 3 * capacity], carried)
        arrived = flip(after(own, mask), "cols", 1)
        gram, carried = add(gram, arrived)
        pieces += [own, arrived]

        own = gather(got[5], got[7])
        own = join(own, flip(own, "cols", 2))
        gram, carried = add(gram, *[flip(carried, "rows", j) for j in (1, 2, 3)])
        pieces += [own, flip(after(own, carried), "cols", 1)]
        arrived = flip(carried, "rows", 4)
    else:
        slots = (row_devs * capacity,)
        mask = slice_mask(gram)
        gram = add_all(gram)
        own = lax.all_to_all(picked[0], "rows", split_axis=0, concat_axis=0, tiled=True)
        own = join(own, flip(own, "cols", 2))
        pieces = [own, flip(own, "cols", 1)]

    vector = jax.ShapeDtypeStruct((own_users, width), f32)
    held = jax.ShapeDtypeStruct((row_devs * capacity, width, side), bf16)
    work = [
        pltpu.VMEM((user_blocks, share, 2 * width), bf16),
        pltpu.VMEM((user_blocks, share, width), f32),
        pltpu.VMEM((2, UNROLL, 2 * share, side), bf16),
    ]
    lists = (places, tile_users, info)
    part, y = call(
        functools.partial(start_kernel, n_cols, slots),
        [vector, held],
        [smem] * 3 + [vmem] * 2 + [anywhere] * len(pieces),
        "start",
        work + [pltpu.SemaphoreType.DMA((n_cols * len(slots),))],
        8 * 10**9,
    )(*lists, start, mask, *pieces)
    if direct:
        gram, _ = add(gram, after(arrived, part))
    pair = jax.ShapeDtypeStruct((n_cols, 2 * col_width, own_users), f32)
    pair_sent, field, first = call(
        first_kernel,
        [pair, vector, vector],
        [smem] * 3 + [vmem] * 5,
        "first",
        work,
        8 * 10**9,
    )(*lists, start, part, gram, y, mask)
    second_sent, dots = call(
        second_kernel,
        [
            jax.ShapeDtypeStruct((n_cols, col_width, own_users), f32),
            jax.ShapeDtypeStruct((devices, 128), f32),
        ],
        [smem] * 3 + [vmem] * 5,
        "second",
        work,
        8 * 10**9,
    )(*lists, field, first, gram, y, mask)

    turned = swap(pair_sent)
    dots = after(dots, *turned)
    turned += swap(second_sent)
    dots = lax.all_to_all(dots, ("rows", "cols"), split_axis=0, concat_axis=0, tiled=True)
    result = jax.ShapeDtypeStruct((col_width, users), f32)
    return tuple(
        call(
            functools.partial(finish_kernel, share),
            [result, result],
            [smem] + [vmem] * (2 + 2 * n_cols),
            "finish",
            [pltpu.VMEM((n_cols, col_width, own_users), f32)] * 3,
            10**9,
        )(info, dots, user_factors, *turned)
    )


def solution(mesh):
    return jax.shard_map(
        on_device,
        mesh=mesh,
        in_specs=(
            P("cols", "rows"),
            P("cols", "rows"),
            P("rows"),
            P("rows"),
            P("rows"),
            P("rows", None, None),
        ),
        out_specs=(P("cols", "rows"), P("cols", "rows")),
        check_vma=False,
    )
```

```python
import functools

import jax
import jax.numpy as jnp
from jax import lax
from jax.experimental import pallas as pl
from jax.experimental.pallas import tpu as pltpu
from jax.sharding import PartitionSpec as P

ridge = 0.5
confidence = 40.0
UNROLL = 8
LIMIT = 24 * 1024 * 1024
f32 = jnp.float32
bf16 = jnp.bfloat16


def matmul(left, right):
    return jnp.dot(left, right, preferred_element_type=f32)


def split(value):
    high = value.astype(bf16)
    low = (value - high.astype(f32)).astype(bf16)
    return high, low


def prepare_kernel(n_cols, side, info_ref, x_hbm, items_hbm, *refs):
    sent, (x_ref, x_pieces, sems) = refs[:n_cols], refs[n_cols:]
    column = info_ref[1]
    share = side // n_cols
    blocks = x_ref.shape[1] // side
    own_users = blocks * share
    span = sent[0].shape[1] - 2 * own_users
    copies = [
        pltpu.make_async_copy(
            items_hbm.at[:, pl.ds(pl.multiple_of((column ^ m) * span, span), span)],
            sent[m].at[:, pl.ds(2 * own_users, span)],
            sems.at[m],
        )
        for m in range(n_cols)
    ]
    fetch = pltpu.make_async_copy(x_hbm, x_ref, sems.at[n_cols])
    fetch.start()
    for copy in copies:
        copy.start()
    fetch.wait()
    for m in range(n_cols):
        x_pieces[m] = jnp.concatenate(
            [x_ref[:, b * side + m * share : b * side + (m + 1) * share] for b in range(blocks)],
            axis=1,
        )
    for m in range(n_cols):
        high, low = split(x_pieces[column ^ m])
        sent[m][:, :own_users] = high
        sent[m][:, own_users : 2 * own_users] = low
    for copy in copies:
        copy.wait()


def mask_kernel(info_ref, mask_hbm, mask, sem):
    tiles, share, side = mask.shape
    copy = pltpu.make_async_copy(
        mask_hbm.at[:, pl.ds(pl.multiple_of(info_ref[1] * share, share), share), :], mask, sem
    )
    copy.start()
    copy.wait()

    def clear(t, carry):
        mask[t] = jnp.zeros((share, side), bf16)
        return carry

    lax.fori_loop(info_ref[0], tiles, clear, 0)


def pick_kernel(direct, info_ref, wanted_ref, items_ref, *out_refs):
    capacity = wanted_ref.shape[1]
    side = out_refs[0].shape[2]
    for o, out_ref in enumerate(out_refs):
        for i in range(out_ref.shape[0] // capacity):
            dest = info_ref[2] ^ o if direct else i
            for r in range(capacity):
                block = jnp.maximum(wanted_ref[dest, r], 0)
                start = pl.multiple_of(block * side, side)
                out_ref[i * capacity + r] = items_ref[:, pl.ds(start, side)]


def pack(ref, gram):
    high, low = split(gram)
    both = jnp.concatenate([high, low], axis=1)
    for k in range(ref.shape[0]):
        ref[k] = both[k * ref.shape[1] : (k + 1) * ref.shape[1]]


def unpack(blocks):
    both = jnp.concatenate([blocks[k] for k in range(blocks.shape[0])], axis=0).astype(f32)
    width = both.shape[1] // 2
    return both[:, :width] + both[:, width:]


def gram_kernel(own_users, info_ref, *refs):
    column = info_ref[1]
    pieces = refs[:-6]
    out_ref, pack_ref, start_ref, starts, items, sems = refs[-6:]
    width = pieces[0].shape[0]
    span = items.shape[1]
    copies = []
    for m, piece in enumerate(pieces):
        place = pl.ds(pl.multiple_of((column ^ m) * width, width), width)
        for source, target in (
            (piece.at[:, pl.ds(0, 2 * own_users)], starts.at[place, :]),
            (piece.at[:, pl.ds(2 * own_users, span)], items.at[place, :]),
        ):
            copies.append(pltpu.make_async_copy(source, target, sems.at[len(copies)]))
            copies[-1].start()
    for copy in copies:
        copy.wait()
    both = starts[...].astype(f32)
    start_ref[...] = both[:, :own_users] + both[:, own_users:]
    gram = lax.dot_general(
        items[...], items[...], (((1,), (1,)), ((), ())), preferred_element_type=f32
    )
    out_ref[...] = gram
    pack(pack_ref, gram)


def add_kernel(gram_ref, *refs):
    out_ref, pack_ref = refs[-2:]
    extra = pack_ref.shape[0]
    total = gram_ref[...]
    for arrived_ref in refs[:-2]:
        total = total + unpack(arrived_ref[arrived_ref.shape[0] - extra :])
    out_ref[...] = total
    pack(pack_ref, total)


def join_kernel(*refs):
    sources, out_ref, sems = refs[:-2], refs[-2], refs[-1]
    copies = []
    base = 0
    for source in sources:
        rows = source.shape[0]
        copies.append(
            pltpu.make_async_copy(source, out_ref.at[pl.ds(base, rows)], sems.at[len(copies)])
        )
        copies[-1].start()
        base += rows
    for copy in copies:
        copy.wait()


def load(p_hl, vector):
    blocks, share, both = p_hl.shape
    width = both // 2
    high, low = split(vector)
    p_hl[:, :, :width] = high.reshape(blocks, share, width)
    p_hl[:, :, width:] = low.reshape(blocks, share, width)


def dense(p_hl, gram_ref, vector):
    blocks, share, both = p_hl.shape
    width = both // 2
    high, low = split(gram_ref[...])
    table = jnp.concatenate(
        [
            jnp.concatenate([high, low], axis=1),
            jnp.concatenate([high, jnp.zeros_like(low)], axis=1),
        ],
        axis=0,
    )
    product = matmul(p_hl[...].reshape(blocks * share, both), table)
    return product[:, :width] + product[:, width:] + ridge * vector


def sparse(starting, slot_ref, user_ref, y, turned, mask, p_hl, acc, held):
    tiles, share, side = mask.shape
    groups = tiles // UNROLL
    acc[...] = jnp.zeros_like(acc)

    def score(group):
        for j in range(UNROLL):
            t = group * UNROLL + j
            tile = y[slot_ref[t]]
            scores = matmul(p_hl[user_ref[t]], jnp.concatenate([tile, tile], axis=0))
            if starting:
                scores = (1.0 + confidence) - confidence * scores
            high, low = split(mask[t].astype(f32) * scores)
            held[group % 2, j, :share] = high
            held[group % 2, j, share:] = low

    def collect(group):
        terms = []
        for j in range(UNROLL):
            t = group * UNROLL + j
            term = matmul(held[group % 2, j], turned[slot_ref[t]])
            terms.append(term[:share] + term[share:])
        return terms

    def add(group, terms):
        for j, term in enumerate(terms):
            acc[user_ref[group * UNROLL + j]] += term

    score(0)

    def step(group, carry):
        terms = collect(group - 1)
        score(group)
        add(group - 1, terms)
        return carry

    lax.fori_loop(1, groups, step, 0)
    add(groups - 1, collect(groups - 1))


def put(column, ref, vector, part=0):
    n_cols, rows, _ = ref.shape
    turned = vector.T
    width = turned.shape[0] // n_cols
    for m in range(n_cols):
        ref[column ^ m, part * width : (part + 1) * width] = turned[m * width : (m + 1) * width]


def start_kernel(n_cols, slots, slot_ref, user_ref, info_ref, x_ref, mask, *refs):
    pieces = refs[: 2 * len(slots)]
    part_ref, y, turned, p_hl, acc, held, sems = refs[2 * len(slots) :]
    piece_width = y.shape[1] // n_cols
    column = info_ref[1]
    copies = []
    base = 0
    for k, count in enumerate(slots):
        for m in range(n_cols):
            place = pl.multiple_of((column ^ m) * piece_width, piece_width)
            source = pieces[2 * k + m % 2].at[pl.ds(m // 2 * count, count)]
            copies.append(
                pltpu.make_async_copy(
                    source,
                    y.at[pl.ds(base, count), pl.ds(place, piece_width), :],
                    sems.at[len(copies)],
                )
            )
        base += count
    for copy in copies:
        copy.start()
    load(p_hl, x_ref[...].T)
    for copy in copies:
        copy.wait()
    def turn(s, carry):
        turned[s] = y[s].T
        return carry

    lax.fori_loop(0, y.shape[0], turn, 0, unroll=8)
    sparse(True, slot_ref, user_ref, y, turned, mask, p_hl, acc, held)
    part_ref[...] = acc[...].reshape(part_ref.shape)


def first_kernel(
    slot_ref, user_ref, info_ref, x_ref, part_ref, gram_ref, y, turned, mask,
    sent_ref, field_ref, first_ref, p_hl, acc, held,
):
    start = x_ref[...].T
    load(p_hl, start)
    field = part_ref[...] - dense(p_hl, gram_ref, start)
    field_ref[...] = field
    put(info_ref[1], sent_ref, field)
    load(p_hl, field)
    sparse(False, slot_ref, user_ref, y, turned, mask, p_hl, acc, held)
    first = confidence * acc[...].reshape(field.shape) + dense(p_hl, gram_ref, field)
    first_ref[...] = first
    put(info_ref[1], sent_ref, first, 1)


def second_kernel(
    slot_ref, user_ref, info_ref, field_ref, first_ref, gram_ref, y, turned, mask, sent_ref, dots_ref, p_hl, acc, held
):
    field = field_ref[...]
    first = first_ref[...]
    load(p_hl, first)
    sparse(False, slot_ref, user_ref, y, turned, mask, p_hl, acc, held)
    second = confidence * acc[...].reshape(field.shape) + dense(p_hl, gram_ref, first)
    put(info_ref[1], sent_ref, second)

    def total(left, right):
        return jnp.sum(left * right)

    aa, ab, bb = total(field, field), total(field, first), total(first, first)
    guess = jnp.where(bb > 0.0, ab / jnp.where(bb > 0.0, bb, 1.0), 0.0)
    near = field - guess * first
    near_image = first - guess * second
    values = (
        aa,
        ab,
        bb,
        guess,
        total(near, near),
        total(near, first),
        total(near, near_image),
        total(near, second) + total(first, near_image),
        total(first, second),
    )
    lane = lax.broadcasted_iota(jnp.int32, dots_ref.shape, 1)
    dots = jnp.zeros(dots_ref.shape, f32)
    for j, value in enumerate(values):
        dots = jnp.where(lane == j, value, dots)
    dots_ref[...] = dots


def finish_kernel(share, info_ref, dots_ref, x_ref, *refs):
    n_cols = (len(refs) - 5) // 2
    x_out, r_out, field_ref, first_ref, second_ref = refs[2 * n_cols :]
    width = field_ref.shape[1]
    for m in range(n_cols):
        place = info_ref[1] ^ m
        field_ref[place] = refs[m][:width]
        first_ref[place] = refs[m][width:]
        second_ref[place] = refs[n_cols + m][...]
    dots = dots_ref[...]

    def column(j):
        return dots[:, j : j + 1]

    def total(value):
        return jnp.sum(value, axis=0, keepdims=True)

    rr0 = total(column(0))
    ab = total(column(1))
    alpha0 = rr0 / ab
    delta = alpha0 - column(3)
    rr1 = total(column(4) - 2.0 * delta * column(5) + delta * delta * column(2))
    curved = total(column(6) - delta * column(7) + delta * delta * column(8))
    crossed = total(column(5) - delta * column(2))
    beta = rr1 / rr0
    alpha1 = rr1 / (curved + 2.0 * beta * crossed + beta * beta * ab)
    along = alpha0 + alpha1 * (1.0 + beta)
    across = alpha1 * alpha0
    blocks = x_ref.shape[1] // (share * n_cols)
    for b in range(blocks):

        def gather(ref):
            return jnp.concatenate(
                [ref[m, :, b * share : (b + 1) * share] for m in range(n_cols)], axis=1
            )

        field, first, second = gather(field_ref), gather(first_ref), gather(second_ref)
        here = slice(b * share * n_cols, (b + 1) * share * n_cols)
        x_out[:, here] = x_ref[:, here] + along * field - across * first
        r_out[:, here] = field - along * first + across * second


def flip(value, axis, bit):
    size = lax.axis_size(axis)
    return lax.ppermute(value, axis, [(i, i ^ bit) for i in range(size)])


def swap(sent):
    return [sent[0]] + [flip(sent[m], "cols", m) for m in range(1, len(sent))]


def after(value, *others):
    return lax.optimization_barrier((value, *others))[0]


def add_all(value):
    for axis in ("cols", "rows"):
        bit = 1
        while bit < lax.axis_size(axis):
            value = value + flip(value, axis, bit)
            bit *= 2
    return value


def on_device(user_factors, item_factors, tile_user, tile_item, tile_count, tile_mask):
    side = tile_mask.shape[1]
    col_width = user_factors.shape[0]
    column = lax.axis_index("cols").astype(jnp.int32)
    row = lax.axis_index("rows").astype(jnp.int32)
    row_devs = lax.axis_size("rows")
    n_cols = lax.axis_size("cols")
    devices = row_devs * n_cols
    width = col_width * n_cols
    tile_total = tile_user.shape[0]
    users = user_factors.shape[1]
    user_blocks = users // side
    item_blocks = item_factors.shape[1] // side
    share = side // n_cols
    own_users = users // n_cols
    capacity = max(2, (tile_total + row_devs - 1) // row_devs)
    direct = row_devs == 8 and 2 * width == side
    vmem = pl.BlockSpec(memory_space=pltpu.VMEM)
    smem = pl.BlockSpec(memory_space=pltpu.SMEM)
    anywhere = pl.BlockSpec(memory_space=pl.ANY)
    params = pltpu.CompilerParams(vmem_limit_bytes=LIMIT)

    def call(kernel, out_shape, in_specs, name, scratch=(), flops=0):
        return pl.pallas_call(
            kernel,
            out_shape=out_shape,
            in_specs=in_specs,
            out_specs=jax.tree.map(lambda _: vmem, out_shape),
            scratch_shapes=scratch,
            compiler_params=params,
            cost_estimate=pl.CostEstimate(
                flops=flops, bytes_accessed=0, transcendentals=0
            ),
            name=name,
        )

    info = jnp.stack([tile_count[0], column, row])
    span = item_factors.shape[1] // n_cols
    sent = call(
        functools.partial(prepare_kernel, n_cols, side),
        [jax.ShapeDtypeStruct((col_width, 2 * own_users + span), bf16)] * n_cols,
        [smem, anywhere, anywhere],
        "prepare",
        [
            pltpu.VMEM(user_factors.shape, f32),
            pltpu.VMEM((n_cols, col_width, own_users), f32),
            pltpu.SemaphoreType.DMA((n_cols + 1,)),
        ],
        10**9,
    )(
        info,
        pltpu.with_memory_space_constraint(user_factors, pltpu.HBM),
        pltpu.with_memory_space_constraint(item_factors, pltpu.HBM),
    )
    shared = swap(sent)

    order = jnp.arange(tile_total, dtype=jnp.int32)
    live = (order < tile_count[0]).astype(jnp.int32)
    tile_item = after(tile_item, sent[0])
    holder = tile_item // item_blocks
    local_block = tile_item % item_blocks
    earlier = (
        (holder[None, :] == holder[:, None])
        & (order[None, :] < order[:, None])
        & (live[None, :] > 0)
    )
    rank = jnp.sum(earlier.astype(jnp.int32), axis=1)
    slot_ids = jnp.minimum(holder * capacity + rank, row_devs * capacity - 1)
    slot_range = jnp.arange(row_devs * capacity, dtype=jnp.int32)
    hits = ((slot_ids[None, :] == slot_range[:, None]) & (live[None, :] > 0)).astype(jnp.int32)
    requests = (jnp.sum(hits * (local_block + 1)[None, :], axis=1) - 1).reshape(row_devs, capacity)
    wanted = lax.all_to_all(requests, "rows", split_axis=0, concat_axis=0, tiled=True)
    block = holder
    if direct:
        step = holder ^ row
        block = step
        for j, spot in ((2, 3), (3, 2), (5, 6), (6, 5)):
            block = jnp.where(step == j, spot, block)
    places = block * capacity + jnp.minimum(rank, capacity - 1)
    places = jnp.where(live > 0, places, places[0])
    tile_users = jnp.where(live > 0, tile_user, tile_user[0])

    picked = call(
        functools.partial(pick_kernel, direct),
        [jax.ShapeDtypeStruct((capacity, col_width, side), bf16)] * row_devs
        if direct
        else [jax.ShapeDtypeStruct((row_devs * capacity, col_width, side), bf16)],
        [smem, smem, vmem],
        "pick",
        flops=10**9,
    )(after(info, *shared), wanted, item_factors)

    def join(*arrays):
        return jnp.concatenate(arrays, axis=0)

    def gather(*arrays):
        rows = sum(array.shape[0] for array in arrays)
        return call(
            join_kernel,
            [jax.ShapeDtypeStruct((rows, *arrays[0].shape[1:]), bf16)],
            [anywhere] * len(arrays),
            "join",
            [pltpu.SemaphoreType.DMA((len(arrays),))],
            2 * 10**10,
        )(*arrays)[0]

    def add(gram, *arrived):
        return call(add_kernel, [square, packed], [vmem] * (1 + len(arrived)), "add")(
            gram, *arrived
        )

    got = {0: picked[0]}
    if direct:
        for j in (1, 3, 4, 6, 2):
            got[j] = flip(picked[j], "rows", j)
        across = flip(got[0], "cols", 2)
        near = after(gather(got[1], got[3]), across)
        for j in (5, 7):
            got[j] = flip(after(picked[j], got[4], got[6], near), "rows", j)

    square = jax.ShapeDtypeStruct((width, width), f32)
    extra = width // col_width
    packed = jax.ShapeDtypeStruct((extra, col_width, 2 * width), bf16)
    gram, carried, start = call(
        functools.partial(gram_kernel, own_users),
        [square, packed, jax.ShapeDtypeStruct((width, own_users), f32)],
        [smem] + [anywhere] * n_cols,
        "gram",
        [
            pltpu.VMEM((width, 2 * own_users), bf16),
            pltpu.VMEM((width, span), bf16),
            pltpu.SemaphoreType.DMA((2 * n_cols,)),
        ],
        10**9,
    )(after(info, near if direct else picked[0]), *shared)
    strengths = jax.ShapeDtypeStruct((tile_total, share, side), bf16)

    def slice_mask(ready):
        return call(
            mask_kernel,
            [strengths],
            [smem, anywhere],
            "mask",
            [pltpu.SemaphoreType.DMA],
            10**9,
        )(after(info, ready), pltpu.with_memory_space_constraint(tile_mask, pltpu.HBM))[0]

    if direct:
        slots = (3 * capacity, 3 * capacity, 2 * capacity)
        early = join(got[0], near, across, flip(near, "cols", 2))
        pieces = [early, flip(early, "cols", 1)]

        own = after(gather(got[2], got[4], got[6], carried), early)
        mask = slice_mask(own)
        arrived = flip(own, "cols", 2)
        gram, carried = add(gram, arrived)
        own = join(own[: 3 * capacity], arrived[: 3 * capacity], carried)
        arrived = flip(after(own, mask), "cols", 1)
        gram, carried = add(gram, arrived)
        pieces += [own, arrived]

        own = gather(got[5], got[7])
        own = join(own, flip(own, "cols", 2))
        gram, carried = add(gram, *[flip(carried, "rows", j) for j in (1, 2, 3)])
        pieces += [own, flip(after(own, carried), "cols", 1)]
        arrived = flip(carried, "rows", 4)
    else:
        slots = (row_devs * capacity,)
        mask = slice_mask(gram)
        gram = add_all(gram)
        own = lax.all_to_all(picked[0], "rows", split_axis=0, concat_axis=0, tiled=True)
        own = join(own, flip(own, "cols", 2))
        pieces = [own, flip(own, "cols", 1)]

    vector = jax.ShapeDtypeStruct((own_users, width), f32)
    held = jax.ShapeDtypeStruct((row_devs * capacity, width, side), bf16)
    work = [
        pltpu.VMEM((user_blocks, share, 2 * width), bf16),
        pltpu.VMEM((user_blocks, share, width), f32),
        pltpu.VMEM((2, UNROLL, 2 * share, side), bf16),
    ]
    lists = (places, tile_users, info)
    part, y, turned_y = call(
        functools.partial(start_kernel, n_cols, slots),
        [vector, held, jax.ShapeDtypeStruct((row_devs * capacity, side, width), bf16)],
        [smem] * 3 + [vmem] * 2 + [anywhere] * len(pieces),
        "start",
        work + [pltpu.SemaphoreType.DMA((n_cols * len(slots),))],
        8 * 10**9,
    )(*lists, start, mask, *pieces)
    if direct:
        gram, _ = add(gram, after(arrived, part))
    pair = jax.ShapeDtypeStruct((n_cols, 2 * col_width, own_users), f32)
    pair_sent, field, first = call(
        first_kernel,
        [pair, vector, vector],
        [smem] * 3 + [vmem] * 6,
        "first",
        work,
        8 * 10**9,
    )(*lists, start, part, gram, y, turned_y, mask)
    second_sent, dots = call(
        second_kernel,
        [
            jax.ShapeDtypeStruct((n_cols, col_width, own_users), f32),
            jax.ShapeDtypeStruct((devices, 128), f32),
        ],
        [smem] * 3 + [vmem] * 6,
        "second",
        work,
        8 * 10**9,
    )(*lists, field, first, gram, y, turned_y, mask)

    turned = swap(pair_sent)
    dots = after(dots, *turned)
    turned += swap(second_sent)
    dots = lax.all_to_all(dots, ("rows", "cols"), split_axis=0, concat_axis=0, tiled=True)
    result = jax.ShapeDtypeStruct((col_width, users), f32)
    return tuple(
        call(
            functools.partial(finish_kernel, share),
            [result, result],
            [smem] + [vmem] * (2 + 2 * n_cols),
            "finish",
            [pltpu.VMEM((n_cols, col_width, own_users), f32)] * 3,
            10**9,
        )(info, dots, user_factors, *turned)
    )


def solution(mesh):
    return jax.shard_map(
        on_device,
        mesh=mesh,
        in_specs=(
            P("cols", "rows"),
            P("cols", "rows"),
            P("rows"),
            P("rows"),
            P("rows"),
            P("rows", None, None),
        ),
        out_specs=(P("cols", "rows"), P("cols", "rows")),
        check_vma=False,
    )
```

```python
import functools

import jax
import jax.numpy as jnp
from jax import lax
from jax.experimental import pallas as pl
from jax.experimental.pallas import tpu as pltpu
from jax.sharding import PartitionSpec as P

ridge = 0.5
confidence = 40.0
UNROLL = 18
LIMIT = 24 * 1024 * 1024
f32 = jnp.float32
bf16 = jnp.bfloat16


def matmul(left, right):
    return jnp.dot(left, right, preferred_element_type=f32)


def split(value):
    high = value.astype(bf16)
    low = (value - high.astype(f32)).astype(bf16)
    return high, low


def prepare_kernel(n_cols, side, info_ref, x_hbm, items_hbm, *refs):
    sent, (x_ref, x_pieces, sems) = refs[:n_cols], refs[n_cols:]
    column = info_ref[1]
    share = side // n_cols
    blocks = x_ref.shape[1] // side
    own_users = blocks * share
    span = sent[0].shape[1] - 2 * own_users
    copies = [
        pltpu.make_async_copy(
            items_hbm.at[:, pl.ds(pl.multiple_of((column ^ m) * span, span), span)],
            sent[m].at[:, pl.ds(2 * own_users, span)],
            sems.at[m],
        )
        for m in range(n_cols)
    ]
    fetch = pltpu.make_async_copy(x_hbm, x_ref, sems.at[n_cols])
    fetch.start()
    for copy in copies:
        copy.start()
    fetch.wait()
    for m in range(n_cols):
        x_pieces[m] = jnp.concatenate(
            [x_ref[:, b * side + m * share : b * side + (m + 1) * share] for b in range(blocks)],
            axis=1,
        )
    for m in range(n_cols):
        high, low = split(x_pieces[column ^ m])
        sent[m][:, :own_users] = high
        sent[m][:, own_users : 2 * own_users] = low
    for copy in copies:
        copy.wait()


def mask_kernel(info_ref, mask_hbm, mask, sem):
    tiles, share, side = mask.shape
    copy = pltpu.make_async_copy(
        mask_hbm.at[:, pl.ds(pl.multiple_of(info_ref[1] * share, share), share), :], mask, sem
    )
    copy.start()
    copy.wait()

    def clear(t, carry):
        mask[t] = jnp.zeros((share, side), bf16)
        return carry

    lax.fori_loop(info_ref[0], tiles, clear, 0)


def pick_kernel(direct, info_ref, wanted_ref, items_ref, *out_refs):
    capacity = wanted_ref.shape[1]
    side = out_refs[0].shape[2]
    for o, out_ref in enumerate(out_refs):
        for i in range(out_ref.shape[0] // capacity):
            dest = info_ref[2] ^ o if direct else i
            for r in range(capacity):
                block = jnp.maximum(wanted_ref[dest, r], 0)
                start = pl.multiple_of(block * side, side)
                out_ref[i * capacity + r] = items_ref[:, pl.ds(start, side)]


def pack(ref, gram):
    high, low = split(gram)
    both = jnp.concatenate([high, low], axis=1)
    for k in range(ref.shape[0]):
        ref[k] = both[k * ref.shape[1] : (k + 1) * ref.shape[1]]


def unpack(blocks):
    both = jnp.concatenate([blocks[k] for k in range(blocks.shape[0])], axis=0).astype(f32)
    width = both.shape[1] // 2
    return both[:, :width] + both[:, width:]


def gram_kernel(own_users, info_ref, *refs):
    column = info_ref[1]
    pieces = refs[:-6]
    out_ref, pack_ref, start_ref, starts, items, sems = refs[-6:]
    width = pieces[0].shape[0]
    span = items.shape[1]
    copies = []
    for m, piece in enumerate(pieces):
        place = pl.ds(pl.multiple_of((column ^ m) * width, width), width)
        for source, target in (
            (piece.at[:, pl.ds(0, 2 * own_users)], starts.at[place, :]),
            (piece.at[:, pl.ds(2 * own_users, span)], items.at[place, :]),
        ):
            copies.append(pltpu.make_async_copy(source, target, sems.at[len(copies)]))
            copies[-1].start()
    for copy in copies:
        copy.wait()
    both = starts[...].astype(f32)
    start_ref[...] = both[:, :own_users] + both[:, own_users:]
    gram = lax.dot_general(
        items[...], items[...], (((1,), (1,)), ((), ())), preferred_element_type=f32
    )
    out_ref[...] = gram
    pack(pack_ref, gram)


def add_kernel(gram_ref, *refs):
    out_ref, pack_ref = refs[-2:]
    extra = pack_ref.shape[0]
    total = gram_ref[...]
    for arrived_ref in refs[:-2]:
        total = total + unpack(arrived_ref[arrived_ref.shape[0] - extra :])
    out_ref[...] = total
    pack(pack_ref, total)


def join_kernel(*refs):
    sources, out_ref, sems = refs[:-2], refs[-2], refs[-1]
    copies = []
    base = 0
    for source in sources:
        rows = source.shape[0]
        copies.append(
            pltpu.make_async_copy(source, out_ref.at[pl.ds(base, rows)], sems.at[len(copies)])
        )
        copies[-1].start()
        base += rows
    for copy in copies:
        copy.wait()


def load(p_hl, vector):
    blocks, share, both = p_hl.shape
    width = both // 2
    high, low = split(vector)
    p_hl[:, :, :width] = high.reshape(blocks, share, width)
    p_hl[:, :, width:] = low.reshape(blocks, share, width)


def dense(p_hl, gram_ref, vector):
    blocks, share, both = p_hl.shape
    width = both // 2
    high, low = split(gram_ref[...])
    table = jnp.concatenate(
        [
            jnp.concatenate([high, low], axis=1),
            jnp.concatenate([high, jnp.zeros_like(low)], axis=1),
        ],
        axis=0,
    )
    product = matmul(p_hl[...].reshape(blocks * share, both), table)
    return product[:, :width] + product[:, width:] + ridge * vector


def sparse(starting, slot_ref, user_ref, y, mask, p_hl, acc, held):
    tiles, share, side = mask.shape
    groups = tiles // UNROLL
    acc[...] = jnp.zeros_like(acc)

    def score(group):
        for j in range(UNROLL):
            t = group * UNROLL + j
            tile = y[slot_ref[t]]
            scores = matmul(p_hl[user_ref[t]], jnp.concatenate([tile, tile], axis=0))
            if starting:
                scores = (1.0 + confidence) - confidence * scores
            high, low = split(mask[t].astype(f32) * scores)
            held[group % 2, j, :share] = high
            held[group % 2, j, share:] = low

    def collect(group):
        terms = []
        for j in range(UNROLL):
            t = group * UNROLL + j
            term = lax.dot_general(
                held[group % 2, j],
                y[slot_ref[t]],
                (((1,), (1,)), ((), ())),
                preferred_element_type=f32,
            )
            terms.append(term[:share] + term[share:])
        return terms

    def add(group, terms):
        for j, term in enumerate(terms):
            acc[user_ref[group * UNROLL + j]] += term

    score(0)

    def step(group, carry):
        terms = collect(group - 1)
        score(group)
        add(group - 1, terms)
        return carry

    lax.fori_loop(1, groups, step, 0)
    add(groups - 1, collect(groups - 1))


def put(column, ref, vector, part=0):
    n_cols, rows, _ = ref.shape
    turned = vector.T
    width = turned.shape[0] // n_cols
    for m in range(n_cols):
        ref[column ^ m, part * width : (part + 1) * width] = turned[m * width : (m + 1) * width]


def start_kernel(n_cols, slots, slot_ref, user_ref, info_ref, x_ref, mask, *refs):
    pieces = refs[: 2 * len(slots)]
    part_ref, y, p_hl, acc, held, sems = refs[2 * len(slots) :]
    piece_width = y.shape[1] // n_cols
    column = info_ref[1]
    copies = []
    base = 0
    for k, count in enumerate(slots):
        for m in range(n_cols):
            place = pl.multiple_of((column ^ m) * piece_width, piece_width)
            source = pieces[2 * k + m % 2].at[pl.ds(m // 2 * count, count)]
            copies.append(
                pltpu.make_async_copy(
                    source,
                    y.at[pl.ds(base, count), pl.ds(place, piece_width), :],
                    sems.at[len(copies)],
                )
            )
        base += count
    for copy in copies:
        copy.start()
    load(p_hl, x_ref[...].T)
    for copy in copies:
        copy.wait()
    sparse(True, slot_ref, user_ref, y, mask, p_hl, acc, held)
    part_ref[...] = acc[...].reshape(part_ref.shape)


def first_kernel(
    slot_ref, user_ref, info_ref, x_ref, part_ref, gram_ref, y, mask, *refs
):
    sent_ref, field_ref, first_ref, gram_out, p_hl, acc, held = refs[-7:]
    gram = gram_ref[...]
    for arrived_ref in refs[:-7]:
        gram = gram + unpack(arrived_ref)
    gram_out[...] = gram
    start = x_ref[...].T
    load(p_hl, start)
    field = part_ref[...] - dense(p_hl, gram_out, start)
    field_ref[...] = field
    put(info_ref[1], sent_ref, field)
    load(p_hl, field)
    sparse(False, slot_ref, user_ref, y, mask, p_hl, acc, held)
    first = confidence * acc[...].reshape(field.shape) + dense(p_hl, gram_out, field)
    first_ref[...] = first
    put(info_ref[1], sent_ref, first, 1)


def second_kernel(
    slot_ref, user_ref, info_ref, field_ref, first_ref, gram_ref, y, mask, sent_ref, dots_ref, p_hl, acc, held
):
    field = field_ref[...]
    first = first_ref[...]
    load(p_hl, first)
    sparse(False, slot_ref, user_ref, y, mask, p_hl, acc, held)
    second = confidence * acc[...].reshape(field.shape) + dense(p_hl, gram_ref, first)
    put(info_ref[1], sent_ref, second)

    def total(left, right):
        return jnp.sum(left * right)

    aa, ab, bb = total(field, field), total(field, first), total(first, first)
    guess = jnp.where(bb > 0.0, ab / jnp.where(bb > 0.0, bb, 1.0), 0.0)
    near = field - guess * first
    near_image = first - guess * second
    values = (
        aa,
        ab,
        bb,
        guess,
        total(near, near),
        total(near, first),
        total(near, near_image),
        total(near, second) + total(first, near_image),
        total(first, second),
    )
    lane = lax.broadcasted_iota(jnp.int32, dots_ref.shape, 1)
    dots = jnp.zeros(dots_ref.shape, f32)
    for j, value in enumerate(values):
        dots = jnp.where(lane == j, value, dots)
    dots_ref[...] = dots


def finish_kernel(share, info_ref, dots_ref, x_ref, *refs):
    n_cols = (len(refs) - 5) // 2
    x_out, r_out, field_ref, first_ref, second_ref = refs[2 * n_cols :]
    width = field_ref.shape[1]
    for m in range(n_cols):
        place = info_ref[1] ^ m
        field_ref[place] = refs[m][:width]
        first_ref[place] = refs[m][width:]
        second_ref[place] = refs[n_cols + m][...]
    dots = dots_ref[...]

    def column(j):
        return dots[:, j : j + 1]

    def total(value):
        return jnp.sum(value, axis=0, keepdims=True)

    rr0 = total(column(0))
    ab = total(column(1))
    alpha0 = rr0 / ab
    delta = alpha0 - column(3)
    rr1 = total(column(4) - 2.0 * delta * column(5) + delta * delta * column(2))
    curved = total(column(6) - delta * column(7) + delta * delta * column(8))
    crossed = total(column(5) - delta * column(2))
    beta = rr1 / rr0
    alpha1 = rr1 / (curved + 2.0 * beta * crossed + beta * beta * ab)
    along = alpha0 + alpha1 * (1.0 + beta)
    across = alpha1 * alpha0
    blocks = x_ref.shape[1] // (share * n_cols)
    for b in range(blocks):

        def gather(ref):
            return jnp.concatenate(
                [ref[m, :, b * share : (b + 1) * share] for m in range(n_cols)], axis=1
            )

        field, first, second = gather(field_ref), gather(first_ref), gather(second_ref)
        here = slice(b * share * n_cols, (b + 1) * share * n_cols)
        x_out[:, here] = x_ref[:, here] + along * field - across * first
        r_out[:, here] = field - along * first + across * second


def flip(value, axis, bit):
    size = lax.axis_size(axis)
    return lax.ppermute(value, axis, [(i, i ^ bit) for i in range(size)])


def swap(sent):
    return [sent[0]] + [flip(sent[m], "cols", m) for m in range(1, len(sent))]


def after(value, *others):
    return lax.optimization_barrier((value, *others))[0]


def add_all(value):
    for axis in ("cols", "rows"):
        bit = 1
        while bit < lax.axis_size(axis):
            value = value + flip(value, axis, bit)
            bit *= 2
    return value


def on_device(user_factors, item_factors, tile_user, tile_item, tile_count, tile_mask):
    side = tile_mask.shape[1]
    col_width = user_factors.shape[0]
    column = lax.axis_index("cols").astype(jnp.int32)
    row = lax.axis_index("rows").astype(jnp.int32)
    row_devs = lax.axis_size("rows")
    n_cols = lax.axis_size("cols")
    devices = row_devs * n_cols
    width = col_width * n_cols
    tile_total = tile_user.shape[0]
    users = user_factors.shape[1]
    user_blocks = users // side
    item_blocks = item_factors.shape[1] // side
    share = side // n_cols
    own_users = users // n_cols
    capacity = max(2, (tile_total + row_devs - 1) // row_devs)
    direct = row_devs == 8 and 2 * width == side
    vmem = pl.BlockSpec(memory_space=pltpu.VMEM)
    smem = pl.BlockSpec(memory_space=pltpu.SMEM)
    anywhere = pl.BlockSpec(memory_space=pl.ANY)
    params = pltpu.CompilerParams(vmem_limit_bytes=LIMIT)

    def call(kernel, out_shape, in_specs, name, scratch=(), flops=0):
        return pl.pallas_call(
            kernel,
            out_shape=out_shape,
            in_specs=in_specs,
            out_specs=jax.tree.map(lambda _: vmem, out_shape),
            scratch_shapes=scratch,
            compiler_params=params,
            cost_estimate=pl.CostEstimate(
                flops=flops, bytes_accessed=0, transcendentals=0
            ),
            name=name,
        )

    info = jnp.stack([tile_count[0], column, row])
    span = item_factors.shape[1] // n_cols
    sent = call(
        functools.partial(prepare_kernel, n_cols, side),
        [jax.ShapeDtypeStruct((col_width, 2 * own_users + span), bf16)] * n_cols,
        [smem, anywhere, anywhere],
        "prepare",
        [
            pltpu.VMEM(user_factors.shape, f32),
            pltpu.VMEM((n_cols, col_width, own_users), f32),
            pltpu.SemaphoreType.DMA((n_cols + 1,)),
        ],
        10**9,
    )(
        info,
        pltpu.with_memory_space_constraint(user_factors, pltpu.HBM),
        pltpu.with_memory_space_constraint(item_factors, pltpu.HBM),
    )
    shared = swap(sent)

    order = jnp.arange(tile_total, dtype=jnp.int32)
    live = (order < tile_count[0]).astype(jnp.int32)
    tile_item = after(tile_item, sent[0])
    holder = tile_item // item_blocks
    local_block = tile_item % item_blocks
    earlier = (
        (holder[None, :] == holder[:, None])
        & (order[None, :] < order[:, None])
        & (live[None, :] > 0)
    )
    rank = jnp.sum(earlier.astype(jnp.int32), axis=1)
    slot_ids = jnp.minimum(holder * capacity + rank, row_devs * capacity - 1)
    slot_range = jnp.arange(row_devs * capacity, dtype=jnp.int32)
    hits = ((slot_ids[None, :] == slot_range[:, None]) & (live[None, :] > 0)).astype(jnp.int32)
    requests = (jnp.sum(hits * (local_block + 1)[None, :], axis=1) - 1).reshape(row_devs, capacity)
    wanted = lax.all_to_all(requests, "rows", split_axis=0, concat_axis=0, tiled=True)
    block = holder
    if direct:
        step = holder ^ row
        block = step
        for j, spot in ((2, 3), (3, 2), (5, 6), (6, 5)):
            block = jnp.where(step == j, spot, block)
    places = block * capacity + jnp.minimum(rank, capacity - 1)
    places = jnp.where(live > 0, places, places[0])
    tile_users = jnp.where(live > 0, tile_user, tile_user[0])

    picked = call(
        functools.partial(pick_kernel, direct),
        [jax.ShapeDtypeStruct((capacity, col_width, side), bf16)] * row_devs
        if direct
        else [jax.ShapeDtypeStruct((row_devs * capacity, col_width, side), bf16)],
        [smem, smem, vmem],
        "pick",
        flops=10**9,
    )(after(info, *shared), wanted, item_factors)

    def join(*arrays):
        return jnp.concatenate(arrays, axis=0)

    def gather(*arrays):
        rows = sum(array.shape[0] for array in arrays)
        return call(
            join_kernel,
            [jax.ShapeDtypeStruct((rows, *arrays[0].shape[1:]), bf16)],
            [anywhere] * len(arrays),
            "join",
            [pltpu.SemaphoreType.DMA((len(arrays),))],
            2 * 10**10,
        )(*arrays)[0]

    def add(gram, *arrived):
        return call(add_kernel, [square, packed], [vmem] * (1 + len(arrived)), "add")(
            gram, *arrived
        )

    got = {0: picked[0]}
    if direct:
        for j in (1, 3, 4, 6, 2):
            got[j] = flip(picked[j], "rows", j)
        across = flip(got[0], "cols", 2)
        near = after(gather(got[1], got[3]), across)
        for j in (5, 7):
            got[j] = flip(after(picked[j], got[4], got[6], near), "rows", j)

    square = jax.ShapeDtypeStruct((width, width), f32)
    extra = width // col_width
    packed = jax.ShapeDtypeStruct((extra, col_width, 2 * width), bf16)
    gram, carried, start = call(
        functools.partial(gram_kernel, own_users),
        [square, packed, jax.ShapeDtypeStruct((width, own_users), f32)],
        [smem] + [anywhere] * n_cols,
        "gram",
        [
            pltpu.VMEM((width, 2 * own_users), bf16),
            pltpu.VMEM((width, span), bf16),
            pltpu.SemaphoreType.DMA((2 * n_cols,)),
        ],
        10**9,
    )(after(info, near if direct else picked[0]), *shared)
    strengths = jax.ShapeDtypeStruct((tile_total, share, side), bf16)

    def slice_mask(ready):
        return call(
            mask_kernel,
            [strengths],
            [smem, anywhere],
            "mask",
            [pltpu.SemaphoreType.DMA],
            10**9,
        )(after(info, ready), pltpu.with_memory_space_constraint(tile_mask, pltpu.HBM))[0]

    if direct:
        slots = (3 * capacity, 3 * capacity, 2 * capacity)
        early = join(got[0], near, across, flip(near, "cols", 2))
        pieces = [early, flip(early, "cols", 1)]

        own = after(gather(got[2], got[4], got[6], carried), early)
        mask = slice_mask(own)
        arrived = flip(own, "cols", 2)
        gram, carried = add(gram, arrived)
        own = join(own[: 3 * capacity], arrived[: 3 * capacity], carried)
        arrived = flip(after(own, mask), "cols", 1)
        gram, carried = add(gram, arrived)
        pieces += [own, arrived]

        own = gather(got[5], got[7])
        own = join(own, flip(own, "cols", 2))
        gram, carried = add(gram, *[flip(carried, "rows", j) for j in (1, 2, 3)])
        pieces += [own, flip(after(own, carried), "cols", 1)]
        arrived = flip(carried, "rows", 4)
    else:
        slots = (row_devs * capacity,)
        mask = slice_mask(gram)
        gram = add_all(gram)
        own = lax.all_to_all(picked[0], "rows", split_axis=0, concat_axis=0, tiled=True)
        own = join(own, flip(own, "cols", 2))
        pieces = [own, flip(own, "cols", 1)]

    vector = jax.ShapeDtypeStruct((own_users, width), f32)
    held = jax.ShapeDtypeStruct((row_devs * capacity, width, side), bf16)
    work = [
        pltpu.VMEM((user_blocks, share, 2 * width), bf16),
        pltpu.VMEM((user_blocks, share, width), f32),
        pltpu.VMEM((2, UNROLL, 2 * share, side), bf16),
    ]
    lists = (places, tile_users, info)
    part, y = call(
        functools.partial(start_kernel, n_cols, slots),
        [vector, held],
        [smem] * 3 + [vmem] * 2 + [anywhere] * len(pieces),
        "start",
        work + [pltpu.SemaphoreType.DMA((n_cols * len(slots),))],
        8 * 10**9,
    )(*lists, start, mask, *pieces)
    rest = [after(arrived, part)] if direct else []
    pair = jax.ShapeDtypeStruct((n_cols, 2 * col_width, own_users), f32)
    pair_sent, field, first, gram = call(
        first_kernel,
        [pair, vector, vector, square],
        [smem] * 3 + [vmem] * (5 + len(rest)),
        "first",
        work,
        8 * 10**9,
    )(*lists, start, part, gram, y, mask, *rest)
    second_sent, dots = call(
        second_kernel,
        [
            jax.ShapeDtypeStruct((n_cols, col_width, own_users), f32),
            jax.ShapeDtypeStruct((devices, 128), f32),
        ],
        [smem] * 3 + [vmem] * 5,
        "second",
        work,
        8 * 10**9,
    )(*lists, field, first, gram, y, mask)

    turned = swap(pair_sent)
    dots = after(dots, *turned)
    turned += swap(second_sent)
    dots = lax.all_to_all(dots, ("rows", "cols"), split_axis=0, concat_axis=0, tiled=True)
    result = jax.ShapeDtypeStruct((col_width, users), f32)
    return tuple(
        call(
            functools.partial(finish_kernel, share),
            [result, result],
            [smem] + [vmem] * (2 + 2 * n_cols),
            "finish",
            [pltpu.VMEM((n_cols, col_width, own_users), f32)] * 3,
            10**9,
        )(info, dots, user_factors, *turned)
    )


def solution(mesh):
    return jax.shard_map(
        on_device,
        mesh=mesh,
        in_specs=(
            P("cols", "rows"),
            P("cols", "rows"),
            P("rows"),
            P("rows"),
            P("rows"),
            P("rows", None, None),
        ),
        out_specs=(P("cols", "rows"), P("cols", "rows")),
        check_vma=False,
    )
```

```python
import functools

import jax
import jax.numpy as jnp
from jax import lax
from jax.experimental import pallas as pl
from jax.experimental.pallas import tpu as pltpu
from jax.sharding import PartitionSpec as P

ridge = 0.5
confidence = 40.0
UNROLL = 18
LIMIT = 24 * 1024 * 1024
f32 = jnp.float32
bf16 = jnp.bfloat16


def matmul(left, right):
    return jnp.dot(left, right, preferred_element_type=f32)


def split(value):
    high = value.astype(bf16)
    low = (value - high.astype(f32)).astype(bf16)
    return high, low


def prepare_kernel(n_cols, side, info_ref, x_hbm, items_hbm, *refs):
    sent, (x_ref, x_pieces, sems) = refs[:n_cols], refs[n_cols:]
    column = info_ref[1]
    share = side // n_cols
    blocks = x_ref.shape[1] // side
    own_users = blocks * share
    span = sent[0].shape[1] - 2 * own_users
    copies = [
        pltpu.make_async_copy(
            items_hbm.at[:, pl.ds(pl.multiple_of((column ^ m) * span, span), span)],
            sent[m].at[:, pl.ds(2 * own_users, span)],
            sems.at[m],
        )
        for m in range(n_cols)
    ]
    fetch = pltpu.make_async_copy(x_hbm, x_ref, sems.at[n_cols])
    fetch.start()
    for copy in copies:
        copy.start()
    fetch.wait()
    for m in range(n_cols):
        x_pieces[m] = jnp.concatenate(
            [x_ref[:, b * side + m * share : b * side + (m + 1) * share] for b in range(blocks)],
            axis=1,
        )
    for m in range(n_cols):
        high, low = split(x_pieces[column ^ m])
        sent[m][:, :own_users] = high
        sent[m][:, own_users : 2 * own_users] = low
    for copy in copies:
        copy.wait()


def mask_kernel(info_ref, mask_hbm, mask, sem):
    tiles, share, side = mask.shape
    copy = pltpu.make_async_copy(
        mask_hbm.at[:, pl.ds(pl.multiple_of(info_ref[1] * share, share), share), :], mask, sem
    )
    copy.start()
    copy.wait()

    def clear(t, carry):
        mask[t] = jnp.zeros((share, side), bf16)
        return carry

    lax.fori_loop(info_ref[0], tiles, clear, 0)


def pick_kernel(direct, info_ref, wanted_ref, items_ref, *out_refs):
    capacity = wanted_ref.shape[1]
    side = out_refs[0].shape[2]
    for o, out_ref in enumerate(out_refs):
        for i in range(out_ref.shape[0] // capacity):
            dest = info_ref[2] ^ o if direct else i
            for r in range(capacity):
                block = jnp.maximum(wanted_ref[dest, r], 0)
                start = pl.multiple_of(block * side, side)
                out_ref[i * capacity + r] = items_ref[:, pl.ds(start, side)]


def pack(ref, gram):
    high, low = split(gram)
    both = jnp.concatenate([high, low], axis=1)
    for k in range(ref.shape[0]):
        ref[k] = both[k * ref.shape[1] : (k + 1) * ref.shape[1]]


def unpack(blocks):
    both = jnp.concatenate([blocks[k] for k in range(blocks.shape[0])], axis=0).astype(f32)
    width = both.shape[1] // 2
    return both[:, :width] + both[:, width:]


def gram_kernel(own_users, info_ref, *refs):
    column = info_ref[1]
    pieces = refs[:-6]
    out_ref, pack_ref, start_ref, starts, items, sems = refs[-6:]
    width = pieces[0].shape[0]
    span = items.shape[1]
    copies = []
    for m, piece in enumerate(pieces):
        place = pl.ds(pl.multiple_of((column ^ m) * width, width), width)
        for source, target in (
            (piece.at[:, pl.ds(0, 2 * own_users)], starts.at[place, :]),
            (piece.at[:, pl.ds(2 * own_users, span)], items.at[place, :]),
        ):
            copies.append(pltpu.make_async_copy(source, target, sems.at[len(copies)]))
            copies[-1].start()
    for copy in copies:
        copy.wait()
    both = starts[...].astype(f32)
    start_ref[...] = both[:, :own_users] + both[:, own_users:]
    gram = lax.dot_general(
        items[...], items[...], (((1,), (1,)), ((), ())), preferred_element_type=f32
    )
    out_ref[...] = gram
    pack(pack_ref, gram)


def add_kernel(gram_ref, *refs):
    out_ref, pack_ref = refs[-2:]
    extra = pack_ref.shape[0]
    total = gram_ref[...]
    for arrived_ref in refs[:-2]:
        total = total + unpack(arrived_ref[arrived_ref.shape[0] - extra :])
    out_ref[...] = total
    pack(pack_ref, total)


def join_kernel(*refs):
    sources, out_ref, sems = refs[:-2], refs[-2], refs[-1]
    copies = []
    base = 0
    for source in sources:
        rows = source.shape[0]
        copies.append(
            pltpu.make_async_copy(source, out_ref.at[pl.ds(base, rows)], sems.at[len(copies)])
        )
        copies[-1].start()
        base += rows
    for copy in copies:
        copy.wait()


def load(p_hl, vector):
    blocks, share, both = p_hl.shape
    width = both // 2
    high, low = split(vector)
    p_hl[:, :, :width] = high.reshape(blocks, share, width)
    p_hl[:, :, width:] = low.reshape(blocks, share, width)


def dense(p_hl, gram_ref, vector):
    blocks, share, both = p_hl.shape
    width = both // 2
    high, low = split(gram_ref[...])
    table = jnp.concatenate(
        [
            jnp.concatenate([high, low], axis=1),
            jnp.concatenate([high, jnp.zeros_like(low)], axis=1),
        ],
        axis=0,
    )
    product = matmul(p_hl[...].reshape(blocks * share, both), table)
    return product[:, :width] + product[:, width:] + ridge * vector


def sparse(starting, slot_ref, user_ref, y, mask, p_hl, acc, held):
    tiles, share, side = mask.shape
    groups = tiles // UNROLL
    acc[...] = jnp.zeros_like(acc)

    def score(group):
        for j in range(UNROLL):
            t = group * UNROLL + j
            tile = y[slot_ref[t]]
            scores = matmul(p_hl[user_ref[t]], jnp.concatenate([tile, tile], axis=0))
            if starting:
                scores = (1.0 + confidence) - confidence * scores
            high, low = split(mask[t].astype(f32) * scores)
            held[group % 2, j, :share] = high
            held[group % 2, j, share:] = low

    def collect(group):
        terms = []
        for j in range(UNROLL):
            t = group * UNROLL + j
            term = lax.dot_general(
                held[group % 2, j],
                y[slot_ref[t]],
                (((1,), (1,)), ((), ())),
                preferred_element_type=f32,
            )
            terms.append(term[:share] + term[share:])
        return terms

    def add(group, terms):
        for j, term in enumerate(terms):
            acc[user_ref[group * UNROLL + j]] += term

    score(0)

    def step(group, carry):
        terms = collect(group - 1)
        score(group)
        add(group - 1, terms)
        return carry

    lax.fori_loop(1, groups, step, 0)
    add(groups - 1, collect(groups - 1))


def put(column, ref, vector, part=0):
    n_cols, rows, _ = ref.shape
    turned = vector.T
    width = turned.shape[0] // n_cols
    for m in range(n_cols):
        ref[column ^ m, part * width : (part + 1) * width] = turned[m * width : (m + 1) * width]


def start_kernel(n_cols, slots, slot_ref, user_ref, info_ref, x_ref, mask, *refs):
    pieces = refs[: 2 * len(slots)]
    part_ref, y, p_hl, acc, held, sems = refs[2 * len(slots) :]
    piece_width = y.shape[1] // n_cols
    column = info_ref[1]
    copies = []
    base = 0
    for k, count in enumerate(slots):
        for m in range(n_cols):
            place = pl.multiple_of((column ^ m) * piece_width, piece_width)
            source = pieces[2 * k + m % 2].at[pl.ds(m // 2 * count, count)]
            copies.append(
                pltpu.make_async_copy(
                    source,
                    y.at[pl.ds(base, count), pl.ds(place, piece_width), :],
                    sems.at[len(copies)],
                )
            )
        base += count
    for copy in copies:
        copy.start()
    load(p_hl, x_ref[...].T)
    for copy in copies:
        copy.wait()
    sparse(True, slot_ref, user_ref, y, mask, p_hl, acc, held)
    part_ref[...] = acc[...].reshape(part_ref.shape)


def first_kernel(
    slot_ref, user_ref, info_ref, x_ref, part_ref, gram_ref, y, mask, *refs
):
    field_ref, first_ref, gram_out, p_hl, acc, held = refs[-6:]
    gram = gram_ref[...]
    for arrived_ref in refs[:-6]:
        gram = gram + unpack(arrived_ref)
    gram_out[...] = gram
    start = x_ref[...].T
    load(p_hl, start)
    field = part_ref[...] - dense(p_hl, gram_out, start)
    field_ref[...] = field
    load(p_hl, field)
    sparse(False, slot_ref, user_ref, y, mask, p_hl, acc, held)
    first = confidence * acc[...].reshape(field.shape) + dense(p_hl, gram_out, field)
    first_ref[...] = first


def second_kernel(
    slot_ref, user_ref, info_ref, field_ref, first_ref, gram_ref, y, mask, sent_ref, dots_ref, p_hl, acc, held
):
    field = field_ref[...]
    first = first_ref[...]
    load(p_hl, first)
    sparse(False, slot_ref, user_ref, y, mask, p_hl, acc, held)
    second = confidence * acc[...].reshape(field.shape) + dense(p_hl, gram_ref, first)
    for part, vector in enumerate((field, first, second)):
        put(info_ref[1], sent_ref, vector, part)

    def total(left, right):
        return jnp.sum(left * right)

    aa, ab, bb = total(field, field), total(field, first), total(first, first)
    guess = jnp.where(bb > 0.0, ab / jnp.where(bb > 0.0, bb, 1.0), 0.0)
    near = field - guess * first
    near_image = first - guess * second
    values = (
        aa,
        ab,
        bb,
        guess,
        total(near, near),
        total(near, first),
        total(near, near_image),
        total(near, second) + total(first, near_image),
        total(first, second),
    )
    lane = lax.broadcasted_iota(jnp.int32, dots_ref.shape, 1)
    dots = jnp.zeros(dots_ref.shape, f32)
    for j, value in enumerate(values):
        dots = jnp.where(lane == j, value, dots)
    dots_ref[...] = dots


def finish_kernel(share, info_ref, dots_ref, x_ref, *refs):
    n_cols = len(refs) - 5
    x_out, r_out, field_ref, first_ref, second_ref = refs[n_cols:]
    width = field_ref.shape[1]
    for m in range(n_cols):
        place = info_ref[1] ^ m
        for part, ref in enumerate((field_ref, first_ref, second_ref)):
            ref[place] = refs[m][part * width : (part + 1) * width]
    dots = dots_ref[...]

    def column(j):
        return dots[:, j : j + 1]

    def total(value):
        return jnp.sum(value, axis=0, keepdims=True)

    rr0 = total(column(0))
    ab = total(column(1))
    alpha0 = rr0 / ab
    delta = alpha0 - column(3)
    rr1 = total(column(4) - 2.0 * delta * column(5) + delta * delta * column(2))
    curved = total(column(6) - delta * column(7) + delta * delta * column(8))
    crossed = total(column(5) - delta * column(2))
    beta = rr1 / rr0
    alpha1 = rr1 / (curved + 2.0 * beta * crossed + beta * beta * ab)
    along = alpha0 + alpha1 * (1.0 + beta)
    across = alpha1 * alpha0
    blocks = x_ref.shape[1] // (share * n_cols)
    for b in range(blocks):

        def gather(ref):
            return jnp.concatenate(
                [ref[m, :, b * share : (b + 1) * share] for m in range(n_cols)], axis=1
            )

        field, first, second = gather(field_ref), gather(first_ref), gather(second_ref)
        here = slice(b * share * n_cols, (b + 1) * share * n_cols)
        x_out[:, here] = x_ref[:, here] + along * field - across * first
        r_out[:, here] = field - along * first + across * second


def flip(value, axis, bit):
    size = lax.axis_size(axis)
    return lax.ppermute(value, axis, [(i, i ^ bit) for i in range(size)])


def swap(sent):
    return [sent[0]] + [flip(sent[m], "cols", m) for m in range(1, len(sent))]


def after(value, *others):
    return lax.optimization_barrier((value, *others))[0]


def add_all(value):
    for axis in ("cols", "rows"):
        bit = 1
        while bit < lax.axis_size(axis):
            value = value + flip(value, axis, bit)
            bit *= 2
    return value


def on_device(user_factors, item_factors, tile_user, tile_item, tile_count, tile_mask):
    side = tile_mask.shape[1]
    col_width = user_factors.shape[0]
    column = lax.axis_index("cols").astype(jnp.int32)
    row = lax.axis_index("rows").astype(jnp.int32)
    row_devs = lax.axis_size("rows")
    n_cols = lax.axis_size("cols")
    devices = row_devs * n_cols
    width = col_width * n_cols
    tile_total = tile_user.shape[0]
    users = user_factors.shape[1]
    user_blocks = users // side
    item_blocks = item_factors.shape[1] // side
    share = side // n_cols
    own_users = users // n_cols
    capacity = max(2, (tile_total + row_devs - 1) // row_devs)
    direct = row_devs == 8 and 2 * width == side
    vmem = pl.BlockSpec(memory_space=pltpu.VMEM)
    smem = pl.BlockSpec(memory_space=pltpu.SMEM)
    anywhere = pl.BlockSpec(memory_space=pl.ANY)
    params = pltpu.CompilerParams(vmem_limit_bytes=LIMIT)

    def call(kernel, out_shape, in_specs, name, scratch=(), flops=0):
        return pl.pallas_call(
            kernel,
            out_shape=out_shape,
            in_specs=in_specs,
            out_specs=jax.tree.map(lambda _: vmem, out_shape),
            scratch_shapes=scratch,
            compiler_params=params,
            cost_estimate=pl.CostEstimate(
                flops=flops, bytes_accessed=0, transcendentals=0
            ),
            name=name,
        )

    info = jnp.stack([tile_count[0], column, row])
    span = item_factors.shape[1] // n_cols
    sent = call(
        functools.partial(prepare_kernel, n_cols, side),
        [jax.ShapeDtypeStruct((col_width, 2 * own_users + span), bf16)] * n_cols,
        [smem, anywhere, anywhere],
        "prepare",
        [
            pltpu.VMEM(user_factors.shape, f32),
            pltpu.VMEM((n_cols, col_width, own_users), f32),
            pltpu.SemaphoreType.DMA((n_cols + 1,)),
        ],
        10**9,
    )(
        info,
        pltpu.with_memory_space_constraint(user_factors, pltpu.HBM),
        pltpu.with_memory_space_constraint(item_factors, pltpu.HBM),
    )
    shared = swap(sent)

    order = jnp.arange(tile_total, dtype=jnp.int32)
    live = (order < tile_count[0]).astype(jnp.int32)
    tile_item = after(tile_item, sent[0])
    holder = tile_item // item_blocks
    local_block = tile_item % item_blocks
    earlier = (
        (holder[None, :] == holder[:, None])
        & (order[None, :] < order[:, None])
        & (live[None, :] > 0)
    )
    rank = jnp.sum(earlier.astype(jnp.int32), axis=1)
    slot_ids = jnp.minimum(holder * capacity + rank, row_devs * capacity - 1)
    slot_range = jnp.arange(row_devs * capacity, dtype=jnp.int32)
    hits = ((slot_ids[None, :] == slot_range[:, None]) & (live[None, :] > 0)).astype(jnp.int32)
    requests = (jnp.sum(hits * (local_block + 1)[None, :], axis=1) - 1).reshape(row_devs, capacity)
    wanted = lax.all_to_all(requests, "rows", split_axis=0, concat_axis=0, tiled=True)
    block = holder
    if direct:
        step = holder ^ row
        block = step
        for j, spot in ((2, 3), (3, 2), (5, 6), (6, 5)):
            block = jnp.where(step == j, spot, block)
    places = block * capacity + jnp.minimum(rank, capacity - 1)
    places = jnp.where(live > 0, places, places[0])
    tile_users = jnp.where(live > 0, tile_user, tile_user[0])

    picked = call(
        functools.partial(pick_kernel, direct),
        [jax.ShapeDtypeStruct((capacity, col_width, side), bf16)] * row_devs
        if direct
        else [jax.ShapeDtypeStruct((row_devs * capacity, col_width, side), bf16)],
        [smem, smem, vmem],
        "pick",
        flops=10**9,
    )(after(info, *shared), wanted, item_factors)

    def join(*arrays):
        return jnp.concatenate(arrays, axis=0)

    def gather(*arrays):
        rows = sum(array.shape[0] for array in arrays)
        return call(
            join_kernel,
            [jax.ShapeDtypeStruct((rows, *arrays[0].shape[1:]), bf16)],
            [anywhere] * len(arrays),
            "join",
            [pltpu.SemaphoreType.DMA((len(arrays),))],
            2 * 10**10,
        )(*arrays)[0]

    def add(gram, *arrived):
        return call(add_kernel, [square, packed], [vmem] * (1 + len(arrived)), "add")(
            gram, *arrived
        )

    got = {0: picked[0]}
    if direct:
        for j in (1, 3, 4, 6, 2):
            got[j] = flip(picked[j], "rows", j)
        across = flip(got[0], "cols", 2)
        near = after(gather(got[1], got[3]), across)
        for j in (5, 7):
            got[j] = flip(after(picked[j], got[4], got[6], near), "rows", j)

    square = jax.ShapeDtypeStruct((width, width), f32)
    extra = width // col_width
    packed = jax.ShapeDtypeStruct((extra, col_width, 2 * width), bf16)
    gram, carried, start = call(
        functools.partial(gram_kernel, own_users),
        [square, packed, jax.ShapeDtypeStruct((width, own_users), f32)],
        [smem] + [anywhere] * n_cols,
        "gram",
        [
            pltpu.VMEM((width, 2 * own_users), bf16),
            pltpu.VMEM((width, span), bf16),
            pltpu.SemaphoreType.DMA((2 * n_cols,)),
        ],
        10**9,
    )(after(info, near if direct else picked[0]), *shared)
    strengths = jax.ShapeDtypeStruct((tile_total, share, side), bf16)

    def slice_mask(ready):
        return call(
            mask_kernel,
            [strengths],
            [smem, anywhere],
            "mask",
            [pltpu.SemaphoreType.DMA],
            10**9,
        )(after(info, ready), pltpu.with_memory_space_constraint(tile_mask, pltpu.HBM))[0]

    if direct:
        slots = (3 * capacity, 3 * capacity, 2 * capacity)
        early = join(got[0], near, across, flip(near, "cols", 2))
        pieces = [early, flip(early, "cols", 1)]

        own = after(gather(got[2], got[4], got[6], carried), early)
        mask = slice_mask(own)
        arrived = flip(own, "cols", 2)
        gram, carried = add(gram, arrived)
        own = join(own[: 3 * capacity], arrived[: 3 * capacity], carried)
        arrived = flip(after(own, mask), "cols", 1)
        gram, carried = add(gram, arrived)
        pieces += [own, arrived]

        own = gather(got[5], got[7])
        own = join(own, flip(own, "cols", 2))
        gram, carried = add(gram, *[flip(carried, "rows", j) for j in (1, 2, 3)])
        pieces += [own, flip(after(own, carried), "cols", 1)]
        arrived = flip(carried, "rows", 4)
    else:
        slots = (row_devs * capacity,)
        mask = slice_mask(gram)
        gram = add_all(gram)
        own = lax.all_to_all(picked[0], "rows", split_axis=0, concat_axis=0, tiled=True)
        own = join(own, flip(own, "cols", 2))
        pieces = [own, flip(own, "cols", 1)]

    vector = jax.ShapeDtypeStruct((own_users, width), f32)
    held = jax.ShapeDtypeStruct((row_devs * capacity, width, side), bf16)
    work = [
        pltpu.VMEM((user_blocks, share, 2 * width), bf16),
        pltpu.VMEM((user_blocks, share, width), f32),
        pltpu.VMEM((2, UNROLL, 2 * share, side), bf16),
    ]
    lists = (places, tile_users, info)
    part, y = call(
        functools.partial(start_kernel, n_cols, slots),
        [vector, held],
        [smem] * 3 + [vmem] * 2 + [anywhere] * len(pieces),
        "start",
        work + [pltpu.SemaphoreType.DMA((n_cols * len(slots),))],
        8 * 10**9,
    )(*lists, start, mask, *pieces)
    rest = [after(arrived, part)] if direct else []
    field, first, gram = call(
        first_kernel,
        [vector, vector, square],
        [smem] * 3 + [vmem] * (5 + len(rest)),
        "first",
        work,
        8 * 10**9,
    )(*lists, start, part, gram, y, mask, *rest)
    sent, dots = call(
        second_kernel,
        [
            jax.ShapeDtypeStruct((n_cols, 3 * col_width, own_users), f32),
            jax.ShapeDtypeStruct((devices, 128), f32),
        ],
        [smem] * 3 + [vmem] * 5,
        "second",
        work,
        8 * 10**9,
    )(*lists, field, first, gram, y, mask)

    turned = swap(sent)
    dots = lax.all_to_all(dots, ("rows", "cols"), split_axis=0, concat_axis=0, tiled=True)
    result = jax.ShapeDtypeStruct((col_width, users), f32)
    return tuple(
        call(
            functools.partial(finish_kernel, share),
            [result, result],
            [smem] + [vmem] * (2 + n_cols),
            "finish",
            [pltpu.VMEM((n_cols, col_width, own_users), f32)] * 3,
            10**9,
        )(info, dots, user_factors, *turned)
    )


def solution(mesh):
    return jax.shard_map(
        on_device,
        mesh=mesh,
        in_specs=(
            P("cols", "rows"),
            P("cols", "rows"),
            P("rows"),
            P("rows"),
            P("rows"),
            P("rows", None, None),
        ),
        out_specs=(P("cols", "rows"), P("cols", "rows")),
        check_vma=False,
    )
```

```python
import functools

import jax
import jax.numpy as jnp
from jax import lax
from jax.experimental import pallas as pl
from jax.experimental.pallas import tpu as pltpu
from jax.sharding import PartitionSpec as P

ridge = 0.5
confidence = 40.0
UNROLL = 12
LIMIT = 24 * 1024 * 1024
f32 = jnp.float32
bf16 = jnp.bfloat16


def matmul(left, right):
    return jnp.dot(left, right, preferred_element_type=f32)


def split(value):
    high = value.astype(bf16)
    low = (value - high.astype(f32)).astype(bf16)
    return high, low


def prepare_kernel(n_cols, side, info_ref, x_hbm, items_hbm, *refs):
    sent, (x_ref, x_pieces, sems) = refs[:n_cols], refs[n_cols:]
    column = info_ref[1]
    share = side // n_cols
    blocks = x_ref.shape[1] // side
    own_users = blocks * share
    span = sent[0].shape[1] - 2 * own_users
    copies = [
        pltpu.make_async_copy(
            items_hbm.at[:, pl.ds(pl.multiple_of((column ^ m) * span, span), span)],
            sent[m].at[:, pl.ds(2 * own_users, span)],
            sems.at[m],
        )
        for m in range(n_cols)
    ]
    fetch = pltpu.make_async_copy(x_hbm, x_ref, sems.at[n_cols])
    fetch.start()
    for copy in copies:
        copy.start()
    fetch.wait()
    for m in range(n_cols):
        x_pieces[m] = jnp.concatenate(
            [x_ref[:, b * side + m * share : b * side + (m + 1) * share] for b in range(blocks)],
            axis=1,
        )
    for m in range(n_cols):
        high, low = split(x_pieces[column ^ m])
        sent[m][:, :own_users] = high
        sent[m][:, own_users : 2 * own_users] = low
    for copy in copies:
        copy.wait()


def mask_kernel(info_ref, mask_hbm, mask, sem):
    tiles, share, side = mask.shape
    copy = pltpu.make_async_copy(
        mask_hbm.at[:, pl.ds(pl.multiple_of(info_ref[1] * share, share), share), :], mask, sem
    )
    copy.start()
    copy.wait()

    def clear(t, carry):
        mask[t] = jnp.zeros((share, side), bf16)
        return carry

    lax.fori_loop(info_ref[0], tiles, clear, 0)


def pick_kernel(direct, info_ref, wanted_ref, items_ref, *out_refs):
    capacity = wanted_ref.shape[1]
    side = out_refs[0].shape[2]
    for o, out_ref in enumerate(out_refs):
        for i in range(out_ref.shape[0] // capacity):
            dest = info_ref[2] ^ o if direct else i
            for r in range(capacity):
                block = jnp.maximum(wanted_ref[dest, r], 0)
                start = pl.multiple_of(block * side, side)
                out_ref[i * capacity + r] = items_ref[:, pl.ds(start, side)]


def pack(ref, gram):
    high, low = split(gram)
    both = jnp.concatenate([high, low], axis=1)
    for k in range(ref.shape[0]):
        ref[k] = both[k * ref.shape[1] : (k + 1) * ref.shape[1]]


def unpack(blocks):
    both = jnp.concatenate([blocks[k] for k in range(blocks.shape[0])], axis=0).astype(f32)
    width = both.shape[1] // 2
    return both[:, :width] + both[:, width:]


def gram_kernel(own_users, info_ref, *refs):
    column = info_ref[1]
    pieces = refs[:-6]
    out_ref, pack_ref, start_ref, starts, items, sems = refs[-6:]
    width = pieces[0].shape[0]
    span = items.shape[1]
    copies = []
    for m, piece in enumerate(pieces):
        place = pl.ds(pl.multiple_of((column ^ m) * width, width), width)
        for source, target in (
            (piece.at[:, pl.ds(0, 2 * own_users)], starts.at[place, :]),
            (piece.at[:, pl.ds(2 * own_users, span)], items.at[place, :]),
        ):
            copies.append(pltpu.make_async_copy(source, target, sems.at[len(copies)]))
            copies[-1].start()
    for copy in copies:
        copy.wait()
    both = starts[...].astype(f32)
    start_ref[...] = both[:, :own_users] + both[:, own_users:]
    gram = lax.dot_general(
        items[...], items[...], (((1,), (1,)), ((), ())), preferred_element_type=f32
    )
    out_ref[...] = gram
    pack(pack_ref, gram)


def add_kernel(gram_ref, *refs):
    out_ref, pack_ref = refs[-2:]
    extra = pack_ref.shape[0]
    total = gram_ref[...]
    for arrived_ref in refs[:-2]:
        total = total + unpack(arrived_ref[arrived_ref.shape[0] - extra :])
    out_ref[...] = total
    pack(pack_ref, total)


def join_kernel(*refs):
    sources, out_ref, sems = refs[:-2], refs[-2], refs[-1]
    copies = []
    base = 0
    for source in sources:
        rows = source.shape[0]
        copies.append(
            pltpu.make_async_copy(source, out_ref.at[pl.ds(base, rows)], sems.at[len(copies)])
        )
        copies[-1].start()
        base += rows
    for copy in copies:
        copy.wait()


def load(p_hl, vector):
    blocks, share, both = p_hl.shape
    width = both // 2
    high, low = split(vector)
    p_hl[:, :, :width] = high.reshape(blocks, share, width)
    p_hl[:, :, width:] = low.reshape(blocks, share, width)


def dense(p_hl, gram_ref, vector):
    blocks, share, both = p_hl.shape
    width = both // 2
    high, low = split(gram_ref[...])
    table = jnp.concatenate(
        [
            jnp.concatenate([high, low], axis=1),
            jnp.concatenate([high, jnp.zeros_like(low)], axis=1),
        ],
        axis=0,
    )
    product = matmul(p_hl[...].reshape(blocks * share, both), table)
    return product[:, :width] + product[:, width:] + ridge * vector


def sparse(starting, slot_ref, user_ref, y, mask, p_hl, acc, held):
    tiles, share, side = mask.shape
    groups = tiles // UNROLL
    acc[...] = jnp.zeros_like(acc)

    def score(group):
        for j in range(UNROLL):
            t = group * UNROLL + j
            tile = y[slot_ref[t]]
            scores = matmul(p_hl[user_ref[t]], jnp.concatenate([tile, tile], axis=0))
            if starting:
                scores = (1.0 + confidence) - confidence * scores
            high, low = split(mask[t].astype(f32) * scores)
            held[group % 2, j, :share] = high
            held[group % 2, j, share:] = low

    def collect(group):
        terms = []
        for j in range(UNROLL):
            t = group * UNROLL + j
            term = lax.dot_general(
                held[group % 2, j],
                y[slot_ref[t]],
                (((1,), (1,)), ((), ())),
                preferred_element_type=f32,
            )
            terms.append(term[:share] + term[share:])
        return terms

    def add(group, terms):
        for j, term in enumerate(terms):
            acc[user_ref[group * UNROLL + j]] += term

    score(0)

    def step(group, carry):
        terms = collect(group - 1)
        score(group)
        add(group - 1, terms)
        return carry

    lax.fori_loop(1, groups, step, 0, unroll=True)
    add(groups - 1, collect(groups - 1))


def put(column, ref, vector, part=0):
    n_cols, rows, _ = ref.shape
    turned = vector.T
    width = turned.shape[0] // n_cols
    for m in range(n_cols):
        ref[column ^ m, part * width : (part + 1) * width] = turned[m * width : (m + 1) * width]


def start_kernel(n_cols, slots, slot_ref, user_ref, info_ref, x_ref, mask, *refs):
    pieces = refs[: 2 * len(slots)]
    part_ref, y, p_hl, acc, held, sems = refs[2 * len(slots) :]
    piece_width = y.shape[1] // n_cols
    column = info_ref[1]
    copies = []
    base = 0
    for k, count in enumerate(slots):
        for m in range(n_cols):
            place = pl.multiple_of((column ^ m) * piece_width, piece_width)
            source = pieces[2 * k + m % 2].at[pl.ds(m // 2 * count, count)]
            copies.append(
                pltpu.make_async_copy(
                    source,
                    y.at[pl.ds(base, count), pl.ds(place, piece_width), :],
                    sems.at[len(copies)],
                )
            )
        base += count
    for copy in copies:
        copy.start()
    load(p_hl, x_ref[...].T)
    for copy in copies:
        copy.wait()
    sparse(True, slot_ref, user_ref, y, mask, p_hl, acc, held)
    part_ref[...] = acc[...].reshape(part_ref.shape)


def iterate_kernel(
    slot_ref, user_ref, info_ref, x_ref, part_ref, gram_ref, y, mask, *refs
):
    sent_ref, dots_ref, p_hl, acc, held, gram, field_ref, first_ref = refs[-8:]
    gram[...] = gram_ref[...]
    for arrived_ref in refs[:-8]:
        gram[...] += unpack(arrived_ref)

    def image(vector):
        load(p_hl, vector)
        sparse(False, slot_ref, user_ref, y, mask, p_hl, acc, held)
        return confidence * acc[...].reshape(vector.shape) + dense(p_hl, gram, vector)

    start = x_ref[...].T
    load(p_hl, start)
    field_ref[...] = part_ref[...] - dense(p_hl, gram, start)
    first_ref[...] = image(field_ref[...])
    second = image(first_ref[...])
    field, first = field_ref[...], first_ref[...]
    for part, vector in enumerate((field, first, second)):
        put(info_ref[1], sent_ref, vector, part)

    def total(left, right):
        return jnp.sum(left * right)

    aa, ab, bb = total(field, field), total(field, first), total(first, first)
    guess = jnp.where(bb > 0.0, ab / jnp.where(bb > 0.0, bb, 1.0), 0.0)
    near = field - guess * first
    near_image = first - guess * second
    values = (
        aa,
        ab,
        bb,
        guess,
        total(near, near),
        total(near, first),
        total(near, near_image),
        total(near, second) + total(first, near_image),
        total(first, second),
    )
    lane = lax.broadcasted_iota(jnp.int32, dots_ref.shape, 1)
    dots = jnp.zeros(dots_ref.shape, f32)
    for j, value in enumerate(values):
        dots = jnp.where(lane == j, value, dots)
    dots_ref[...] = dots


def finish_kernel(share, info_ref, dots_ref, x_ref, *refs):
    n_cols = len(refs) - 5
    x_out, r_out, field_ref, first_ref, second_ref = refs[n_cols:]
    width = field_ref.shape[1]
    for m in range(n_cols):
        place = info_ref[1] ^ m
        for part, ref in enumerate((field_ref, first_ref, second_ref)):
            ref[place] = refs[m][part * width : (part + 1) * width]
    dots = dots_ref[...]

    def column(j):
        return dots[:, j : j + 1]

    def total(value):
        return jnp.sum(value, axis=0, keepdims=True)

    rr0 = total(column(0))
    ab = total(column(1))
    alpha0 = rr0 / ab
    delta = alpha0 - column(3)
    rr1 = total(column(4) - 2.0 * delta * column(5) + delta * delta * column(2))
    curved = total(column(6) - delta * column(7) + delta * delta * column(8))
    crossed = total(column(5) - delta * column(2))
    beta = rr1 / rr0
    alpha1 = rr1 / (curved + 2.0 * beta * crossed + beta * beta * ab)
    along = alpha0 + alpha1 * (1.0 + beta)
    across = alpha1 * alpha0
    blocks = x_ref.shape[1] // (share * n_cols)
    for b in range(blocks):

        def gather(ref):
            return jnp.concatenate(
                [ref[m, :, b * share : (b + 1) * share] for m in range(n_cols)], axis=1
            )

        field, first, second = gather(field_ref), gather(first_ref), gather(second_ref)
        here = slice(b * share * n_cols, (b + 1) * share * n_cols)
        x_out[:, here] = x_ref[:, here] + along * field - across * first
        r_out[:, here] = field - along * first + across * second


def flip(value, axis, bit):
    size = lax.axis_size(axis)
    return lax.ppermute(value, axis, [(i, i ^ bit) for i in range(size)])


def swap(sent):
    return [sent[0]] + [flip(sent[m], "cols", m) for m in range(1, len(sent))]


def after(value, *others):
    return lax.optimization_barrier((value, *others))[0]


def add_all(value):
    for axis in ("cols", "rows"):
        bit = 1
        while bit < lax.axis_size(axis):
            value = value + flip(value, axis, bit)
            bit *= 2
    return value


def on_device(user_factors, item_factors, tile_user, tile_item, tile_count, tile_mask):
    side = tile_mask.shape[1]
    col_width = user_factors.shape[0]
    column = lax.axis_index("cols").astype(jnp.int32)
    row = lax.axis_index("rows").astype(jnp.int32)
    row_devs = lax.axis_size("rows")
    n_cols = lax.axis_size("cols")
    devices = row_devs * n_cols
    width = col_width * n_cols
    tile_total = tile_user.shape[0]
    users = user_factors.shape[1]
    user_blocks = users // side
    item_blocks = item_factors.shape[1] // side
    share = side // n_cols
    own_users = users // n_cols
    capacity = max(2, (tile_total + row_devs - 1) // row_devs)
    direct = row_devs == 8 and 2 * width == side
    vmem = pl.BlockSpec(memory_space=pltpu.VMEM)
    smem = pl.BlockSpec(memory_space=pltpu.SMEM)
    anywhere = pl.BlockSpec(memory_space=pl.ANY)
    params = pltpu.CompilerParams(vmem_limit_bytes=LIMIT)

    def call(kernel, out_shape, in_specs, name, scratch=(), flops=0):
        return pl.pallas_call(
            kernel,
            out_shape=out_shape,
            in_specs=in_specs,
            out_specs=jax.tree.map(lambda _: vmem, out_shape),
            scratch_shapes=scratch,
            compiler_params=params,
            cost_estimate=pl.CostEstimate(
                flops=flops, bytes_accessed=0, transcendentals=0
            ),
            name=name,
        )

    info = jnp.stack([tile_count[0], column, row])
    span = item_factors.shape[1] // n_cols
    sent = call(
        functools.partial(prepare_kernel, n_cols, side),
        [jax.ShapeDtypeStruct((col_width, 2 * own_users + span), bf16)] * n_cols,
        [smem, anywhere, anywhere],
        "prepare",
        [
            pltpu.VMEM(user_factors.shape, f32),
            pltpu.VMEM((n_cols, col_width, own_users), f32),
            pltpu.SemaphoreType.DMA((n_cols + 1,)),
        ],
        10**9,
    )(
        info,
        pltpu.with_memory_space_constraint(user_factors, pltpu.HBM),
        pltpu.with_memory_space_constraint(item_factors, pltpu.HBM),
    )
    shared = swap(sent)

    order = jnp.arange(tile_total, dtype=jnp.int32)
    live = (order < tile_count[0]).astype(jnp.int32)
    tile_item = after(tile_item, sent[0])
    holder = tile_item // item_blocks
    local_block = tile_item % item_blocks
    earlier = (
        (holder[None, :] == holder[:, None])
        & (order[None, :] < order[:, None])
        & (live[None, :] > 0)
    )
    rank = jnp.sum(earlier.astype(jnp.int32), axis=1)
    slot_ids = jnp.minimum(holder * capacity + rank, row_devs * capacity - 1)
    slot_range = jnp.arange(row_devs * capacity, dtype=jnp.int32)
    hits = ((slot_ids[None, :] == slot_range[:, None]) & (live[None, :] > 0)).astype(jnp.int32)
    requests = (jnp.sum(hits * (local_block + 1)[None, :], axis=1) - 1).reshape(row_devs, capacity)
    wanted = lax.all_to_all(requests, "rows", split_axis=0, concat_axis=0, tiled=True)
    block = holder
    if direct:
        step = holder ^ row
        block = step
        for j, spot in ((2, 3), (3, 2), (5, 6), (6, 5)):
            block = jnp.where(step == j, spot, block)
    places = block * capacity + jnp.minimum(rank, capacity - 1)
    places = jnp.where(live > 0, places, places[0])
    tile_users = jnp.where(live > 0, tile_user, tile_user[0])

    picked = call(
        functools.partial(pick_kernel, direct),
        [jax.ShapeDtypeStruct((capacity, col_width, side), bf16)] * row_devs
        if direct
        else [jax.ShapeDtypeStruct((row_devs * capacity, col_width, side), bf16)],
        [smem, smem, vmem],
        "pick",
        flops=10**9,
    )(after(info, *shared), wanted, item_factors)

    def join(*arrays):
        return jnp.concatenate(arrays, axis=0)

    def gather(*arrays):
        rows = sum(array.shape[0] for array in arrays)
        return call(
            join_kernel,
            [jax.ShapeDtypeStruct((rows, *arrays[0].shape[1:]), bf16)],
            [anywhere] * len(arrays),
            "join",
            [pltpu.SemaphoreType.DMA((len(arrays),))],
            2 * 10**10,
        )(*arrays)[0]

    def add(gram, *arrived):
        return call(add_kernel, [square, packed], [vmem] * (1 + len(arrived)), "add")(
            gram, *arrived
        )

    got = {0: picked[0]}
    if direct:
        for j in (1, 3, 4, 6, 2):
            got[j] = flip(picked[j], "rows", j)
        across = flip(got[0], "cols", 2)
        near = after(gather(got[1], got[3]), across)
        for j in (5, 7):
            got[j] = flip(after(picked[j], got[4], got[6], near), "rows", j)

    square = jax.ShapeDtypeStruct((width, width), f32)
    extra = width // col_width
    packed = jax.ShapeDtypeStruct((extra, col_width, 2 * width), bf16)
    gram, carried, start = call(
        functools.partial(gram_kernel, own_users),
        [square, packed, jax.ShapeDtypeStruct((width, own_users), f32)],
        [smem] + [anywhere] * n_cols,
        "gram",
        [
            pltpu.VMEM((width, 2 * own_users), bf16),
            pltpu.VMEM((width, span), bf16),
            pltpu.SemaphoreType.DMA((2 * n_cols,)),
        ],
        10**9,
    )(after(info, near if direct else picked[0]), *shared)
    strengths = jax.ShapeDtypeStruct((tile_total, share, side), bf16)

    def slice_mask(ready):
        return call(
            mask_kernel,
            [strengths],
            [smem, anywhere],
            "mask",
            [pltpu.SemaphoreType.DMA],
            10**9,
        )(after(info, ready), pltpu.with_memory_space_constraint(tile_mask, pltpu.HBM))[0]

    if direct:
        slots = (3 * capacity, 3 * capacity, 2 * capacity)
        early = join(got[0], near, across, flip(near, "cols", 2))
        pieces = [early, flip(early, "cols", 1)]

        own = after(gather(got[2], got[4], got[6], carried), early)
        mask = slice_mask(own)
        arrived = flip(own, "cols", 2)
        gram, carried = add(gram, arrived)
        own = join(own[: 3 * capacity], arrived[: 3 * capacity], carried)
        arrived = flip(after(own, mask), "cols", 1)
        gram, carried = add(gram, arrived)
        pieces += [own, arrived]

        own = gather(got[5], got[7])
        own = join(own, flip(own, "cols", 2))
        gram, carried = add(gram, *[flip(carried, "rows", j) for j in (1, 2, 3)])
        pieces += [own, flip(after(own, carried), "cols", 1)]
        arrived = flip(carried, "rows", 4)
    else:
        slots = (row_devs * capacity,)
        mask = slice_mask(gram)
        gram = add_all(gram)
        own = lax.all_to_all(picked[0], "rows", split_axis=0, concat_axis=0, tiled=True)
        own = join(own, flip(own, "cols", 2))
        pieces = [own, flip(own, "cols", 1)]

    vector = jax.ShapeDtypeStruct((own_users, width), f32)
    held = jax.ShapeDtypeStruct((row_devs * capacity, width, side), bf16)
    work = [
        pltpu.VMEM((user_blocks, share, 2 * width), bf16),
        pltpu.VMEM((user_blocks, share, width), f32),
        pltpu.VMEM((2, UNROLL, 2 * share, side), bf16),
    ]
    lists = (places, tile_users, info)
    part, y = call(
        functools.partial(start_kernel, n_cols, slots),
        [vector, held],
        [smem] * 3 + [vmem] * 2 + [anywhere] * len(pieces),
        "start",
        work + [pltpu.SemaphoreType.DMA((n_cols * len(slots),))],
        8 * 10**9,
    )(*lists, start, mask, *pieces)
    rest = [after(arrived, part)] if direct else []
    sent, dots = call(
        iterate_kernel,
        [
            jax.ShapeDtypeStruct((n_cols, 3 * col_width, own_users), f32),
            jax.ShapeDtypeStruct((devices, 128), f32),
        ],
        [smem] * 3 + [vmem] * (5 + len(rest)),
        "iterate",
        work
        + [
            pltpu.VMEM((width, width), f32),
            pltpu.VMEM((own_users, width), f32),
            pltpu.VMEM((own_users, width), f32),
        ],
        16 * 10**9,
    )(*lists, start, part, gram, y, mask, *rest)

    turned = swap(sent)
    dots = lax.all_to_all(dots, ("rows", "cols"), split_axis=0, concat_axis=0, tiled=True)
    result = jax.ShapeDtypeStruct((col_width, users), f32)
    return tuple(
        call(
            functools.partial(finish_kernel, share),
            [result, result],
            [smem] + [vmem] * (2 + n_cols),
            "finish",
            [pltpu.VMEM((n_cols, col_width, own_users), f32)] * 3,
            10**9,
        )(info, dots, user_factors, *turned)
    )


def solution(mesh):
    return jax.shard_map(
        on_device,
        mesh=mesh,
        in_specs=(
            P("cols", "rows"),
            P("cols", "rows"),
            P("rows"),
            P("rows"),
            P("rows"),
            P("rows", None, None),
        ),
        out_specs=(P("cols", "rows"), P("cols", "rows")),
        check_vma=False,
    )
```

```python
import functools

import jax
import jax.numpy as jnp
from jax import lax
from jax.experimental import pallas as pl
from jax.experimental.pallas import tpu as pltpu
from jax.sharding import PartitionSpec as P

ridge = 0.5
confidence = 40.0
UNROLL = 8
LIMIT = 24 * 1024 * 1024
f32 = jnp.float32
bf16 = jnp.bfloat16


def matmul(left, right):
    return jnp.dot(left, right, preferred_element_type=f32)


def split(value):
    high = value.astype(bf16)
    low = (value - high.astype(f32)).astype(bf16)
    return high, low


def prepare_kernel(n_cols, side, info_ref, x_hbm, items_hbm, *refs):
    sent, (x_ref, x_pieces, sems) = refs[:n_cols], refs[n_cols:]
    column = info_ref[1]
    share = side // n_cols
    blocks = x_ref.shape[1] // side
    own_users = blocks * share
    span = sent[0].shape[1] - 2 * own_users
    copies = [
        pltpu.make_async_copy(
            items_hbm.at[:, pl.ds(pl.multiple_of((column ^ m) * span, span), span)],
            sent[m].at[:, pl.ds(2 * own_users, span)],
            sems.at[m],
        )
        for m in range(n_cols)
    ]
    fetch = pltpu.make_async_copy(x_hbm, x_ref, sems.at[n_cols])
    fetch.start()
    for copy in copies:
        copy.start()
    fetch.wait()
    for m in range(n_cols):
        x_pieces[m] = jnp.concatenate(
            [x_ref[:, b * side + m * share : b * side + (m + 1) * share] for b in range(blocks)],
            axis=1,
        )
    for m in range(n_cols):
        high, low = split(x_pieces[column ^ m])
        sent[m][:, :own_users] = high
        sent[m][:, own_users : 2 * own_users] = low
    for copy in copies:
        copy.wait()


def mask_kernel(info_ref, mask_hbm, mask, sem):
    tiles, share, side = mask.shape
    copy = pltpu.make_async_copy(
        mask_hbm.at[:, pl.ds(pl.multiple_of(info_ref[1] * share, share), share), :], mask, sem
    )
    copy.start()
    copy.wait()

    def clear(t, carry):
        mask[t] = jnp.zeros((share, side), bf16)
        return carry

    lax.fori_loop(info_ref[0], tiles, clear, 0)


def pick_kernel(direct, info_ref, wanted_ref, items_hbm, *refs):
    out_refs, (items_ref, sem) = refs[:-2], refs[-2:]
    copy = pltpu.make_async_copy(items_hbm, items_ref, sem)
    copy.start()
    copy.wait()
    capacity = wanted_ref.shape[1]
    side = out_refs[0].shape[2]
    for o, out_ref in enumerate(out_refs):
        for i in range(out_ref.shape[0] // capacity):
            dest = info_ref[2] ^ o if direct else i
            for r in range(capacity):
                block = jnp.maximum(wanted_ref[dest, r], 0)
                start = pl.multiple_of(block * side, side)
                out_ref[i * capacity + r] = items_ref[:, pl.ds(start, side)]


def pack(ref, gram):
    high, low = split(gram)
    both = jnp.concatenate([high, low], axis=1)
    for k in range(ref.shape[0]):
        ref[k] = both[k * ref.shape[1] : (k + 1) * ref.shape[1]]


def unpack(blocks):
    both = jnp.concatenate([blocks[k] for k in range(blocks.shape[0])], axis=0).astype(f32)
    width = both.shape[1] // 2
    return both[:, :width] + both[:, width:]


def gram_kernel(own_users, info_ref, *refs):
    column = info_ref[1]
    pieces = refs[:-6]
    out_ref, pack_ref, start_ref, starts, items, sems = refs[-6:]
    width = pieces[0].shape[0]
    span = items.shape[1]
    copies = []
    for m, piece in enumerate(pieces):
        place = pl.ds(pl.multiple_of((column ^ m) * width, width), width)
        for source, target in (
            (piece.at[:, pl.ds(0, 2 * own_users)], starts.at[place, :]),
            (piece.at[:, pl.ds(2 * own_users, span)], items.at[place, :]),
        ):
            copies.append(pltpu.make_async_copy(source, target, sems.at[len(copies)]))
            copies[-1].start()
    for copy in copies:
        copy.wait()
    both = starts[...].astype(f32)
    start_ref[...] = both[:, :own_users] + both[:, own_users:]
    gram = lax.dot_general(
        items[...], items[...], (((1,), (1,)), ((), ())), preferred_element_type=f32
    )
    out_ref[...] = gram
    pack(pack_ref, gram)


def add_kernel(gram_ref, *refs):
    out_ref, pack_ref = refs[-2:]
    extra = pack_ref.shape[0]
    total = gram_ref[...]
    for arrived_ref in refs[:-2]:
        total = total + unpack(arrived_ref[arrived_ref.shape[0] - extra :])
    out_ref[...] = total
    pack(pack_ref, total)


def join_kernel(*refs):
    sources, out_ref, sems = refs[:-2], refs[-2], refs[-1]
    copies = []
    base = 0
    for source in sources:
        rows = source.shape[0]
        copies.append(
            pltpu.make_async_copy(source, out_ref.at[pl.ds(base, rows)], sems.at[len(copies)])
        )
        copies[-1].start()
        base += rows
    for copy in copies:
        copy.wait()


def load(p_hl, vector):
    blocks, share, both = p_hl.shape
    width = both // 2
    high, low = split(vector)
    p_hl[:, :, :width] = high.reshape(blocks, share, width)
    p_hl[:, :, width:] = low.reshape(blocks, share, width)


def dense(p_hl, gram_ref, vector):
    blocks, share, both = p_hl.shape
    width = both // 2
    high, low = split(gram_ref[...])
    table = jnp.concatenate(
        [
            jnp.concatenate([high, low], axis=1),
            jnp.concatenate([high, jnp.zeros_like(low)], axis=1),
        ],
        axis=0,
    )
    product = matmul(p_hl[...].reshape(blocks * share, both), table)
    return product[:, :width] + product[:, width:] + ridge * vector


def sparse(starting, slot_ref, user_ref, y, mask, p_hl, acc, held):
    tiles, share, side = mask.shape
    groups = tiles // UNROLL
    acc[...] = jnp.zeros_like(acc)

    def score(group):
        for j in range(UNROLL):
            t = group * UNROLL + j
            tile = y[slot_ref[t]]
            scores = matmul(p_hl[user_ref[t]], jnp.concatenate([tile, tile], axis=0))
            if starting:
                scores = (1.0 + confidence) - confidence * scores
            high, low = split(mask[t].astype(f32) * scores)
            held[group % 2, j, :share] = high
            held[group % 2, j, share:] = low

    def collect(group):
        terms = []
        for j in range(UNROLL):
            t = group * UNROLL + j
            term = lax.dot_general(
                held[group % 2, j],
                y[slot_ref[t]],
                (((1,), (1,)), ((), ())),
                preferred_element_type=f32,
            )
            terms.append(term[:share] + term[share:])
        return terms

    def add(group, terms):
        for j, term in enumerate(terms):
            acc[user_ref[group * UNROLL + j]] += term

    score(0)

    def step(group, carry):
        terms = collect(group - 1)
        score(group)
        add(group - 1, terms)
        return carry

    lax.fori_loop(1, groups, step, 0, unroll=True)
    add(groups - 1, collect(groups - 1))


def put(column, ref, vector, part=0):
    n_cols, rows, _ = ref.shape
    turned = vector.T
    width = turned.shape[0] // n_cols
    for m in range(n_cols):
        ref[column ^ m, part * width : (part + 1) * width] = turned[m * width : (m + 1) * width]


def start_kernel(n_cols, slots, slot_ref, user_ref, info_ref, x_ref, mask, *refs):
    pieces = refs[: 2 * len(slots)]
    part_ref, y, p_hl, acc, held, sems = refs[2 * len(slots) :]
    piece_width = y.shape[1] // n_cols
    column = info_ref[1]
    copies = []
    base = 0
    for k, count in enumerate(slots):
        for m in range(n_cols):
            place = pl.multiple_of((column ^ m) * piece_width, piece_width)
            source = pieces[2 * k + m % 2].at[pl.ds(m // 2 * count, count)]
            copies.append(
                pltpu.make_async_copy(
                    source,
                    y.at[pl.ds(base, count), pl.ds(place, piece_width), :],
                    sems.at[len(copies)],
                )
            )
        base += count
    for copy in copies:
        copy.start()
    load(p_hl, x_ref[...].T)
    for copy in copies:
        copy.wait()
    sparse(True, slot_ref, user_ref, y, mask, p_hl, acc, held)
    part_ref[...] = acc[...].reshape(part_ref.shape)


def iterate_kernel(
    slot_ref, user_ref, info_ref, x_ref, part_ref, gram_ref, y, mask, *refs
):
    sent_ref, dots_ref, p_hl, acc, held, gram, field_ref, first_ref = refs[-8:]
    gram[...] = gram_ref[...]
    for arrived_ref in refs[:-8]:
        gram[...] += unpack(arrived_ref)

    def image(vector):
        load(p_hl, vector)
        sparse(False, slot_ref, user_ref, y, mask, p_hl, acc, held)
        return confidence * acc[...].reshape(vector.shape) + dense(p_hl, gram, vector)

    start = x_ref[...].T
    load(p_hl, start)
    field_ref[...] = part_ref[...] - dense(p_hl, gram, start)
    first_ref[...] = image(field_ref[...])
    second = image(first_ref[...])
    field, first = field_ref[...], first_ref[...]
    for part, vector in enumerate((field, first, second)):
        put(info_ref[1], sent_ref, vector, part)

    def total(left, right):
        return jnp.sum(left * right)

    aa, ab, bb = total(field, field), total(field, first), total(first, first)
    guess = jnp.where(bb > 0.0, ab / jnp.where(bb > 0.0, bb, 1.0), 0.0)
    near = field - guess * first
    near_image = first - guess * second
    values = (
        aa,
        ab,
        bb,
        guess,
        total(near, near),
        total(near, first),
        total(near, near_image),
        total(near, second) + total(first, near_image),
        total(first, second),
    )
    lane = lax.broadcasted_iota(jnp.int32, dots_ref.shape, 1)
    dots = jnp.zeros(dots_ref.shape, f32)
    for j, value in enumerate(values):
        dots = jnp.where(lane == j, value, dots)
    dots_ref[...] = dots


def finish_kernel(share, info_ref, dots_ref, x_ref, *refs):
    n_cols = len(refs) - 5
    x_out, r_out, field_ref, first_ref, second_ref = refs[n_cols:]
    width = field_ref.shape[1]
    for m in range(n_cols):
        place = info_ref[1] ^ m
        for part, ref in enumerate((field_ref, first_ref, second_ref)):
            ref[place] = refs[m][part * width : (part + 1) * width]
    dots = dots_ref[...]

    def column(j):
        return dots[:, j : j + 1]

    def total(value):
        return jnp.sum(value, axis=0, keepdims=True)

    rr0 = total(column(0))
    ab = total(column(1))
    alpha0 = rr0 / ab
    delta = alpha0 - column(3)
    rr1 = total(column(4) - 2.0 * delta * column(5) + delta * delta * column(2))
    curved = total(column(6) - delta * column(7) + delta * delta * column(8))
    crossed = total(column(5) - delta * column(2))
    beta = rr1 / rr0
    alpha1 = rr1 / (curved + 2.0 * beta * crossed + beta * beta * ab)
    along = alpha0 + alpha1 * (1.0 + beta)
    across = alpha1 * alpha0
    blocks = x_ref.shape[1] // (share * n_cols)
    for b in range(blocks):

        def gather(ref):
            return jnp.concatenate(
                [ref[m, :, b * share : (b + 1) * share] for m in range(n_cols)], axis=1
            )

        field, first, second = gather(field_ref), gather(first_ref), gather(second_ref)
        here = slice(b * share * n_cols, (b + 1) * share * n_cols)
        x_out[:, here] = x_ref[:, here] + along * field - across * first
        r_out[:, here] = field - along * first + across * second


def flip(value, axis, bit):
    size = lax.axis_size(axis)
    return lax.ppermute(value, axis, [(i, i ^ bit) for i in range(size)])


def swap(sent):
    return [sent[0]] + [flip(sent[m], "cols", m) for m in range(1, len(sent))]


def after(value, *others):
    return lax.optimization_barrier((value, *others))[0]


def add_all(value):
    for axis in ("cols", "rows"):
        bit = 1
        while bit < lax.axis_size(axis):
            value = value + flip(value, axis, bit)
            bit *= 2
    return value


def on_device(user_factors, item_factors, tile_user, tile_item, tile_count, tile_mask):
    side = tile_mask.shape[1]
    col_width = user_factors.shape[0]
    column = lax.axis_index("cols").astype(jnp.int32)
    row = lax.axis_index("rows").astype(jnp.int32)
    row_devs = lax.axis_size("rows")
    n_cols = lax.axis_size("cols")
    devices = row_devs * n_cols
    width = col_width * n_cols
    tile_total = tile_user.shape[0]
    users = user_factors.shape[1]
    user_blocks = users // side
    item_blocks = item_factors.shape[1] // side
    share = side // n_cols
    own_users = users // n_cols
    capacity = max(2, (tile_total + row_devs - 1) // row_devs)
    direct = row_devs == 8 and 2 * width == side
    vmem = pl.BlockSpec(memory_space=pltpu.VMEM)
    smem = pl.BlockSpec(memory_space=pltpu.SMEM)
    anywhere = pl.BlockSpec(memory_space=pl.ANY)
    params = pltpu.CompilerParams(vmem_limit_bytes=LIMIT)

    def call(kernel, out_shape, in_specs, name, scratch=(), flops=0):
        return pl.pallas_call(
            kernel,
            out_shape=out_shape,
            in_specs=in_specs,
            out_specs=jax.tree.map(lambda _: vmem, out_shape),
            scratch_shapes=scratch,
            compiler_params=params,
            cost_estimate=pl.CostEstimate(
                flops=flops, bytes_accessed=0, transcendentals=0
            ),
            name=name,
        )

    info = jnp.stack([tile_count[0], column, row])
    span = item_factors.shape[1] // n_cols
    sent = call(
        functools.partial(prepare_kernel, n_cols, side),
        [jax.ShapeDtypeStruct((col_width, 2 * own_users + span), bf16)] * n_cols,
        [smem, anywhere, anywhere],
        "prepare",
        [
            pltpu.VMEM(user_factors.shape, f32),
            pltpu.VMEM((n_cols, col_width, own_users), f32),
            pltpu.SemaphoreType.DMA((n_cols + 1,)),
        ],
        10**9,
    )(
        info,
        pltpu.with_memory_space_constraint(user_factors, pltpu.HBM),
        pltpu.with_memory_space_constraint(item_factors, pltpu.HBM),
    )
    shared = swap(sent)

    order = jnp.arange(tile_total, dtype=jnp.int32)
    live = (order < tile_count[0]).astype(jnp.int32)
    tile_item = after(tile_item, sent[0])
    holder = tile_item // item_blocks
    local_block = tile_item % item_blocks
    earlier = (
        (holder[None, :] == holder[:, None])
        & (order[None, :] < order[:, None])
        & (live[None, :] > 0)
    )
    rank = jnp.sum(earlier.astype(jnp.int32), axis=1)
    slot_ids = jnp.minimum(holder * capacity + rank, row_devs * capacity - 1)
    slot_range = jnp.arange(row_devs * capacity, dtype=jnp.int32)
    hits = ((slot_ids[None, :] == slot_range[:, None]) & (live[None, :] > 0)).astype(jnp.int32)
    requests = (jnp.sum(hits * (local_block + 1)[None, :], axis=1) - 1).reshape(row_devs, capacity)
    wanted = lax.all_to_all(requests, "rows", split_axis=0, concat_axis=0, tiled=True)
    block = holder
    if direct:
        step = holder ^ row
        block = step
        for j, spot in ((2, 3), (3, 2), (5, 6), (6, 5)):
            block = jnp.where(step == j, spot, block)
    places = block * capacity + jnp.minimum(rank, capacity - 1)
    places = jnp.where(live > 0, places, places[0])
    tile_users = jnp.where(live > 0, tile_user, tile_user[0])

    picked = call(
        functools.partial(pick_kernel, direct),
        [jax.ShapeDtypeStruct((capacity, col_width, side), bf16)] * row_devs
        if direct
        else [jax.ShapeDtypeStruct((row_devs * capacity, col_width, side), bf16)],
        [smem, smem, anywhere],
        "pick",
        [pltpu.VMEM(item_factors.shape, bf16), pltpu.SemaphoreType.DMA],
        10**9,
    )(
        after(info, *shared),
        wanted,
        pltpu.with_memory_space_constraint(item_factors, pltpu.HBM),
    )

    def join(*arrays):
        return jnp.concatenate(arrays, axis=0)

    def gather(*arrays):
        rows = sum(array.shape[0] for array in arrays)
        return call(
            join_kernel,
            [jax.ShapeDtypeStruct((rows, *arrays[0].shape[1:]), bf16)],
            [anywhere] * len(arrays),
            "join",
            [pltpu.SemaphoreType.DMA((len(arrays),))],
            2 * 10**10,
        )(*arrays)[0]

    def add(gram, *arrived):
        return call(add_kernel, [square, packed], [vmem] * (1 + len(arrived)), "add")(
            gram, *arrived
        )

    got = {0: picked[0]}
    if direct:
        for j in (1, 3, 4, 6, 2):
            got[j] = flip(picked[j], "rows", j)
        across = flip(got[0], "cols", 2)
        near = after(gather(got[1], got[3]), across)
        for j in (5, 7):
            got[j] = flip(after(picked[j], got[4], got[6], near), "rows", j)

    square = jax.ShapeDtypeStruct((width, width), f32)
    extra = width // col_width
    packed = jax.ShapeDtypeStruct((extra, col_width, 2 * width), bf16)
    gram, carried, start = call(
        functools.partial(gram_kernel, own_users),
        [square, packed, jax.ShapeDtypeStruct((width, own_users), f32)],
        [smem] + [anywhere] * n_cols,
        "gram",
        [
            pltpu.VMEM((width, 2 * own_users), bf16),
            pltpu.VMEM((width, span), bf16),
            pltpu.SemaphoreType.DMA((2 * n_cols,)),
        ],
        10**9,
    )(after(info, near if direct else picked[0]), *shared)
    strengths = jax.ShapeDtypeStruct((tile_total, share, side), bf16)

    def slice_mask(ready):
        return call(
            mask_kernel,
            [strengths],
            [smem, anywhere],
            "mask",
            [pltpu.SemaphoreType.DMA],
            10**9,
        )(after(info, ready), pltpu.with_memory_space_constraint(tile_mask, pltpu.HBM))[0]

    if direct:
        slots = (3 * capacity, 3 * capacity, 2 * capacity)
        early = join(got[0], near, across, flip(near, "cols", 2))
        pieces = [early, flip(early, "cols", 1)]

        own = after(gather(got[2], got[4], got[6], carried), early)
        mask = slice_mask(own)
        arrived = flip(own, "cols", 2)
        gram, carried = add(gram, arrived)
        own = join(own[: 3 * capacity], arrived[: 3 * capacity], carried)
        arrived = flip(after(own, mask), "cols", 1)
        gram, carried = add(gram, arrived)
        pieces += [own, arrived]

        own = gather(got[5], got[7])
        own = join(own, flip(own, "cols", 2))
        gram, carried = add(gram, *[flip(carried, "rows", j) for j in (1, 2, 3)])
        pieces += [own, flip(after(own, carried), "cols", 1)]
        arrived = flip(carried, "rows", 4)
    else:
        slots = (row_devs * capacity,)
        mask = slice_mask(gram)
        gram = add_all(gram)
        own = lax.all_to_all(picked[0], "rows", split_axis=0, concat_axis=0, tiled=True)
        own = join(own, flip(own, "cols", 2))
        pieces = [own, flip(own, "cols", 1)]

    vector = jax.ShapeDtypeStruct((own_users, width), f32)
    held = jax.ShapeDtypeStruct((row_devs * capacity, width, side), bf16)
    work = [
        pltpu.VMEM((user_blocks, share, 2 * width), bf16),
        pltpu.VMEM((user_blocks, share, width), f32),
        pltpu.VMEM((2, UNROLL, 2 * share, side), bf16),
    ]
    lists = (places, tile_users, info)
    part, y = call(
        functools.partial(start_kernel, n_cols, slots),
        [vector, held],
        [smem] * 3 + [vmem] * 2 + [anywhere] * len(pieces),
        "start",
        work + [pltpu.SemaphoreType.DMA((n_cols * len(slots),))],
        8 * 10**9,
    )(*lists, start, mask, *pieces)
    rest = [after(arrived, part)] if direct else []
    sent, dots = call(
        iterate_kernel,
        [
            jax.ShapeDtypeStruct((n_cols, 3 * col_width, own_users), f32),
            jax.ShapeDtypeStruct((devices, 128), f32),
        ],
        [smem] * 3 + [vmem] * (5 + len(rest)),
        "iterate",
        work
        + [
            pltpu.VMEM((width, width), f32),
            pltpu.VMEM((own_users, width), f32),
            pltpu.VMEM((own_users, width), f32),
        ],
        16 * 10**9,
    )(*lists, start, part, gram, y, mask, *rest)

    turned = swap(sent)
    dots = lax.all_to_all(dots, ("rows", "cols"), split_axis=0, concat_axis=0, tiled=True)
    result = jax.ShapeDtypeStruct((col_width, users), f32)
    return tuple(
        call(
            functools.partial(finish_kernel, share),
            [result, result],
            [smem] + [vmem] * (2 + n_cols),
            "finish",
            [pltpu.VMEM((n_cols, col_width, own_users), f32)] * 3,
            10**9,
        )(info, dots, user_factors, *turned)
    )


def solution(mesh):
    return jax.shard_map(
        on_device,
        mesh=mesh,
        in_specs=(
            P("cols", "rows"),
            P("cols", "rows"),
            P("rows"),
            P("rows"),
            P("rows"),
            P("rows", None, None),
        ),
        out_specs=(P("cols", "rows"), P("cols", "rows")),
        check_vma=False,
    )
```

```python
import functools

import jax
import jax.numpy as jnp
from jax import lax
from jax.experimental import pallas as pl
from jax.experimental.pallas import tpu as pltpu
from jax.sharding import PartitionSpec as P

ridge = 0.5
confidence = 40.0
UNROLL = 8
LIMIT = 24 * 1024 * 1024
f32 = jnp.float32
bf16 = jnp.bfloat16


def matmul(left, right):
    return jnp.dot(left, right, preferred_element_type=f32)


def split(value):
    high = value.astype(bf16)
    low = (value - high.astype(f32)).astype(bf16)
    return high, low


def prepare_kernel(n_cols, side, info_ref, x_hbm, items_hbm, *refs):
    sent, (x_ref, x_pieces, sems) = refs[:n_cols], refs[n_cols:]
    column = info_ref[1]
    share = side // n_cols
    blocks = x_ref.shape[1] // side
    own_users = blocks * share
    span = sent[0].shape[1] - 2 * own_users
    copies = [
        pltpu.make_async_copy(
            items_hbm.at[:, pl.ds(pl.multiple_of((column ^ m) * span, span), span)],
            sent[m].at[:, pl.ds(2 * own_users, span)],
            sems.at[m],
        )
        for m in range(n_cols)
    ]
    fetch = pltpu.make_async_copy(x_hbm, x_ref, sems.at[n_cols])
    fetch.start()
    for copy in copies:
        copy.start()
    fetch.wait()
    for m in range(n_cols):
        x_pieces[m] = jnp.concatenate(
            [x_ref[:, b * side + m * share : b * side + (m + 1) * share] for b in range(blocks)],
            axis=1,
        )
    for m in range(n_cols):
        high, low = split(x_pieces[column ^ m])
        sent[m][:, :own_users] = high
        sent[m][:, own_users : 2 * own_users] = low
    for copy in copies:
        copy.wait()


def mask_kernel(info_ref, mask_hbm, mask, sem):
    tiles, share, side = mask.shape
    copy = pltpu.make_async_copy(
        mask_hbm.at[:, pl.ds(pl.multiple_of(info_ref[1] * share, share), share), :], mask, sem
    )
    copy.start()
    copy.wait()

    def clear(t, carry):
        mask[t] = jnp.zeros((share, side), bf16)
        return carry

    lax.fori_loop(info_ref[0], tiles, clear, 0)


def pick_kernel(direct, info_ref, wanted_ref, items_hbm, *refs):
    out_refs, (items_ref, sem) = refs[:-2], refs[-2:]
    copy = pltpu.make_async_copy(items_hbm, items_ref, sem)
    copy.start()
    copy.wait()
    capacity = wanted_ref.shape[1]
    side = out_refs[0].shape[2]
    for o, out_ref in enumerate(out_refs):
        for i in range(out_ref.shape[0] // capacity):
            dest = info_ref[2] ^ o if direct else i
            for r in range(capacity):
                block = jnp.maximum(wanted_ref[dest, r], 0)
                start = pl.multiple_of(block * side, side)
                out_ref[i * capacity + r] = items_ref[:, pl.ds(start, side)]


def pack(ref, gram):
    high, low = split(gram)
    both = jnp.concatenate([high, low], axis=1)
    for k in range(ref.shape[0]):
        ref[k] = both[k * ref.shape[1] : (k + 1) * ref.shape[1]]


def unpack(blocks):
    both = jnp.concatenate([blocks[k] for k in range(blocks.shape[0])], axis=0).astype(f32)
    width = both.shape[1] // 2
    return both[:, :width] + both[:, width:]


def gram_kernel(own_users, info_ref, *refs):
    column = info_ref[1]
    pieces = refs[:-6]
    out_ref, pack_ref, start_ref, starts, items, sems = refs[-6:]
    width = pieces[0].shape[0]
    span = items.shape[1]
    copies = []
    for m, piece in enumerate(pieces):
        place = pl.ds(pl.multiple_of((column ^ m) * width, width), width)
        for source, target in (
            (piece.at[:, pl.ds(0, 2 * own_users)], starts.at[place, :]),
            (piece.at[:, pl.ds(2 * own_users, span)], items.at[place, :]),
        ):
            copies.append(pltpu.make_async_copy(source, target, sems.at[len(copies)]))
            copies[-1].start()
    for copy in copies:
        copy.wait()
    both = starts[...].astype(f32)
    start_ref[...] = both[:, :own_users] + both[:, own_users:]
    gram = lax.dot_general(
        items[...], items[...], (((1,), (1,)), ((), ())), preferred_element_type=f32
    )
    out_ref[...] = gram
    pack(pack_ref, gram)


def add_kernel(gram_ref, *refs):
    out_ref, pack_ref = refs[-2:]
    extra = pack_ref.shape[0]
    total = gram_ref[...]
    for arrived_ref in refs[:-2]:
        total = total + unpack(arrived_ref[arrived_ref.shape[0] - extra :])
    out_ref[...] = total
    pack(pack_ref, total)


def join_kernel(*refs):
    sources, out_ref, sems = refs[:-2], refs[-2], refs[-1]
    copies = []
    base = 0
    for source in sources:
        rows = source.shape[0]
        copies.append(
            pltpu.make_async_copy(source, out_ref.at[pl.ds(base, rows)], sems.at[len(copies)])
        )
        copies[-1].start()
        base += rows
    for copy in copies:
        copy.wait()


def load(p_hl, vector):
    blocks, share, both = p_hl.shape
    width = both // 2
    high, low = split(vector)
    p_hl[:, :, :width] = high.reshape(blocks, share, width)
    p_hl[:, :, width:] = low.reshape(blocks, share, width)


def dense(p_hl, gram_ref, vector):
    blocks, share, both = p_hl.shape
    width = both // 2
    high, low = split(gram_ref[...])
    table = jnp.concatenate(
        [
            jnp.concatenate([high, low], axis=1),
            jnp.concatenate([high, jnp.zeros_like(low)], axis=1),
        ],
        axis=0,
    )
    product = matmul(p_hl[...].reshape(blocks * share, both), table)
    return product[:, :width] + product[:, width:] + ridge * vector


def sparse(starting, slot_ref, user_ref, y, mask, p_hl, acc, held):
    tiles, share, side = mask.shape
    groups = tiles // UNROLL
    acc[...] = jnp.zeros_like(acc)

    def score(group):
        for j in range(UNROLL):
            t = group * UNROLL + j
            tile = y[slot_ref[t]]
            scores = matmul(p_hl[user_ref[t]], jnp.concatenate([tile, tile], axis=0))
            if starting:
                scores = (1.0 + confidence) - confidence * scores
            high, low = split(mask[t].astype(f32) * scores)
            held[group % 2, j, :share] = high
            held[group % 2, j, share:] = low

    def collect(group):
        terms = []
        for j in range(UNROLL):
            t = group * UNROLL + j
            term = lax.dot_general(
                held[group % 2, j],
                y[slot_ref[t]],
                (((1,), (1,)), ((), ())),
                preferred_element_type=f32,
            )
            terms.append(term[:share] + term[share:])
        return terms

    def add(group, terms):
        for j, term in enumerate(terms):
            acc[user_ref[group * UNROLL + j]] += term

    score(0)

    def step(group, carry):
        terms = collect(group - 1)
        score(group)
        add(group - 1, terms)
        return carry

    lax.fori_loop(1, groups, step, 0, unroll=True)
    add(groups - 1, collect(groups - 1))


def put(column, ref, vector, part=0):
    n_cols, rows, _ = ref.shape
    turned = vector.T
    width = turned.shape[0] // n_cols
    for m in range(n_cols):
        ref[column ^ m, part * width : (part + 1) * width] = turned[m * width : (m + 1) * width]


def start_kernel(n_cols, slots, slot_ref, user_ref, info_ref, x_ref, mask, *refs):
    pieces = refs[: 2 * len(slots)]
    part_ref, y, p_hl, acc, held, sems = refs[2 * len(slots) :]
    piece_width = y.shape[1] // n_cols
    column = info_ref[1]
    copies = []
    base = 0
    for k, count in enumerate(slots):
        for m in range(n_cols):
            place = pl.multiple_of((column ^ m) * piece_width, piece_width)
            source = pieces[2 * k + m % 2].at[pl.ds(m // 2 * count, count)]
            copies.append(
                pltpu.make_async_copy(
                    source,
                    y.at[pl.ds(base, count), pl.ds(place, piece_width), :],
                    sems.at[len(copies)],
                )
            )
        base += count
    for copy in copies:
        copy.start()
    load(p_hl, x_ref[...].T)
    for copy in copies:
        copy.wait()
    sparse(True, slot_ref, user_ref, y, mask, p_hl, acc, held)
    part_ref[...] = acc[...].reshape(part_ref.shape)


def iterate_kernel(
    slot_ref, user_ref, info_ref, x_ref, part_ref, gram_ref, y, mask, *refs
):
    sent_ref, dots_ref, p_hl, acc, held, gram, field_ref, first_ref = refs[-8:]
    gram[...] = gram_ref[...]
    for arrived_ref in refs[:-8]:
        gram[...] += unpack(arrived_ref)

    def image(vector):
        load(p_hl, vector)
        sparse(False, slot_ref, user_ref, y, mask, p_hl, acc, held)
        return confidence * acc[...].reshape(vector.shape) + dense(p_hl, gram, vector)

    start = x_ref[...].T
    load(p_hl, start)
    field_ref[...] = part_ref[...] - dense(p_hl, gram, start)
    first_ref[...] = image(field_ref[...])
    second = image(first_ref[...])
    field, first = field_ref[...], first_ref[...]
    for part, vector in enumerate((field, first, second)):
        put(info_ref[1], sent_ref, vector, part)

    def total(left, right):
        return jnp.sum(left * right)

    aa, ab, bb = total(field, field), total(field, first), total(first, first)
    guess = jnp.where(bb > 0.0, ab / jnp.where(bb > 0.0, bb, 1.0), 0.0)
    near = field - guess * first
    near_image = first - guess * second
    values = (
        aa,
        ab,
        bb,
        guess,
        total(near, near),
        total(near, first),
        total(near, near_image),
        total(near, second) + total(first, near_image),
        total(first, second),
    )
    lane = lax.broadcasted_iota(jnp.int32, dots_ref.shape, 1)
    dots = jnp.zeros(dots_ref.shape, f32)
    for j, value in enumerate(values):
        dots = jnp.where(lane == j, value, dots)
    dots_ref[...] = dots


def finish_kernel(share, info_ref, dots_ref, x_ref, *refs):
    n_cols = len(refs) - 5
    x_out, r_out, field_ref, first_ref, second_ref = refs[n_cols:]
    width = field_ref.shape[1]
    for m in range(n_cols):
        place = info_ref[1] ^ m
        for part, ref in enumerate((field_ref, first_ref, second_ref)):
            ref[place] = refs[m][part * width : (part + 1) * width]
    dots = dots_ref[...]

    def column(j):
        return dots[:, j : j + 1]

    def total(value):
        return jnp.sum(value, axis=0, keepdims=True)

    rr0 = total(column(0))
    ab = total(column(1))
    alpha0 = rr0 / ab
    delta = alpha0 - column(3)
    rr1 = total(column(4) - 2.0 * delta * column(5) + delta * delta * column(2))
    curved = total(column(6) - delta * column(7) + delta * delta * column(8))
    crossed = total(column(5) - delta * column(2))
    beta = rr1 / rr0
    alpha1 = rr1 / (curved + 2.0 * beta * crossed + beta * beta * ab)
    along = alpha0 + alpha1 * (1.0 + beta)
    across = alpha1 * alpha0
    blocks = x_ref.shape[1] // (share * n_cols)
    for b in range(blocks):

        def gather(ref):
            return jnp.concatenate(
                [ref[m, :, b * share : (b + 1) * share] for m in range(n_cols)], axis=1
            )

        field, first, second = gather(field_ref), gather(first_ref), gather(second_ref)
        here = slice(b * share * n_cols, (b + 1) * share * n_cols)
        x_out[:, here] = x_ref[:, here] + along * field - across * first
        r_out[:, here] = field - along * first + across * second


def flip(value, axis, bit):
    size = lax.axis_size(axis)
    return lax.ppermute(value, axis, [(i, i ^ bit) for i in range(size)])


def swap(sent):
    return [sent[0]] + [flip(sent[m], "cols", m) for m in range(1, len(sent))]


def after(value, *others):
    return lax.optimization_barrier((value, *others))[0]


def add_all(value):
    for axis in ("cols", "rows"):
        bit = 1
        while bit < lax.axis_size(axis):
            value = value + flip(value, axis, bit)
            bit *= 2
    return value


def on_device(user_factors, item_factors, tile_user, tile_item, tile_count, tile_mask):
    side = tile_mask.shape[1]
    col_width = user_factors.shape[0]
    column = lax.axis_index("cols").astype(jnp.int32)
    row = lax.axis_index("rows").astype(jnp.int32)
    row_devs = lax.axis_size("rows")
    n_cols = lax.axis_size("cols")
    devices = row_devs * n_cols
    width = col_width * n_cols
    tile_total = tile_user.shape[0]
    users = user_factors.shape[1]
    user_blocks = users // side
    item_blocks = item_factors.shape[1] // side
    share = side // n_cols
    own_users = users // n_cols
    capacity = max(2, (tile_total + row_devs - 1) // row_devs)
    direct = row_devs == 8 and 2 * width == side
    vmem = pl.BlockSpec(memory_space=pltpu.VMEM)
    smem = pl.BlockSpec(memory_space=pltpu.SMEM)
    anywhere = pl.BlockSpec(memory_space=pl.ANY)
    params = pltpu.CompilerParams(vmem_limit_bytes=LIMIT)

    def call(kernel, out_shape, in_specs, name, scratch=(), flops=0):
        return pl.pallas_call(
            kernel,
            out_shape=out_shape,
            in_specs=in_specs,
            out_specs=jax.tree.map(lambda _: vmem, out_shape),
            scratch_shapes=scratch,
            compiler_params=params,
            cost_estimate=pl.CostEstimate(
                flops=flops, bytes_accessed=0, transcendentals=0
            ),
            name=name,
        )

    info = jnp.stack([tile_count[0], column, row])
    span = item_factors.shape[1] // n_cols
    sent = call(
        functools.partial(prepare_kernel, n_cols, side),
        [jax.ShapeDtypeStruct((col_width, 2 * own_users + span), bf16)] * n_cols,
        [smem, anywhere, anywhere],
        "prepare",
        [
            pltpu.VMEM(user_factors.shape, f32),
            pltpu.VMEM((n_cols, col_width, own_users), f32),
            pltpu.SemaphoreType.DMA((n_cols + 1,)),
        ],
        10**9,
    )(
        info,
        pltpu.with_memory_space_constraint(user_factors, pltpu.HBM),
        pltpu.with_memory_space_constraint(item_factors, pltpu.HBM),
    )
    shared = swap(sent)

    order = jnp.arange(tile_total, dtype=jnp.int32)
    live = (order < tile_count[0]).astype(jnp.int32)
    tile_item = after(tile_item, sent[0])
    holder = tile_item // item_blocks
    local_block = tile_item % item_blocks
    earlier = (
        (holder[None, :] == holder[:, None])
        & (order[None, :] < order[:, None])
        & (live[None, :] > 0)
    )
    rank = jnp.sum(earlier.astype(jnp.int32), axis=1)
    slot_ids = jnp.minimum(holder * capacity + rank, row_devs * capacity - 1)
    slot_range = jnp.arange(row_devs * capacity, dtype=jnp.int32)
    hits = ((slot_ids[None, :] == slot_range[:, None]) & (live[None, :] > 0)).astype(jnp.int32)
    requests = (jnp.sum(hits * (local_block + 1)[None, :], axis=1) - 1).reshape(row_devs, capacity)
    wanted = lax.all_to_all(requests, "rows", split_axis=0, concat_axis=0, tiled=True)
    block = holder
    if direct:
        step = holder ^ row
        block = step
        for j, spot in ((2, 3), (3, 2), (5, 6), (6, 5)):
            block = jnp.where(step == j, spot, block)
    places = block * capacity + jnp.minimum(rank, capacity - 1)
    places = jnp.where(live > 0, places, places[0])
    tile_users = jnp.where(live > 0, tile_user, tile_user[0])

    picked = call(
        functools.partial(pick_kernel, direct),
        [jax.ShapeDtypeStruct((capacity, col_width, side), bf16)] * row_devs
        if direct
        else [jax.ShapeDtypeStruct((row_devs * capacity, col_width, side), bf16)],
        [smem, smem, anywhere],
        "pick",
        [pltpu.VMEM(item_factors.shape, bf16), pltpu.SemaphoreType.DMA],
        10**9,
    )(
        after(info, shared[1]),
        wanted,
        pltpu.with_memory_space_constraint(item_factors, pltpu.HBM),
    )

    def join(*arrays):
        return jnp.concatenate(arrays, axis=0)

    def gather(*arrays):
        rows = sum(array.shape[0] for array in arrays)
        return call(
            join_kernel,
            [jax.ShapeDtypeStruct((rows, *arrays[0].shape[1:]), bf16)],
            [anywhere] * len(arrays),
            "join",
            [pltpu.SemaphoreType.DMA((len(arrays),))],
            2 * 10**10,
        )(*arrays)[0]

    def add(gram, *arrived):
        return call(add_kernel, [square, packed], [vmem] * (1 + len(arrived)), "add")(
            gram, *arrived
        )

    got = {0: picked[0]}
    if direct:
        for j in (1, 3, 4, 6, 2):
            got[j] = flip(picked[j], "rows", j)
        across = flip(got[0], "cols", 2)
        near = after(gather(got[1], got[3]), across)
        for j in (5, 7):
            got[j] = flip(after(picked[j], got[4], got[6], near), "rows", j)

    square = jax.ShapeDtypeStruct((width, width), f32)
    extra = width // col_width
    packed = jax.ShapeDtypeStruct((extra, col_width, 2 * width), bf16)
    gram, carried, start = call(
        functools.partial(gram_kernel, own_users),
        [square, packed, jax.ShapeDtypeStruct((width, own_users), f32)],
        [smem] + [anywhere] * n_cols,
        "gram",
        [
            pltpu.VMEM((width, 2 * own_users), bf16),
            pltpu.VMEM((width, span), bf16),
            pltpu.SemaphoreType.DMA((2 * n_cols,)),
        ],
        10**9,
    )(after(info, near if direct else picked[0]), *shared)
    strengths = jax.ShapeDtypeStruct((tile_total, share, side), bf16)

    def slice_mask(ready):
        return call(
            mask_kernel,
            [strengths],
            [smem, anywhere],
            "mask",
            [pltpu.SemaphoreType.DMA],
            10**9,
        )(after(info, ready), pltpu.with_memory_space_constraint(tile_mask, pltpu.HBM))[0]

    if direct:
        slots = (3 * capacity, 3 * capacity, 2 * capacity)
        early = join(got[0], near, across, flip(near, "cols", 2))
        pieces = [early, flip(early, "cols", 1)]

        own = after(gather(got[2], got[4], got[6], carried), early)
        mask = slice_mask(own)
        arrived = flip(own, "cols", 2)
        gram, carried = add(gram, arrived)
        own = join(own[: 3 * capacity], arrived[: 3 * capacity], carried)
        arrived = flip(after(own, mask), "cols", 1)
        gram, carried = add(gram, arrived)
        pieces += [own, arrived]

        own = gather(got[5], got[7])
        own = join(own, flip(own, "cols", 2))
        gram, carried = add(gram, *[flip(carried, "rows", j) for j in (1, 2, 3)])
        pieces += [own, flip(after(own, carried), "cols", 1)]
        arrived = flip(carried, "rows", 4)
    else:
        slots = (row_devs * capacity,)
        mask = slice_mask(gram)
        gram = add_all(gram)
        own = lax.all_to_all(picked[0], "rows", split_axis=0, concat_axis=0, tiled=True)
        own = join(own, flip(own, "cols", 2))
        pieces = [own, flip(own, "cols", 1)]

    vector = jax.ShapeDtypeStruct((own_users, width), f32)
    held = jax.ShapeDtypeStruct((row_devs * capacity, width, side), bf16)
    work = [
        pltpu.VMEM((user_blocks, share, 2 * width), bf16),
        pltpu.VMEM((user_blocks, share, width), f32),
        pltpu.VMEM((2, UNROLL, 2 * share, side), bf16),
    ]
    lists = (places, tile_users, info)
    part, y = call(
        functools.partial(start_kernel, n_cols, slots),
        [vector, held],
        [smem] * 3 + [vmem] * 2 + [anywhere] * len(pieces),
        "start",
        work + [pltpu.SemaphoreType.DMA((n_cols * len(slots),))],
        8 * 10**9,
    )(*lists, start, mask, *pieces)
    rest = [after(arrived, part)] if direct else []
    sent, dots = call(
        iterate_kernel,
        [
            jax.ShapeDtypeStruct((n_cols, 3 * col_width, own_users), f32),
            jax.ShapeDtypeStruct((devices, 128), f32),
        ],
        [smem] * 3 + [vmem] * (5 + len(rest)),
        "iterate",
        work
        + [
            pltpu.VMEM((width, width), f32),
            pltpu.VMEM((own_users, width), f32),
            pltpu.VMEM((own_users, width), f32),
        ],
        16 * 10**9,
    )(*lists, start, part, gram, y, mask, *rest)

    turned = swap(sent)
    dots = lax.all_to_all(dots, ("rows", "cols"), split_axis=0, concat_axis=0, tiled=True)
    result = jax.ShapeDtypeStruct((col_width, users), f32)
    return tuple(
        call(
            functools.partial(finish_kernel, share),
            [result, result],
            [smem] + [vmem] * (2 + n_cols),
            "finish",
            [pltpu.VMEM((n_cols, col_width, own_users), f32)] * 3,
            10**9,
        )(info, dots, user_factors, *turned)
    )


def solution(mesh):
    return jax.shard_map(
        on_device,
        mesh=mesh,
        in_specs=(
            P("cols", "rows"),
            P("cols", "rows"),
            P("rows"),
            P("rows"),
            P("rows"),
            P("rows", None, None),
        ),
        out_specs=(P("cols", "rows"), P("cols", "rows")),
        check_vma=False,
    )
```

```python
import functools

import jax
import jax.numpy as jnp
from jax import lax
from jax.experimental import pallas as pl
from jax.experimental.pallas import tpu as pltpu
from jax.sharding import PartitionSpec as P

ridge = 0.5
confidence = 40.0
UNROLL = 8
LIMIT = 24 * 1024 * 1024
f32 = jnp.float32
bf16 = jnp.bfloat16


def matmul(left, right):
    return jnp.dot(left, right, preferred_element_type=f32)


def split(value):
    high = value.astype(bf16)
    low = (value - high.astype(f32)).astype(bf16)
    return high, low


def prepare_kernel(n_cols, side, info_ref, x_hbm, items_hbm, *refs):
    sent, (x_ref, x_pieces, sems) = refs[:n_cols], refs[n_cols:]
    column = info_ref[1]
    share = side // n_cols
    blocks = x_ref.shape[1] // side
    own_users = blocks * share
    span = sent[0].shape[1] - 2 * own_users
    copies = [
        pltpu.make_async_copy(
            items_hbm.at[:, pl.ds(pl.multiple_of((column ^ m) * span, span), span)],
            sent[m].at[:, pl.ds(2 * own_users, span)],
            sems.at[m],
        )
        for m in range(n_cols)
    ]
    fetch = pltpu.make_async_copy(x_hbm, x_ref, sems.at[n_cols])
    fetch.start()
    for copy in copies:
        copy.start()
    fetch.wait()
    for m in range(n_cols):
        x_pieces[m] = jnp.concatenate(
            [x_ref[:, b * side + m * share : b * side + (m + 1) * share] for b in range(blocks)],
            axis=1,
        )
    for m in range(n_cols):
        high, low = split(x_pieces[column ^ m])
        sent[m][:, :own_users] = high
        sent[m][:, own_users : 2 * own_users] = low
    for copy in copies:
        copy.wait()


def mask_kernel(info_ref, mask_hbm, mask, sem):
    tiles, share, side = mask.shape
    copy = pltpu.make_async_copy(
        mask_hbm.at[:, pl.ds(pl.multiple_of(info_ref[1] * share, share), share), :], mask, sem
    )
    copy.start()
    copy.wait()

    def clear(t, carry):
        mask[t] = jnp.zeros((share, side), bf16)
        return carry

    lax.fori_loop(info_ref[0], tiles, clear, 0)


def pick_kernel(direct, info_ref, wanted_ref, items_hbm, *refs):
    out_refs, (items_ref, sem) = refs[:-2], refs[-2:]
    copy = pltpu.make_async_copy(items_hbm, items_ref, sem)
    copy.start()
    copy.wait()
    capacity = wanted_ref.shape[1]
    side = out_refs[0].shape[2]
    for o, out_ref in enumerate(out_refs):
        for i in range(out_ref.shape[0] // capacity):
            dest = info_ref[2] ^ o if direct else i
            for r in range(capacity):
                block = jnp.maximum(wanted_ref[dest, r], 0)
                start = pl.multiple_of(block * side, side)
                out_ref[i * capacity + r] = items_ref[:, pl.ds(start, side)]


def pack(ref, gram):
    high, low = split(gram)
    both = jnp.concatenate([high, low], axis=1)
    for k in range(ref.shape[0]):
        ref[k] = both[k * ref.shape[1] : (k + 1) * ref.shape[1]]


def unpack(blocks):
    both = jnp.concatenate([blocks[k] for k in range(blocks.shape[0])], axis=0).astype(f32)
    width = both.shape[1] // 2
    return both[:, :width] + both[:, width:]


def gram_kernel(own_users, info_ref, *refs):
    column = info_ref[1]
    pieces = refs[:-6]
    out_ref, pack_ref, start_ref, starts, items, sems = refs[-6:]
    width = pieces[0].shape[0]
    span = items.shape[1]
    copies = []
    for m, piece in enumerate(pieces):
        place = pl.ds(pl.multiple_of((column ^ m) * width, width), width)
        for source, target in (
            (piece.at[:, pl.ds(0, 2 * own_users)], starts.at[place, :]),
            (piece.at[:, pl.ds(2 * own_users, span)], items.at[place, :]),
        ):
            copies.append(pltpu.make_async_copy(source, target, sems.at[len(copies)]))
            copies[-1].start()
    for copy in copies:
        copy.wait()
    both = starts[...].astype(f32)
    start_ref[...] = both[:, :own_users] + both[:, own_users:]
    gram = lax.dot_general(
        items[...], items[...], (((1,), (1,)), ((), ())), preferred_element_type=f32
    )
    out_ref[...] = gram
    pack(pack_ref, gram)


def add_kernel(gram_ref, *refs):
    out_ref, pack_ref = refs[-2:]
    extra = pack_ref.shape[0]
    total = gram_ref[...]
    for arrived_ref in refs[:-2]:
        total = total + unpack(arrived_ref[arrived_ref.shape[0] - extra :])
    out_ref[...] = total
    pack(pack_ref, total)


def join_kernel(*refs):
    sources, out_ref, sems = refs[:-2], refs[-2], refs[-1]
    copies = []
    base = 0
    for source in sources:
        rows = source.shape[0]
        copies.append(
            pltpu.make_async_copy(source, out_ref.at[pl.ds(base, rows)], sems.at[len(copies)])
        )
        copies[-1].start()
        base += rows
    for copy in copies:
        copy.wait()


def load(p_hl, vector):
    blocks, share, both = p_hl.shape
    width = both // 2
    high, low = split(vector)
    p_hl[:, :, :width] = high.reshape(blocks, share, width)
    p_hl[:, :, width:] = low.reshape(blocks, share, width)


def dense(p_hl, gram_ref, vector):
    blocks, share, both = p_hl.shape
    width = both // 2
    high, low = split(gram_ref[...])
    table = jnp.concatenate(
        [
            jnp.concatenate([high, low], axis=1),
            jnp.concatenate([high, jnp.zeros_like(low)], axis=1),
        ],
        axis=0,
    )
    product = matmul(p_hl[...].reshape(blocks * share, both), table)
    return product[:, :width] + product[:, width:] + ridge * vector


def sparse(starting, slot_ref, user_ref, y, mask, p_hl, acc, held):
    tiles, share, side = mask.shape
    groups = tiles // UNROLL
    acc[...] = jnp.zeros_like(acc)

    def score(group):
        for j in range(UNROLL):
            t = group * UNROLL + j
            tile = y[slot_ref[t]]
            scores = matmul(p_hl[user_ref[t]], jnp.concatenate([tile, tile], axis=0))
            if starting:
                scores = (1.0 + confidence) - confidence * scores
            high, low = split(mask[t].astype(f32) * scores)
            held[group % 2, j, :share] = high
            held[group % 2, j, share:] = low

    def collect(group):
        terms = []
        for j in range(UNROLL):
            t = group * UNROLL + j
            term = lax.dot_general(
                held[group % 2, j],
                y[slot_ref[t]],
                (((1,), (1,)), ((), ())),
                preferred_element_type=f32,
            )
            terms.append(term[:share] + term[share:])
        return terms

    def add(group, terms):
        for j, term in enumerate(terms):
            acc[user_ref[group * UNROLL + j]] += term

    score(0)

    def step(group, carry):
        terms = collect(group - 1)
        score(group)
        add(group - 1, terms)
        return carry

    lax.fori_loop(1, groups, step, 0, unroll=True)
    add(groups - 1, collect(groups - 1))


def put(column, ref, vector, part=0):
    n_cols, rows, _ = ref.shape
    turned = vector.T
    width = turned.shape[0] // n_cols
    for m in range(n_cols):
        ref[column ^ m, part * width : (part + 1) * width] = turned[m * width : (m + 1) * width]


def start_kernel(n_cols, slots, slot_ref, user_ref, info_ref, x_ref, mask, *refs):
    pieces = refs[: 2 * len(slots)]
    part_ref, y, p_hl, acc, held, sems = refs[2 * len(slots) :]
    piece_width = y.shape[1] // n_cols
    column = info_ref[1]
    copies = []
    base = 0
    for k, count in enumerate(slots):
        for m in range(n_cols):
            place = pl.multiple_of((column ^ m) * piece_width, piece_width)
            source = pieces[2 * k + m % 2].at[pl.ds(m // 2 * count, count)]
            copies.append(
                pltpu.make_async_copy(
                    source,
                    y.at[pl.ds(base, count), pl.ds(place, piece_width), :],
                    sems.at[len(copies)],
                )
            )
        base += count
    for copy in copies:
        copy.start()
    load(p_hl, x_ref[...].T)
    for copy in copies:
        copy.wait()
    sparse(True, slot_ref, user_ref, y, mask, p_hl, acc, held)
    part_ref[...] = acc[...].reshape(part_ref.shape)


def iterate_kernel(
    slot_ref, user_ref, info_ref, x_ref, part_ref, gram_ref, y, mask, *refs
):
    sent_ref, dots_ref, p_hl, acc, held, gram, field_ref, first_ref = refs[-8:]
    gram[...] = gram_ref[...]
    for arrived_ref in refs[:-8]:
        gram[...] += unpack(arrived_ref)

    def image(vector):
        load(p_hl, vector)
        sparse(False, slot_ref, user_ref, y, mask, p_hl, acc, held)
        return confidence * acc[...].reshape(vector.shape) + dense(p_hl, gram, vector)

    start = x_ref[...].T
    load(p_hl, start)
    field_ref[...] = part_ref[...] - dense(p_hl, gram, start)
    first_ref[...] = image(field_ref[...])
    second = image(first_ref[...])
    field, first = field_ref[...], first_ref[...]
    for part, vector in enumerate((field, first, second)):
        put(info_ref[1], sent_ref, vector, part)

    def total(left, right):
        return jnp.sum(left * right)

    aa, ab, bb = total(field, field), total(field, first), total(first, first)
    guess = jnp.where(bb > 0.0, ab / jnp.where(bb > 0.0, bb, 1.0), 0.0)
    near = field - guess * first
    near_image = first - guess * second
    values = (
        aa,
        ab,
        bb,
        guess,
        total(near, near),
        total(near, first),
        total(near, near_image),
        total(near, second) + total(first, near_image),
        total(first, second),
    )
    lane = lax.broadcasted_iota(jnp.int32, dots_ref.shape, 1)
    dots = jnp.zeros(dots_ref.shape, f32)
    for j, value in enumerate(values):
        dots = jnp.where(lane == j, value, dots)
    dots_ref[...] = dots


def finish_kernel(share, info_ref, dots_ref, x_ref, *refs):
    pieces, (x_out, r_out) = refs[:-2], refs[-2:]
    own = info_ref[1]
    odd = own % 2 == 1
    width = x_ref.shape[0]
    dots = dots_ref[...]

    def column(j):
        return dots[:, j : j + 1]

    def total(value):
        return jnp.sum(value, axis=0, keepdims=True)

    rr0 = total(column(0))
    ab = total(column(1))
    alpha0 = rr0 / ab
    delta = alpha0 - column(3)
    rr1 = total(column(4) - 2.0 * delta * column(5) + delta * delta * column(2))
    curved = total(column(6) - delta * column(7) + delta * delta * column(8))
    crossed = total(column(5) - delta * column(2))
    beta = rr1 / rr0
    alpha1 = rr1 / (curved + 2.0 * beta * crossed + beta * beta * ab)
    along = alpha0 + alpha1 * (1.0 + beta)
    across = alpha1 * alpha0
    n_cols = len(pieces)
    for b in range(x_ref.shape[1] // (share * n_cols)):
        for k in range(0, n_cols, 2):

            def pair(part):
                left, right = (
                    ref[part * width : (part + 1) * width, b * share : (b + 1) * share]
                    for ref in pieces[k : k + 2]
                )
                return jnp.concatenate(
                    [jnp.where(odd, right, left), jnp.where(odd, left, right)], axis=1
                )

            field, first, second = pair(0), pair(1), pair(2)
            place = (b * n_cols + ((own // 2) ^ (k // 2)) * 2) * share
            here = pl.ds(pl.multiple_of(place, 2 * share), 2 * share)
            x_out[:, here] = x_ref[:, here] + along * field - across * first
            r_out[:, here] = field - along * first + across * second


def flip(value, axis, bit):
    size = lax.axis_size(axis)
    return lax.ppermute(value, axis, [(i, i ^ bit) for i in range(size)])


def swap(sent):
    return [sent[0]] + [flip(sent[m], "cols", m) for m in range(1, len(sent))]


def after(value, *others):
    return lax.optimization_barrier((value, *others))[0]


def add_all(value):
    for axis in ("cols", "rows"):
        bit = 1
        while bit < lax.axis_size(axis):
            value = value + flip(value, axis, bit)
            bit *= 2
    return value


def on_device(user_factors, item_factors, tile_user, tile_item, tile_count, tile_mask):
    side = tile_mask.shape[1]
    col_width = user_factors.shape[0]
    column = lax.axis_index("cols").astype(jnp.int32)
    row = lax.axis_index("rows").astype(jnp.int32)
    row_devs = lax.axis_size("rows")
    n_cols = lax.axis_size("cols")
    devices = row_devs * n_cols
    width = col_width * n_cols
    tile_total = tile_user.shape[0]
    users = user_factors.shape[1]
    user_blocks = users // side
    item_blocks = item_factors.shape[1] // side
    share = side // n_cols
    own_users = users // n_cols
    capacity = max(2, (tile_total + row_devs - 1) // row_devs)
    direct = row_devs == 8 and 2 * width == side
    vmem = pl.BlockSpec(memory_space=pltpu.VMEM)
    smem = pl.BlockSpec(memory_space=pltpu.SMEM)
    anywhere = pl.BlockSpec(memory_space=pl.ANY)
    params = pltpu.CompilerParams(vmem_limit_bytes=LIMIT)

    def call(kernel, out_shape, in_specs, name, scratch=(), flops=0):
        return pl.pallas_call(
            kernel,
            out_shape=out_shape,
            in_specs=in_specs,
            out_specs=jax.tree.map(lambda _: vmem, out_shape),
            scratch_shapes=scratch,
            compiler_params=params,
            cost_estimate=pl.CostEstimate(
                flops=flops, bytes_accessed=0, transcendentals=0
            ),
            name=name,
        )

    info = jnp.stack([tile_count[0], column, row])
    span = item_factors.shape[1] // n_cols
    sent = call(
        functools.partial(prepare_kernel, n_cols, side),
        [jax.ShapeDtypeStruct((col_width, 2 * own_users + span), bf16)] * n_cols,
        [smem, anywhere, anywhere],
        "prepare",
        [
            pltpu.VMEM(user_factors.shape, f32),
            pltpu.VMEM((n_cols, col_width, own_users), f32),
            pltpu.SemaphoreType.DMA((n_cols + 1,)),
        ],
        10**9,
    )(
        info,
        pltpu.with_memory_space_constraint(user_factors, pltpu.HBM),
        pltpu.with_memory_space_constraint(item_factors, pltpu.HBM),
    )
    shared = swap(sent)

    order = jnp.arange(tile_total, dtype=jnp.int32)
    live = (order < tile_count[0]).astype(jnp.int32)
    tile_item = after(tile_item, sent[0])
    holder = tile_item // item_blocks
    local_block = tile_item % item_blocks
    earlier = (
        (holder[None, :] == holder[:, None])
        & (order[None, :] < order[:, None])
        & (live[None, :] > 0)
    )
    rank = jnp.sum(earlier.astype(jnp.int32), axis=1)
    slot_ids = jnp.minimum(holder * capacity + rank, row_devs * capacity - 1)
    slot_range = jnp.arange(row_devs * capacity, dtype=jnp.int32)
    hits = ((slot_ids[None, :] == slot_range[:, None]) & (live[None, :] > 0)).astype(jnp.int32)
    requests = (jnp.sum(hits * (local_block + 1)[None, :], axis=1) - 1).reshape(row_devs, capacity)
    wanted = lax.all_to_all(requests, "rows", split_axis=0, concat_axis=0, tiled=True)
    block = holder
    if direct:
        step = holder ^ row
        block = step
        for j, spot in ((2, 3), (3, 2), (5, 6), (6, 5)):
            block = jnp.where(step == j, spot, block)
    places = block * capacity + jnp.minimum(rank, capacity - 1)
    places = jnp.where(live > 0, places, places[0])
    tile_users = jnp.where(live > 0, tile_user, tile_user[0])

    picked = call(
        functools.partial(pick_kernel, direct),
        [jax.ShapeDtypeStruct((capacity, col_width, side), bf16)] * row_devs
        if direct
        else [jax.ShapeDtypeStruct((row_devs * capacity, col_width, side), bf16)],
        [smem, smem, anywhere],
        "pick",
        [pltpu.VMEM(item_factors.shape, bf16), pltpu.SemaphoreType.DMA],
        10**9,
    )(
        after(info, *shared),
        wanted,
        pltpu.with_memory_space_constraint(item_factors, pltpu.HBM),
    )

    def join(*arrays):
        return jnp.concatenate(arrays, axis=0)

    def gather(*arrays):
        rows = sum(array.shape[0] for array in arrays)
        return call(
            join_kernel,
            [jax.ShapeDtypeStruct((rows, *arrays[0].shape[1:]), bf16)],
            [anywhere] * len(arrays),
            "join",
            [pltpu.SemaphoreType.DMA((len(arrays),))],
            2 * 10**10,
        )(*arrays)[0]

    def add(gram, *arrived):
        return call(add_kernel, [square, packed], [vmem] * (1 + len(arrived)), "add")(
            gram, *arrived
        )

    got = {0: picked[0]}
    if direct:
        for j in (1, 3, 4, 6, 2):
            got[j] = flip(picked[j], "rows", j)
        across = flip(got[0], "cols", 2)
        near = after(gather(got[1], got[3]), across)
        for j in (5, 7):
            got[j] = flip(after(picked[j], got[4], got[6], near), "rows", j)

    square = jax.ShapeDtypeStruct((width, width), f32)
    extra = width // col_width
    packed = jax.ShapeDtypeStruct((extra, col_width, 2 * width), bf16)
    gram, carried, start = call(
        functools.partial(gram_kernel, own_users),
        [square, packed, jax.ShapeDtypeStruct((width, own_users), f32)],
        [smem] + [anywhere] * n_cols,
        "gram",
        [
            pltpu.VMEM((width, 2 * own_users), bf16),
            pltpu.VMEM((width, span), bf16),
            pltpu.SemaphoreType.DMA((2 * n_cols,)),
        ],
        10**9,
    )(after(info, near if direct else picked[0]), *shared)
    strengths = jax.ShapeDtypeStruct((tile_total, share, side), bf16)

    def slice_mask(ready):
        return call(
            mask_kernel,
            [strengths],
            [smem, anywhere],
            "mask",
            [pltpu.SemaphoreType.DMA],
            10**9,
        )(after(info, ready), pltpu.with_memory_space_constraint(tile_mask, pltpu.HBM))[0]

    if direct:
        slots = (3 * capacity, 3 * capacity, 2 * capacity)
        early = join(got[0], near, across, flip(near, "cols", 2))
        pieces = [early, flip(early, "cols", 1)]

        own = after(gather(got[2], got[4], got[6], carried), early)
        mask = slice_mask(own)
        arrived = flip(own, "cols", 2)
        gram, carried = add(gram, arrived)
        own = join(own[: 3 * capacity], arrived[: 3 * capacity], carried)
        arrived = flip(after(own, mask), "cols", 1)
        gram, carried = add(gram, arrived)
        pieces += [own, arrived]

        own = gather(got[5], got[7])
        own = join(own, flip(own, "cols", 2))
        gram, carried = add(gram, *[flip(carried, "rows", j) for j in (1, 2, 3)])
        pieces += [own, flip(after(own, carried), "cols", 1)]
        arrived = flip(carried, "rows", 4)
    else:
        slots = (row_devs * capacity,)
        mask = slice_mask(gram)
        gram = add_all(gram)
        own = lax.all_to_all(picked[0], "rows", split_axis=0, concat_axis=0, tiled=True)
        own = join(own, flip(own, "cols", 2))
        pieces = [own, flip(own, "cols", 1)]

    vector = jax.ShapeDtypeStruct((own_users, width), f32)
    held = jax.ShapeDtypeStruct((row_devs * capacity, width, side), bf16)
    work = [
        pltpu.VMEM((user_blocks, share, 2 * width), bf16),
        pltpu.VMEM((user_blocks, share, width), f32),
        pltpu.VMEM((2, UNROLL, 2 * share, side), bf16),
    ]
    lists = (places, tile_users, info)
    part, y = call(
        functools.partial(start_kernel, n_cols, slots),
        [vector, held],
        [smem] * 3 + [vmem] * 2 + [anywhere] * len(pieces),
        "start",
        work + [pltpu.SemaphoreType.DMA((n_cols * len(slots),))],
        8 * 10**9,
    )(*lists, start, mask, *pieces)
    rest = [after(arrived, part)] if direct else []
    sent, dots = call(
        iterate_kernel,
        [
            jax.ShapeDtypeStruct((n_cols, 3 * col_width, own_users), f32),
            jax.ShapeDtypeStruct((devices, 128), f32),
        ],
        [smem] * 3 + [vmem] * (5 + len(rest)),
        "iterate",
        work
        + [
            pltpu.VMEM((width, width), f32),
            pltpu.VMEM((own_users, width), f32),
            pltpu.VMEM((own_users, width), f32),
        ],
        16 * 10**9,
    )(*lists, start, part, gram, y, mask, *rest)

    turned = swap(sent)
    dots = lax.all_to_all(dots, ("rows", "cols"), split_axis=0, concat_axis=0, tiled=True)
    result = jax.ShapeDtypeStruct((col_width, users), f32)
    return tuple(
        call(
            functools.partial(finish_kernel, share),
            [result, result],
            [smem] + [vmem] * (2 + n_cols),
            "finish",
            (),
            10**9,
        )(info, dots, user_factors, *turned)
    )


def solution(mesh):
    return jax.shard_map(
        on_device,
        mesh=mesh,
        in_specs=(
            P("cols", "rows"),
            P("cols", "rows"),
            P("rows"),
            P("rows"),
            P("rows"),
            P("rows", None, None),
        ),
        out_specs=(P("cols", "rows"), P("cols", "rows")),
        check_vma=False,
    )
```
